512 devices in a mesh: dp: 32 (over y, x), seq: 16 (over z, core).
Axes of the slice: x: 4, y: 8, z: 8, core: 2. Of those that a mesh axis runs over, the one named last changes fastest.
Arguments:
- qkv_vis: bfloat16 [57344, 9216], P(('dp', 'seq')), may hold values from -8 to 8
- qkv_txt: bfloat16 [8192, 9216], P(('dp', 'seq')), may hold values from -8 to 8
- vis_segments: int32 [57344], P(('dp', 'seq')), may hold values from 0 to 63, as said below
- txt_segments: int32 [8192], P(('dp', 'seq')), may hold values from 0 to 63, as said below
- head_map: int32 [24], replicated, may hold values from 0 to 15, as said below
- w_out: bfloat16 [3072, 1536], P('dp'), may hold values from -0.109375 to 0.109375
Outputs:
- vis_out: bfloat16 [57344, 1536], P(('dp', 'seq'))
- txt_out: bfloat16 [8192, 3072], P(('dp', 'seq'))
- lse_slots: float32 [32, 65536], P('seq', 'dp')
The draws below stay inside these ranges and needn't reach their ends.
Inputs may be any that keep to these rules, and one draw needn't show every extreme that they name: `vis_segments`: within each group of 1792 rows (group g), a first run of rows carries 2 g and the rest 2 g + 1; each run holds 448 rows or more. `txt_segments`: within each group of 256 rows (group g), a first run of rows carries 2 g and the rest 2 g + 1; each run holds 64 rows or more. `head_map`: each index of seq is named by 2 heads or by one fewer; which indices are named 2 times changes from draw to draw.
All inputs are finite; a program needn't handle non-finite values.
Results may differ from the reference program's by a relative error of at most 0.008.
Values may be sent and summed in bfloat16 or wider, within the bound.
No kernel may reach another device: no remote copies, remote signals or barrier semaphores. Data moves between devices by JAX's collectives and lax.ppermute only.
A program may use at most 64 MiB of HBM per device.

```python
import math
import jax
import jax.numpy as jnp
from jax import lax

HEADS = 24
HEAD_DIM = 128
INNER = 3072
DOUT = 1536
VIS_SEQ = 1792
TXT_SEQ = 256
JOINT = 2048
TOKV = 57344
TOKT = 8192
HMAX = 2
SLOTS = 32
N_DP = 32
N_SEQ = 16


def group_runs(key, seq_len):
    cuts = jax.random.randint(key, (N_DP, 1), seq_len // 4, 3 * seq_len // 4 + 1)
    local_ids = jnp.arange(seq_len, dtype=jnp.int32)[None, :]
    group_ids = jnp.arange(N_DP, dtype=jnp.int32)[:, None]
    return (2 * group_ids + (local_ids >= cuts).astype(jnp.int32)).reshape(N_DP * seq_len)


def draw_vis_segments(key, part):
    key = jax.random.fold_in(key, 5)
    return group_runs(key, VIS_SEQ)


def draw_txt_segments(key, part):
    key = jax.random.fold_in(key, 6)
    return group_runs(key, TXT_SEQ)


def draw_head_map(key, part):
    key = jax.random.fold_in(key, 7)
    order_key, device_key = jax.random.split(key)
    head_order = jax.random.permutation(order_key, HEADS)
    device_order = jax.random.permutation(device_key, N_SEQ)
    position = jnp.argsort(head_order)
    return device_order[position % N_SEQ].astype(jnp.int32)


def draw_qkv_vis(key, part):
    key = jax.random.fold_in(key, 3)
    base_key = jax.random.fold_in(key, 0)
    full_shape = (TOKV, 3, HEADS, HEAD_DIM)
    values = jnp.clip(1.6 * jax.random.normal(base_key, full_shape, jnp.float32), -8.0, 8.0)
    return values.reshape(TOKV, 3 * HEADS * HEAD_DIM).astype(jnp.bfloat16)


def level_of(stream_key, dims, cuts, least, largest):
    loudness, own = 1.0, jax.random.fold_in(stream_key, 6)
    for dim, shards_of in cuts:
        draws = jnp.exp(jax.random.uniform(jax.random.fold_in(own, dim), (shards_of,), jnp.float32, least / len(cuts), largest / len(cuts)))
        loudness = loudness * jnp.repeat(draws, dims[dim] // shards_of).reshape([-1 if axis == dim else 1 for axis in range(len(dims))])
    return loudness


def bell_draw(key, extent, deviation, bound, shards=(), held_as=jnp.bfloat16):
    entries = jax.random.normal(key, extent, jnp.float32) * deviation
    if len(shards) > 0:
        entries = level_of(key, extent, shards, -0.22, 0.18) * entries
    return jnp.clip(entries, min=-bound, max=bound).astype(held_as)


def setup_inputs(seed: int = 0) -> dict:
    splits = jax.random.split(jax.random.key(seed), 7)
    return {
        "qkv_vis": draw_qkv_vis(jax.random.fold_in(splits[6], 71), 0),
        "qkv_txt": bell_draw(splits[1], (TOKT, 3 * INNER), 1.6, 8.0, ((0, 512),)),
        "vis_segments": draw_vis_segments(jax.random.fold_in(splits[6], 71), 0),
        "txt_segments": draw_txt_segments(jax.random.fold_in(splits[6], 71), 0),
        "head_map": draw_head_map(jax.random.fold_in(splits[6], 71), 0),
        "w_out": bell_draw(splits[5], (INNER, DOUT), INNER ** -0.5, 0.109375, ((0, 32),)),
    }


neg_large = -1.0e30


def attend_rows(queries, key_rows, value_rows, seg_queries, seg_keys):
    row_count = queries.shape[0]
    block_rows = math.gcd(row_count, 512)
    scaling = queries.shape[-1] ** -0.5

    def one_block(number):
        offset = number * block_rows
        query_block = lax.dynamic_slice_in_dim(queries, offset, block_rows, 0)
        labels = lax.dynamic_slice_in_dim(seg_queries, offset, block_rows, 0)
        scores = jnp.dot(query_block, key_rows.T, preferred_element_type=jnp.float32) * scaling
        scores = jnp.where(labels[:, None] == seg_keys[None, :], scores, neg_large)
        highest = jnp.max(scores, axis=1, keepdims=True)
        exponent = jnp.exp(scores - highest)
        totals = jnp.sum(exponent, axis=1, keepdims=True)
        weights = (exponent / totals).astype(jnp.bfloat16)
        blended = jnp.dot(weights, value_rows, preferred_element_type=jnp.float32).astype(jnp.bfloat16)
        return blended, highest[:, 0] + jnp.log(totals[:, 0])

    blended, log_totals = lax.map(one_block, jnp.arange(row_count // block_rows, dtype=jnp.int32))
    return blended.reshape(row_count, value_rows.shape[-1]), log_totals.reshape(row_count)


def slot_table(head_map, seq_count, slot_most):
    devices_all = jnp.arange(seq_count, dtype=jnp.int32)
    same_device = (head_map[None, :] == devices_all[:, None]).astype(jnp.int32)
    head_ranks = jnp.cumsum(same_device, axis=1) - 1
    slot_ids = jnp.arange(slot_most, dtype=jnp.int32)
    picked = same_device[:, None, :] * (head_ranks[:, None, :] == slot_ids[None, :, None]).astype(jnp.int32)
    head_ids = jnp.arange(head_map.shape[0], dtype=jnp.int32)
    head_of_slot = jnp.sum(picked * head_ids[None, None, :], axis=2)
    slot_valid = jnp.sum(picked, axis=2)
    own_rank = jnp.sum(same_device * head_ranks, axis=0)
    slot_of_head = head_map * slot_most + own_rank
    return head_of_slot, slot_valid, slot_of_head


def reference(qkv_vis, qkv_txt, vis_segments, txt_segments, head_map, w_out):
    vis_rows = qkv_vis.reshape(N_DP, VIS_SEQ, 3, HEADS, HEAD_DIM)
    txt_rows = qkv_txt.reshape(N_DP, TXT_SEQ, 3, HEADS, HEAD_DIM)
    joint_rows = jnp.concatenate([vis_rows, txt_rows], axis=1)
    labels = jnp.concatenate([vis_segments.reshape(N_DP, VIS_SEQ), txt_segments.reshape(N_DP, TXT_SEQ)], axis=1)

    def one_group(inputs):
        group_rows, group_labels = inputs

        def one_head(head_index):
            picked = lax.dynamic_index_in_dim(group_rows, head_index, 2, keepdims=False)
            return attend_rows(picked[:, 0], picked[:, 1], picked[:, 2], group_labels, group_labels)

        return lax.map(one_head, jnp.arange(HEADS, dtype=jnp.int32))

    blended, log_totals = lax.map(one_group, (joint_rows, labels))
    attention = jnp.transpose(blended, (0, 2, 1, 3)).reshape(N_DP, JOINT, INNER)
    vis_attention = attention[:, :VIS_SEQ].reshape(TOKV, INNER)
    txt_out = attention[:, VIS_SEQ:].reshape(TOKT, INNER)
    vis_out = jnp.dot(vis_attention, w_out, preferred_element_type=jnp.float32).astype(jnp.bfloat16)
    head_of_slot, slot_valid, slot_of_head = slot_table(head_map, N_SEQ, HMAX)
    gathered = jnp.take(log_totals, head_of_slot.reshape(SLOTS), axis=1)
    gathered = jnp.where(slot_valid.reshape(SLOTS)[None, :, None] > 0, gathered, jnp.zeros_like(gathered))
    lse_slots = jnp.transpose(gathered, (1, 0, 2)).reshape(SLOTS, N_DP * JOINT)
    return vis_out, txt_out, lse_slots
```

```python
import functools

import jax
import jax.numpy as jnp
from jax import lax
from jax.experimental import pallas as pl
from jax.experimental.pallas import tpu as pltpu
from jax.sharding import PartitionSpec as P

HEADS = 24
HEAD_DIM = 128
N_SEQ = 16
VIS_ROWS = 112
TXT_ROWS = 16
ROWS = VIS_ROWS + TXT_ROWS
HALF = ROWS // 2
TRIO = 3 * HEAD_DIM
CHIPS = 8
A_ROWS = 3 * ROWS
SEND_ROWS = A_ROWS + 3 * HALF
CUT_ROWS = 16
PAYLOAD = SEND_ROWS + CUT_ROWS
RET_ROWS = ROWS + HALF
VIS_SEQ = VIS_ROWS * N_SEQ
TXT_SEQ = TXT_ROWS * N_SEQ
SLOTS = 2
LOG2E = 1.4426950408889634
LN2 = 0.6931471805599453
BIG = -1e30


def pack_kernel(seg_vis, seg_txt, vq, vk, vv, tq, tk, tv, out):
    for part, (vis, txt) in enumerate(((vq, tq), (vk, tk), (vv, tv))):
        row = part * ROWS
        for core, column in ((0, 0), (1, 2 * HEAD_DIM)):
            out[core, row : row + VIS_ROWS, :] = vis[:, column : column + HEAD_DIM]
            out[core, row + VIS_ROWS : row + ROWS, :] = txt[:, column : column + HEAD_DIM]
        row = A_ROWS + part * HALF
        middle = slice(HEAD_DIM, 2 * HEAD_DIM)
        out[0, row : row + HALF, :] = vis[:HALF, middle]
        out[1, row : row + VIS_ROWS - HALF, :] = vis[HALF:, middle]
        out[1, row + VIS_ROWS - HALF : row + HALF, :] = txt[:, middle]

    def even(ref):
        parity = (ref[...] & 1).astype(jnp.float32)
        count = jnp.sum(1.0 - parity, axis=1, keepdims=True)
        return jnp.broadcast_to(count, (CUT_ROWS // 2, HEAD_DIM))

    cuts = jnp.concatenate([even(seg_vis), even(seg_txt)], axis=0).astype(jnp.bfloat16)
    out[0, SEND_ROWS:PAYLOAD, :] = cuts
    out[1, SEND_ROWS:PAYLOAD, :] = cuts


def pack(qkv_vis, qkv_txt, vis_segments, txt_segments):
    def spec(rows, part):
        return pl.BlockSpec((rows, TRIO), lambda i: (0, part * CHIPS + i))

    return pl.pallas_call(
        pack_kernel,
        grid=(CHIPS,),
        in_specs=[
            pl.BlockSpec((1, VIS_ROWS), lambda i: (0, 0)),
            pl.BlockSpec((1, TXT_ROWS), lambda i: (0, 0)),
            *[spec(VIS_ROWS, part) for part in range(3)],
            *[spec(TXT_ROWS, part) for part in range(3)],
        ],
        out_specs=pl.BlockSpec((2, PAYLOAD, HEAD_DIM), lambda i: (i, 0, 0)),
        out_shape=jax.ShapeDtypeStruct((N_SEQ, PAYLOAD, HEAD_DIM), jnp.bfloat16),
        name="pack",
    )(
        vis_segments.reshape(1, VIS_ROWS),
        txt_segments.reshape(1, TXT_ROWS),
        *[qkv_vis] * 3,
        *[qkv_txt] * 3,
    )


def second_clip(cut_ref, source, row):
    cuts = jnp.sum(cut_ref[...].astype(jnp.float32), axis=0)
    vis_cut, txt_cut = cuts[0:1, 0:1], cuts[CUT_ROWS // 2 : CUT_ROWS // 2 + 1, 0:1]
    vis_place = (source * VIS_ROWS + row).astype(jnp.float32)
    txt_place = (source * TXT_ROWS + row - VIS_ROWS).astype(jnp.float32)
    is_second = jnp.where(row < VIS_ROWS, vis_place - vis_cut, txt_place - txt_cut) >= 0.0
    return jnp.where(is_second, 1.0, 0.0)


def clip_columns(second, first_value, second_value):
    lane = lax.broadcasted_iota(jnp.int32, second.shape, 1)
    feature = jnp.where(lane == 0, first_value(second), second_value(second))
    return jnp.where(lane < 2, feature, 0.0).astype(jnp.bfloat16)


def attend_block(q, q_clip, k_wide, v_turned, keys):
    q_wide = jnp.concatenate([q, q_clip], axis=1)
    scores = lax.dot_general(
        k_wide, q_wide, (((1,), (1,)), ((), ())), preferred_element_type=jnp.float32
    )
    factor = HEAD_DIM**-0.5 * LOG2E
    highest = jnp.max(scores, axis=0, keepdims=True)
    exponent = jnp.exp2((scores - highest) * factor)
    total = jnp.sum(exponent, axis=0, keepdims=True)
    blended = jnp.dot(v_turned, exponent.astype(jnp.bfloat16), preferred_element_type=jnp.float32)
    out = jnp.swapaxes(blended * (1.0 / total), 0, 1).astype(jnp.bfloat16)
    return out, highest * HEAD_DIM**-0.5 + jnp.log2(total) * LN2


def attention_kernel(q_rows, half, *refs):
    if half is None:
        cut, q, k, v, out, lse, k_wide, v_turned = refs
        pairs = ((k, v, 0),)
    else:
        core, cut, q, own_kv, far_kv, _, out, lse, k_wide, v_turned = refs
        pairs = ((own_kv, None, 0), (far_kv, None, 1))
    step = pl.program_id(0)
    rows = ROWS if half is None else HALF

    def token(shape, first_source, offset):
        index = lax.broadcasted_iota(jnp.int32, shape, 0)
        return first_source + index // rows, index % rows + offset

    @pl.when(step == 0)
    def _():
        for k_ref, v_ref, place in pairs:
            keys = N_SEQ * rows
            offset = 0
            if half is not None:
                offset = HALF * (core[0] if place == 0 else 1 - core[0])
                kv = k_ref[...]
                k_now, v_now = kv[:, :HALF], kv[:, HALF:]
            else:
                k_now, v_now = k_ref[...], v_ref[...]
            source, row = token((keys, HEAD_DIM), 0, offset)
            second = second_clip(cut, source, row)
            at = slice(place * keys, (place + 1) * keys)
            k_wide[at, :HEAD_DIM] = k_now.reshape(keys, HEAD_DIM)
            k_wide[at, HEAD_DIM:] = clip_columns(second, lambda s: BIG * s, lambda s: BIG * (1.0 - s))
            v_turned[:, at] = jnp.swapaxes(v_now.reshape(keys, HEAD_DIM), 0, 1)

    offset = 0 if half is None else HALF * core[0]
    source, row = token((q_rows, HEAD_DIM), step * (q_rows // rows), offset)
    q_clip = clip_columns(second_clip(cut, source, row), lambda s: 1.0 - s, lambda s: s)
    result, log_total = attend_block(
        q[...].reshape(q_rows, HEAD_DIM), q_clip, k_wide[...], v_turned[...], None
    )
    out[...] = result.reshape(out.shape)
    lse[...] = log_total.reshape(lse.shape)


Q_ROWS = 256
VMEM = 48 * 2**20


def attention_cost(queries, keys):
    return pl.CostEstimate(
        flops=queries * keys * HEAD_DIM * 8,
        bytes_accessed=4 * keys * HEAD_DIM * 2,
        transcendentals=queries * keys,
    )


def attend_whole(received):
    sources = Q_ROWS // ROWS
    steps = N_SEQ // sources
    keys = N_SEQ * ROWS
    return pl.pallas_call(
        functools.partial(attention_kernel, Q_ROWS, None),
        grid=(steps,),
        in_specs=[
            pl.BlockSpec((N_SEQ, CUT_ROWS, HEAD_DIM), lambda i: (0, SEND_ROWS // CUT_ROWS, 0)),
            pl.BlockSpec((sources, ROWS, HEAD_DIM), lambda i: (i, 0, 0)),
            pl.BlockSpec((N_SEQ, ROWS, HEAD_DIM), lambda i: (0, 1, 0)),
            pl.BlockSpec((N_SEQ, ROWS, HEAD_DIM), lambda i: (0, 2, 0)),
        ],
        out_specs=[
            pl.BlockSpec((sources, ROWS, HEAD_DIM), lambda i: (i, 0, 0)),
            pl.BlockSpec((1, 1, Q_ROWS), lambda i: (i, 0, 0)),
        ],
        out_shape=[
            jax.ShapeDtypeStruct((N_SEQ, RET_ROWS, HEAD_DIM), jnp.bfloat16),
            jax.ShapeDtypeStruct((steps, 1, Q_ROWS), jnp.float32),
        ],
        scratch_shapes=[
            pltpu.VMEM((keys, 2 * HEAD_DIM), jnp.bfloat16),
            pltpu.VMEM((HEAD_DIM, keys), jnp.bfloat16),
        ],
        compiler_params=pltpu.CompilerParams(vmem_limit_bytes=VMEM),
        cost_estimate=attention_cost(keys, keys),
        name="attend_whole",
    )(*[received] * 4)


def attend_shared(core, received, far_kv, returning):
    sources = Q_ROWS // HALF
    steps = N_SEQ // sources
    keys = N_SEQ * ROWS
    return pl.pallas_call(
        functools.partial(attention_kernel, Q_ROWS, True),
        grid_spec=pltpu.PrefetchScalarGridSpec(
            num_scalar_prefetch=1,
            grid=(steps,),
            in_specs=[
                pl.BlockSpec((N_SEQ, CUT_ROWS, HEAD_DIM), lambda i, c: (0, SEND_ROWS // CUT_ROWS, 0)),
                pl.BlockSpec((sources, HALF, HEAD_DIM), lambda i, c: (i, A_ROWS // HALF, 0)),
                pl.BlockSpec((N_SEQ, 2 * HALF, HEAD_DIM), lambda i, c: (0, 0, 0)),
                pl.BlockSpec((N_SEQ, 2 * HALF, HEAD_DIM), lambda i, c: (0, 0, 0)),
                pl.BlockSpec(memory_space=pl.ANY),
            ],
            out_specs=[
                pl.BlockSpec((sources, HALF, HEAD_DIM), lambda i, c: (i, ROWS // HALF, 0)),
                pl.BlockSpec((1, 1, Q_ROWS), lambda i, c: (i, 0, 0)),
            ],
            scratch_shapes=[
                pltpu.VMEM((keys, 2 * HEAD_DIM), jnp.bfloat16),
                pltpu.VMEM((HEAD_DIM, keys), jnp.bfloat16),
            ],
        ),
        out_shape=[
            jax.ShapeDtypeStruct((N_SEQ, RET_ROWS, HEAD_DIM), jnp.bfloat16),
            jax.ShapeDtypeStruct((steps, 1, Q_ROWS), jnp.float32),
        ],
        input_output_aliases={5: 0},
        compiler_params=pltpu.CompilerParams(vmem_limit_bytes=VMEM),
        cost_estimate=attention_cost(keys // 2, keys),
        name="attend_shared",
    )(core, received, received, *far_kv, returning)


def project_kernel(core, ret, own, far, vis_out, txt_out, total):
    step = pl.program_id(0)
    columns = own.shape[1]
    pieces = []
    for chip in range(2):
        low, high = ret[2 * chip], ret[2 * chip + 1]
        shared = jnp.concatenate([low[ROWS:], high[ROWS:]], axis=0)
        pieces += [low[:ROWS], shared, high[:ROWS]]
    attention = jnp.concatenate(pieces, axis=1)
    txt_out[...] = attention[VIS_ROWS:]

    @pl.when(step == 0)
    def _():
        total[...] = jnp.zeros_like(total)

    for index, weights in ((0, own), (1, far)):
        total[index] += jnp.dot(attention, weights[...], preferred_element_type=jnp.float32)

    @pl.when(step == pl.num_programs(0) - 1)
    def _():
        for index in range(2):
            at = index + core[0] - 2 * index * core[0]
            start = pl.multiple_of(at * columns, columns)
            vis_out[:, pl.ds(start, columns)] = total[index, :VIS_ROWS].astype(jnp.bfloat16)


def project(core, returned, own, far):
    columns = own.shape[1]
    depth = 2 * TRIO
    steps = CHIPS // 2
    return pl.pallas_call(
        project_kernel,
        grid_spec=pltpu.PrefetchScalarGridSpec(
            num_scalar_prefetch=1,
            grid=(steps,),
            in_specs=[
                pl.BlockSpec((4, RET_ROWS, HEAD_DIM), lambda i, c: (i, 0, 0)),
                pl.BlockSpec((depth, columns), lambda i, c: (i, 0)),
                pl.BlockSpec((depth, columns), lambda i, c: (i, 0)),
            ],
            out_specs=[
                pl.BlockSpec((VIS_ROWS, 2 * columns), lambda i, c: (0, 0)),
                pl.BlockSpec((TXT_ROWS, depth), lambda i, c: (0, i)),
            ],
            scratch_shapes=[pltpu.VMEM((2, ROWS, columns), jnp.float32)],
        ),
        out_shape=[
            jax.ShapeDtypeStruct((VIS_ROWS, 2 * columns), jnp.bfloat16),
            jax.ShapeDtypeStruct((TXT_ROWS, HEADS * HEAD_DIM), jnp.bfloat16),
        ],
        compiler_params=pltpu.CompilerParams(vmem_limit_bytes=VMEM),
        name="project",
    )(core, returned, own, far)


def slot_rows(gathered, head_map, seq_index):
    whole = gathered[:, :N_SEQ].reshape(CHIPS, 2, N_SEQ, ROWS)
    shared = gathered[:, N_SEQ:].reshape(CHIPS, 2, N_SEQ, HALF)
    shared = jnp.concatenate([shared[:, 0], shared[:, 1]], axis=2)
    table = jnp.stack([whole[:, 0], shared, whole[:, 1]], axis=1).reshape(HEADS, N_SEQ, ROWS)
    mine = (head_map == seq_index).astype(jnp.int32)
    rank = jnp.cumsum(mine) - 1
    rows = []
    for slot in range(SLOTS):
        picked = (mine * (rank == slot)) > 0
        rows.append(jnp.sum(jnp.where(picked[:, None, None], table, 0.0), axis=0))
    rows = jnp.stack(rows)
    vis = rows[:, :, :VIS_ROWS].reshape(SLOTS, VIS_SEQ)
    txt = rows[:, :, VIS_ROWS:].reshape(SLOTS, TXT_SEQ)
    return jnp.concatenate([vis, txt], axis=1)


def on_device(qkv_vis, qkv_txt, vis_segments, txt_segments, head_map, w_out):
    seq_index = lax.axis_index("seq")
    core = seq_index % 2
    core_scalar = core.reshape(1).astype(jnp.int32)
    swap = [(i, i ^ 1) for i in range(N_SEQ)]
    columns = w_out.shape[1] // 2

    half = lax.dynamic_slice_in_dim(w_out, core * columns, columns, 1)
    own_w = lax.all_gather(half, "dp", axis=0, tiled=True)
    far_w = lax.ppermute(own_w, "seq", swap)

    sending = pack(qkv_vis, qkv_txt, vis_segments, txt_segments)
    received = lax.all_to_all(sending, "seq", split_axis=0, concat_axis=0, tiled=True)
    own_kv = received[:, A_ROWS + HALF : SEND_ROWS]
    far_kv = lax.ppermute(own_kv, "seq", swap)
    returning, lse_whole = attend_whole(received)
    returning, lse_shared = attend_shared(core_scalar, received, (own_kv, far_kv), returning)
    returned = lax.all_to_all(returning, "seq", split_axis=0, concat_axis=0, tiled=True)
    lse = jnp.concatenate([lse_whole.reshape(-1, HEAD_DIM), lse_shared.reshape(-1, HEAD_DIM)], axis=0)
    lse_slots = slot_rows(lax.all_gather(lse, "seq", axis=0), head_map, seq_index)
    vis_out, txt_out = project(core_scalar, returned, own_w, far_w)
    return vis_out, txt_out, lse_slots


def solution(mesh):
    in_specs = (
        P(("dp", "seq"), None),
        P(("dp", "seq"), None),
        P(("dp", "seq")),
        P(("dp", "seq")),
        P(),
        P("dp", None),
    )
    out_specs = (P(("dp", "seq"), None), P(("dp", "seq"), None), P("seq", "dp"))
    return jax.shard_map(
        on_device, mesh=mesh, in_specs=in_specs, out_specs=out_specs, check_vma=False
    )
```

```python
import functools

import jax
import jax.numpy as jnp
from jax import lax
from jax.experimental import pallas as pl
from jax.experimental.pallas import tpu as pltpu
from jax.sharding import PartitionSpec as P

HEADS = 24
HEAD_DIM = 128
N_SEQ = 16
VIS_ROWS = 112
TXT_ROWS = 16
ROWS = VIS_ROWS + TXT_ROWS
HALF = ROWS // 2
TRIO = 3 * HEAD_DIM
CHIPS = 8
A_ROWS = 3 * ROWS
SEND_ROWS = A_ROWS + 3 * HALF
CUT_ROWS = 16
PAYLOAD = SEND_ROWS + CUT_ROWS
RET_ROWS = ROWS + HALF
WHOLE_LSE = RET_ROWS
SHARED_LSE = WHOLE_LSE + N_SEQ
RETURN = SHARED_LSE + N_SEQ
PACK_CHIPS = 4
VIS_SEQ = VIS_ROWS * N_SEQ
TXT_SEQ = TXT_ROWS * N_SEQ
SLOTS = 2
LOG2E = 1.4426950408889634
LN2 = 0.6931471805599453
BIG = -1e30


def pack_kernel(seg_vis, seg_txt, vq, vk, vv, tq, tk, tv, out):
    def even(ref):
        parity = (ref[...] & 1).astype(jnp.float32)
        count = jnp.sum(1.0 - parity, axis=1, keepdims=True)
        return jnp.broadcast_to(count, (CUT_ROWS // 2, HEAD_DIM))

    cuts = jnp.concatenate([even(seg_vis), even(seg_txt)], axis=0).astype(jnp.bfloat16)
    for chip in range(PACK_CHIPS):
        low, high = 2 * chip, 2 * chip + 1
        for part, (vis, txt) in enumerate(((vq, tq), (vk, tk), (vv, tv))):
            row = part * ROWS
            for device, column in ((low, chip * TRIO), (high, chip * TRIO + 2 * HEAD_DIM)):
                columns = slice(column, column + HEAD_DIM)
                out[device, row : row + VIS_ROWS, :] = vis[:, columns]
                out[device, row + VIS_ROWS : row + ROWS, :] = txt[:, columns]
            row = A_ROWS + part * HALF
            columns = slice(chip * TRIO + HEAD_DIM, chip * TRIO + 2 * HEAD_DIM)
            out[low, row : row + HALF, :] = vis[:HALF, columns]
            out[high, row : row + VIS_ROWS - HALF, :] = vis[HALF:, columns]
            out[high, row + VIS_ROWS - HALF : row + HALF, :] = txt[:, columns]
        out[low, SEND_ROWS:PAYLOAD, :] = cuts
        out[high, SEND_ROWS:PAYLOAD, :] = cuts


def pack(qkv_vis, qkv_txt, vis_segments, txt_segments):
    steps = CHIPS // PACK_CHIPS

    def spec(rows, part):
        return pl.BlockSpec((rows, PACK_CHIPS * TRIO), lambda i: (0, part * steps + i))

    return pl.pallas_call(
        pack_kernel,
        grid=(steps,),
        in_specs=[
            pl.BlockSpec((1, VIS_ROWS), lambda i: (0, 0)),
            pl.BlockSpec((1, TXT_ROWS), lambda i: (0, 0)),
            *[spec(VIS_ROWS, part) for part in range(3)],
            *[spec(TXT_ROWS, part) for part in range(3)],
        ],
        out_specs=pl.BlockSpec((2 * PACK_CHIPS, PAYLOAD, HEAD_DIM), lambda i: (i, 0, 0)),
        out_shape=jax.ShapeDtypeStruct((N_SEQ, PAYLOAD, HEAD_DIM), jnp.bfloat16),
        name="pack",
    )(
        vis_segments.reshape(1, VIS_ROWS),
        txt_segments.reshape(1, TXT_ROWS),
        *[qkv_vis] * 3,
        *[qkv_txt] * 3,
    )


def second_clip(cut_ref, source, row):
    cuts = jnp.sum(cut_ref[...].astype(jnp.float32), axis=0)
    vis_cut, txt_cut = cuts[0:1, 0:1], cuts[CUT_ROWS // 2 : CUT_ROWS // 2 + 1, 0:1]
    vis_place = (source * VIS_ROWS + row).astype(jnp.float32)
    txt_place = (source * TXT_ROWS + row - VIS_ROWS).astype(jnp.float32)
    is_second = jnp.where(row < VIS_ROWS, vis_place - vis_cut, txt_place - txt_cut) >= 0.0
    return jnp.where(is_second, 1.0, 0.0)


def clip_columns(second, first_value, second_value):
    lane = lax.broadcasted_iota(jnp.int32, second.shape, 1)
    feature = jnp.where(lane == 0, first_value(second), second_value(second))
    return jnp.where(lane < 2, feature, 0.0).astype(jnp.bfloat16)


def attend(queries, k_wide, v_turned, write):
    factor = HEAD_DIM**-0.5 * LOG2E

    def score(block):
        return lax.dot_general(
            k_wide[...], queries(block), (((1,), (1,)), ((), ())), preferred_element_type=jnp.float32
        )

    blocks = STEP_ROWS // Q_ROWS
    scores = score(0)
    for block in range(blocks):
        upcoming = score(block + 1) if block + 1 < blocks else None
        highest = jnp.max(scores, axis=0, keepdims=True)
        exponent = jnp.exp2((scores - highest) * factor)
        total = jnp.sum(exponent, axis=0, keepdims=True)
        blended = jnp.dot(
            v_turned[...], exponent.astype(jnp.bfloat16), preferred_element_type=jnp.float32
        )
        result = jnp.swapaxes(blended * (1.0 / total), 0, 1).astype(jnp.bfloat16)
        write(block, result, highest * HEAD_DIM**-0.5 + jnp.log2(total) * LN2)
        scores = upcoming


def place_of(shape, rows, first_source, offset):
    index = lax.broadcasted_iota(jnp.int32, shape, 0)
    return first_source + index // rows, index % rows + offset


def key_features(cut, keys, rows, offset):
    second = second_clip(cut, *place_of((keys, HEAD_DIM), rows, 0, offset))
    return clip_columns(second, lambda s: BIG * s, lambda s: BIG * (1.0 - s))


def query_features(cut, count, rows, first_source, offset):
    second = second_clip(cut, *place_of((count, HEAD_DIM), rows, first_source, offset))
    return clip_columns(second, lambda s: 1.0 - s, lambda s: s)


def whole_kernel(cut, q, k, v, out, lse, k_wide, v_turned, q_wide):
    step = pl.program_id(0)
    keys = N_SEQ * ROWS
    sources = STEP_ROWS // ROWS

    @pl.when(step == 0)
    def _():
        k_wide[:, :HEAD_DIM] = k[...].reshape(keys, HEAD_DIM)
        k_wide[:, HEAD_DIM:] = key_features(cut, keys, ROWS, 0)
        v_turned[...] = jnp.swapaxes(v[...].reshape(keys, HEAD_DIM), 0, 1)

    q_wide[:, :HEAD_DIM] = q[...].reshape(STEP_ROWS, HEAD_DIM)
    q_wide[:, HEAD_DIM:] = query_features(cut, STEP_ROWS, ROWS, step * sources, 0)

    def write(block, result, log_total):
        count = Q_ROWS // ROWS
        out[block * count : (block + 1) * count] = result.reshape(count, ROWS, HEAD_DIM)
        for row in range(count):
            lse[block * count + row : block * count + row + 1, :] = log_total[
                :, row * HEAD_DIM : (row + 1) * HEAD_DIM
            ]

    attend(lambda block: q_wide[block * Q_ROWS : (block + 1) * Q_ROWS, :], k_wide, v_turned, write)


def shared_kernel(where, cut, q, own_kv, far_kv, whole, whole_lse, out, k_wide, v_turned, q_wide):
    core = where[2]
    keys = N_SEQ * HALF
    for place, (kv, offset) in enumerate(((own_kv, HALF * core), (far_kv, HALF * (1 - core)))):
        at = slice(place * keys, (place + 1) * keys)
        k_wide[at, :HEAD_DIM] = kv[:, :HALF].reshape(keys, HEAD_DIM)
        k_wide[at, HEAD_DIM:] = key_features(cut, keys, HALF, offset)
        v_turned[:, at] = jnp.swapaxes(kv[:, HALF:].reshape(keys, HEAD_DIM), 0, 1)
    q_wide[:, :HEAD_DIM] = q[...].reshape(STEP_ROWS, HEAD_DIM)
    q_wide[:, HEAD_DIM:] = query_features(cut, STEP_ROWS, HALF, 0, HALF * core)
    log_totals = []

    def write(block, result, log_total):
        count = Q_ROWS // HALF
        out[block * count : (block + 1) * count, ROWS:RET_ROWS, :] = result.reshape(count, HALF, HEAD_DIM)
        for row in range(Q_ROWS // HEAD_DIM):
            log_totals.append(log_total[:, row * HEAD_DIM : (row + 1) * HEAD_DIM])

    attend(lambda block: q_wide[block * Q_ROWS : (block + 1) * Q_ROWS, :], k_wide, v_turned, write)
    out[:, :ROWS, :] = whole[...]
    log_totals.append(jnp.zeros((RETURN - SHARED_LSE - len(log_totals), HEAD_DIM), jnp.float32))
    rows = jnp.concatenate([whole_lse[...], *log_totals], axis=0).astype(jnp.bfloat16)
    for device in range(N_SEQ):
        out[device, WHOLE_LSE:, :] = rows


Q_ROWS = 512
STEP_ROWS = 1024
VMEM = 40 * 2**20


def attention_scratch():
    keys = N_SEQ * ROWS
    return [
        pltpu.VMEM((keys, 2 * HEAD_DIM), jnp.bfloat16),
        pltpu.VMEM((HEAD_DIM, keys), jnp.bfloat16),
        pltpu.VMEM((STEP_ROWS, 2 * HEAD_DIM), jnp.bfloat16),
    ]


def attention_cost(queries, keys):
    return pl.CostEstimate(
        flops=queries * keys * HEAD_DIM * 8,
        bytes_accessed=4 * keys * HEAD_DIM * 2,
        transcendentals=queries * keys,
    )


def attend_whole(received):
    keys = N_SEQ * ROWS
    steps = keys // STEP_ROWS
    sources = STEP_ROWS // ROWS
    return pl.pallas_call(
        whole_kernel,
        grid=(steps,),
        in_specs=[
            pl.BlockSpec((N_SEQ, CUT_ROWS, HEAD_DIM), lambda i: (0, SEND_ROWS // CUT_ROWS, 0)),
            pl.BlockSpec((sources, ROWS, HEAD_DIM), lambda i: (i, 0, 0)),
            pl.BlockSpec((N_SEQ, ROWS, HEAD_DIM), lambda i: (0, 1, 0)),
            pl.BlockSpec((N_SEQ, ROWS, HEAD_DIM), lambda i: (0, 2, 0)),
        ],
        out_specs=[
            pl.BlockSpec((sources, ROWS, HEAD_DIM), lambda i: (i, 0, 0)),
            pl.BlockSpec((sources, ROWS), lambda i: (i, 0)),
        ],
        out_shape=[
            jax.ShapeDtypeStruct((N_SEQ, ROWS, HEAD_DIM), jnp.bfloat16),
            jax.ShapeDtypeStruct((N_SEQ, ROWS), jnp.float32),
        ],
        scratch_shapes=attention_scratch(),
        compiler_params=pltpu.CompilerParams(vmem_limit_bytes=VMEM),
        cost_estimate=attention_cost(keys, keys),
        name="attend_whole",
    )(*[received] * 4)


def attend_shared(where, received, own_kv, far_kv, whole, whole_lse):
    keys = N_SEQ * ROWS
    full = lambda *shape: pl.BlockSpec(shape, lambda i, c: (0,) * len(shape))
    return pl.pallas_call(
        shared_kernel,
        grid_spec=pltpu.PrefetchScalarGridSpec(
            num_scalar_prefetch=1,
            grid=(1,),
            in_specs=[
                pl.BlockSpec((N_SEQ, CUT_ROWS, HEAD_DIM), lambda i, c: (0, SEND_ROWS // CUT_ROWS, 0)),
                pl.BlockSpec((N_SEQ, HALF, HEAD_DIM), lambda i, c: (0, A_ROWS // HALF, 0)),
                full(N_SEQ, 2 * HALF, HEAD_DIM),
                full(N_SEQ, 2 * HALF, HEAD_DIM),
                full(N_SEQ, ROWS, HEAD_DIM),
                full(N_SEQ, ROWS),
            ],
            out_specs=full(N_SEQ, RETURN, HEAD_DIM),
            scratch_shapes=attention_scratch(),
        ),
        out_shape=jax.ShapeDtypeStruct((N_SEQ, RETURN, HEAD_DIM), jnp.bfloat16),
        compiler_params=pltpu.CompilerParams(vmem_limit_bytes=VMEM),
        cost_estimate=attention_cost(keys // 2, keys),
        name="attend_shared",
    )(where, received, received, own_kv, far_kv, whole, whole_lse)


def place_kernel(where, mine, near, near_far, part, part_far, out):
    x, core = where[1], where[2]
    sign = 1 - 2 * core
    out[x] = mine[...]
    out[(x - sign + 4) % 4] = near[...]
    out[(x + sign + 4) % 4] = near_far[...]
    columns = part.shape[1]
    low, high = pl.multiple_of(core * columns, columns), pl.multiple_of((1 - core) * columns, columns)
    opposite = (x + 2) % 4
    out[opposite, :, pl.ds(low, columns)] = part[...]
    out[opposite, :, pl.ds(high, columns)] = part_far[...]


def place(where, mine, near, near_far, part, part_far):
    rows, columns = mine.shape
    return pl.pallas_call(
        place_kernel,
        grid_spec=pltpu.PrefetchScalarGridSpec(
            num_scalar_prefetch=1,
            grid=(),
            in_specs=[pl.BlockSpec(memory_space=pltpu.VMEM)] * 5,
            out_specs=pl.BlockSpec(memory_space=pltpu.VMEM),
        ),
        out_shape=jax.ShapeDtypeStruct((4, rows, columns), jnp.bfloat16),
        name="place",
    )(where, mine, near, near_far, part, part_far)


def slot_of(ret, head):
    chip, member = head // 3, head % 3
    low, high = ret.at[2 * chip], ret.at[2 * chip + 1]
    lane = lax.broadcasted_iota(jnp.int32, (1, HEAD_DIM), 1)
    rows = []
    for source in range(N_SEQ):
        whole = [ref[WHOLE_LSE : WHOLE_LSE + N_SEQ, :].astype(jnp.float32) for ref in (low, high)]
        shared = [ref[SHARED_LSE : SHARED_LSE + N_SEQ, :].astype(jnp.float32) for ref in (low, high)]
        left, right = (item[source // 2 : source // 2 + 1] for item in shared)
        if source % 2 == 0:
            right = pltpu.roll(right, HALF, 1)
        else:
            left = pltpu.roll(left, HALF, 1)
        both = jnp.where(lane < HALF, left, right)
        first, last = (item[source : source + 1] for item in whole)
        rows.append(jnp.where(member == 0, first, jnp.where(member == 1, both, last)))
    return rows


def project_kernel(where, ret, *refs):
    weights, (vis_out, txt_out, slots, held, sems) = refs[:9], refs[9:]
    y, core = where[0], where[2]
    sign = 1 - 2 * core
    columns = held.shape[2] // 2
    copies = []
    for index in range(7):
        copies.append(pltpu.make_async_copy(weights[index], held.at[index], sems.at[index]))
    for index in range(2):
        at = core if index == 0 else 1 - core
        start = pl.multiple_of(at * columns, columns)
        copies.append(
            pltpu.make_async_copy(
                weights[7 + index], held.at[7, :, pl.ds(start, columns)], sems.at[7 + index]
            )
        )
    for copy in copies:
        copy.start()
    for slot in range(SLOTS):
        valid = where[5 + slot] > 0
        for source, row in enumerate(slot_of(ret, where[3 + slot])):
            row = jnp.where(valid, row, 0.0)
            at = source * VIS_ROWS
            slots[slot : slot + 1, at : at + VIS_ROWS] = row[:, :VIS_ROWS]
            at = VIS_SEQ + source * TXT_ROWS
            slots[slot : slot + 1, at : at + TXT_ROWS] = row[:, VIS_ROWS:]
    total = jnp.zeros((ROWS, 2 * columns), jnp.float32)
    for index, hops in enumerate((0, 1, 2, 3, -1, -2, -3, 4)):
        chip = (y - hops * sign + 8) % 8
        low, high = ret[2 * chip], ret[2 * chip + 1]
        shared = jnp.concatenate([low[ROWS:RET_ROWS], high[ROWS:RET_ROWS]], axis=0)
        attention = jnp.concatenate([low[:ROWS], shared, high[:ROWS]], axis=1)
        txt_out[:, pl.ds(pl.multiple_of(chip * TRIO, TRIO), TRIO)] = attention[VIS_ROWS:]
        copies[index].wait()
        if index == 7:
            copies[8].wait()
        total += jnp.dot(attention, held[index], preferred_element_type=jnp.float32)
    vis_out[...] = total[:VIS_ROWS].astype(jnp.bfloat16)


def project(where, returned, chunks, far_chunks):
    columns = chunks[0].shape[1]
    return pl.pallas_call(
        project_kernel,
        grid_spec=pltpu.PrefetchScalarGridSpec(
            num_scalar_prefetch=1,
            grid=(),
            in_specs=[pl.BlockSpec(memory_space=pltpu.VMEM)] + [pl.BlockSpec(memory_space=pl.ANY)] * 9,
            out_specs=[pl.BlockSpec(memory_space=pltpu.VMEM)] * 3,
            scratch_shapes=[
                pltpu.VMEM((8, TRIO, columns), jnp.bfloat16),
                pltpu.SemaphoreType.DMA((9,)),
            ],
        ),
        out_shape=[
            jax.ShapeDtypeStruct((VIS_ROWS, columns), jnp.bfloat16),
            jax.ShapeDtypeStruct((TXT_ROWS, HEADS * HEAD_DIM), jnp.bfloat16),
            jax.ShapeDtypeStruct((SLOTS, VIS_SEQ + TXT_SEQ), jnp.float32),
        ],
        compiler_params=pltpu.CompilerParams(vmem_limit_bytes=VMEM),
        name="project",
    )(where, returned, *chunks[:4], *far_chunks[:3], chunks[4], far_chunks[3])


AXES = ("dp", "seq")
X_SIZE = 4
Y_SIZE = 8


def permute(operand, target):
    pairs = []
    for y in range(Y_SIZE):
        for x in range(X_SIZE):
            for s in range(N_SEQ):
                ty, tx, ts = target(y, x, s)
                there = (ty % Y_SIZE) * X_SIZE + tx % X_SIZE
                pairs.append(((y * X_SIZE + x) * N_SEQ + s, there * N_SEQ + ts))
    return lax.ppermute(operand, AXES, pairs)


def swap(operand):
    return permute(operand, lambda y, x, s: (y, x, s ^ 1))


def shift_x(operand, hops):
    return permute(operand, lambda y, x, s: (y, x + hops * (1 - 2 * (s % 2)), s))


def shift_y(operand):
    return permute(operand, lambda y, x, s: (y + 1 - 2 * (s % 2), x, s))


def heads_of_slots(head_map, seq_index):
    mine = (head_map == seq_index).astype(jnp.int32)
    rank = jnp.cumsum(mine) - 1
    ids = jnp.arange(HEADS, dtype=jnp.int32)
    picked = mine[None] * (rank[None] == jnp.arange(SLOTS, dtype=jnp.int32)[:, None])
    return jnp.concatenate([jnp.sum(picked * ids[None], axis=1), jnp.sum(picked, axis=1)])


def on_device(qkv_vis, qkv_txt, vis_segments, txt_segments, head_map, w_out):
    seq_index = lax.axis_index("seq")
    dp_index = lax.axis_index("dp")
    core = seq_index % 2
    half = w_out.shape[1] // 2
    place_here = jnp.stack([dp_index // X_SIZE, dp_index % X_SIZE, core]).astype(jnp.int32)
    where = jnp.concatenate([place_here, heads_of_slots(head_map, seq_index)])

    near = shift_x(w_out, 1)
    part = shift_x(lax.dynamic_slice_in_dim(w_out, core * half, half, 1), 2)
    sending = pack(qkv_vis, qkv_txt, vis_segments, txt_segments)
    sending, near, part = lax.optimization_barrier((sending, near, part))
    received = lax.all_to_all(sending, "seq", split_axis=0, concat_axis=0, tiled=True)
    chunks = [place(where, w_out, near, swap(near), part, swap(part)).reshape(-1, 2 * half)]
    chunks.append(shift_y(chunks[0]))
    chunks.append(shift_y(chunks[1]))
    received, chunks[2] = lax.optimization_barrier((received, chunks[2]))
    chunks.append(shift_y(chunks[2]))
    own_kv = received[:, A_ROWS + HALF : SEND_ROWS]
    far_kv = swap(own_kv)
    whole, whole_lse = attend_whole(received)
    returning = attend_shared(where, received, own_kv, far_kv, whole, whole_lse)
    returning, chunks[1], chunks[2], chunks[3] = lax.optimization_barrier((returning, *chunks[1:]))
    returned = lax.all_to_all(returning, "seq", split_axis=0, concat_axis=0, tiled=True)
    chunks.append(shift_y(lax.dynamic_slice_in_dim(chunks[3], core * half, half, 1)))
    far_chunks = [swap(chunk) for chunk in chunks[1:]]
    vis_out, txt_out, lse_slots = project(where, returned, chunks, far_chunks)
    return vis_out, txt_out, lse_slots


def solution(mesh):
    in_specs = (
        P(("dp", "seq"), None),
        P(("dp", "seq"), None),
        P(("dp", "seq")),
        P(("dp", "seq")),
        P(),
        P("dp", None),
    )
    out_specs = (P(("dp", "seq"), None), P(("dp", "seq"), None), P("seq", "dp"))
    return jax.shard_map(
        on_device, mesh=mesh, in_specs=in_specs, out_specs=out_specs, check_vma=False
    )
```

```python
import functools

import jax
import jax.numpy as jnp
from jax import lax
from jax.experimental import pallas as pl
from jax.experimental.pallas import tpu as pltpu
from jax.sharding import PartitionSpec as P

HEADS = 24
HEAD_DIM = 128
N_SEQ = 16
VIS_ROWS = 112
TXT_ROWS = 16
ROWS = VIS_ROWS + TXT_ROWS
HALF = ROWS // 2
TRIO = 3 * HEAD_DIM
CHIPS = 8
A_ROWS = 3 * ROWS
SEND_ROWS = A_ROWS + 3 * HALF
CUT_ROWS = 16
PAYLOAD = SEND_ROWS + CUT_ROWS
RET_ROWS = ROWS + HALF
WHOLE_LSE = RET_ROWS
SHARED_LSE = WHOLE_LSE + N_SEQ
RETURN = SHARED_LSE + N_SEQ
PACK_CHIPS = 4
VIS_SEQ = VIS_ROWS * N_SEQ
TXT_SEQ = TXT_ROWS * N_SEQ
SLOTS = 2
LOG2E = 1.4426950408889634
LN2 = 0.6931471805599453
BIG = -1e30


def pack_kernel(seg_vis, seg_txt, vq, vk, vv, tq, tk, tv, out):
    def even(ref):
        parity = (ref[...] & 1).astype(jnp.float32)
        count = jnp.sum(1.0 - parity, axis=1, keepdims=True)
        return jnp.broadcast_to(count, (CUT_ROWS // 2, HEAD_DIM))

    cuts = jnp.concatenate([even(seg_vis), even(seg_txt)], axis=0).astype(jnp.bfloat16)
    for chip in range(PACK_CHIPS):
        low, high = 2 * chip, 2 * chip + 1
        for part, (vis, txt) in enumerate(((vq, tq), (vk, tk), (vv, tv))):
            row = part * ROWS
            for device, column in ((low, chip * TRIO), (high, chip * TRIO + 2 * HEAD_DIM)):
                columns = slice(column, column + HEAD_DIM)
                out[device, row : row + VIS_ROWS, :] = vis[:, columns]
                out[device, row + VIS_ROWS : row + ROWS, :] = txt[:, columns]
            row = A_ROWS + part * HALF
            columns = slice(chip * TRIO + HEAD_DIM, chip * TRIO + 2 * HEAD_DIM)
            out[low, row : row + HALF, :] = vis[:HALF, columns]
            out[high, row : row + VIS_ROWS - HALF, :] = vis[HALF:, columns]
            out[high, row + VIS_ROWS - HALF : row + HALF, :] = txt[:, columns]
        out[low, SEND_ROWS:PAYLOAD, :] = cuts
        out[high, SEND_ROWS:PAYLOAD, :] = cuts


def pack(qkv_vis, qkv_txt, vis_segments, txt_segments):
    steps = CHIPS // PACK_CHIPS

    def spec(rows, part):
        return pl.BlockSpec((rows, PACK_CHIPS * TRIO), lambda i: (0, part * steps + i))

    return pl.pallas_call(
        pack_kernel,
        grid=(steps,),
        in_specs=[
            pl.BlockSpec((1, VIS_ROWS), lambda i: (0, 0)),
            pl.BlockSpec((1, TXT_ROWS), lambda i: (0, 0)),
            *[spec(VIS_ROWS, part) for part in range(3)],
            *[spec(TXT_ROWS, part) for part in range(3)],
        ],
        out_specs=pl.BlockSpec((2 * PACK_CHIPS, PAYLOAD, HEAD_DIM), lambda i: (i, 0, 0)),
        out_shape=jax.ShapeDtypeStruct((N_SEQ, PAYLOAD, HEAD_DIM), jnp.bfloat16),
        name="pack",
    )(
        vis_segments.reshape(1, VIS_ROWS),
        txt_segments.reshape(1, TXT_ROWS),
        *[qkv_vis] * 3,
        *[qkv_txt] * 3,
    )


def second_clip(cut_ref, source, row):
    cuts = jnp.sum(cut_ref[...].astype(jnp.float32), axis=0)
    vis_cut, txt_cut = cuts[0:1, 0:1], cuts[CUT_ROWS // 2 : CUT_ROWS // 2 + 1, 0:1]
    vis_place = (source * VIS_ROWS + row).astype(jnp.float32)
    txt_place = (source * TXT_ROWS + row - VIS_ROWS).astype(jnp.float32)
    is_second = jnp.where(row < VIS_ROWS, vis_place - vis_cut, txt_place - txt_cut) >= 0.0
    return jnp.where(is_second, 1.0, 0.0)


def clip_columns(second, first_value, second_value):
    lane = lax.broadcasted_iota(jnp.int32, second.shape, 1)
    feature = jnp.where(lane == 0, first_value(second), second_value(second))
    return jnp.where(lane < 2, feature, 0.0).astype(jnp.bfloat16)


def attend(queries, k_wide, v_turned, write):
    factor = HEAD_DIM**-0.5 * LOG2E

    def score(block):
        return lax.dot_general(
            k_wide[...], queries(block), (((1,), (1,)), ((), ())), preferred_element_type=jnp.float32
        )

    blocks = STEP_ROWS // Q_ROWS
    scores = score(0)
    for block in range(blocks):
        upcoming = score(block + 1) if block + 1 < blocks else None
        highest = jnp.max(scores, axis=0, keepdims=True)
        exponent = jnp.exp2((scores - highest) * factor)
        total = jnp.sum(exponent, axis=0, keepdims=True)
        blended = jnp.dot(
            v_turned[...], exponent.astype(jnp.bfloat16), preferred_element_type=jnp.float32
        )
        result = jnp.swapaxes(blended * (1.0 / total), 0, 1).astype(jnp.bfloat16)
        write(block, result, highest * HEAD_DIM**-0.5 + jnp.log2(total) * LN2)
        scores = upcoming


def place_of(shape, rows, first_source, offset):
    index = lax.broadcasted_iota(jnp.int32, shape, 0)
    return first_source + index // rows, index % rows + offset


def key_features(cut, keys, rows, offset):
    second = second_clip(cut, *place_of((keys, HEAD_DIM), rows, 0, offset))
    return clip_columns(second, lambda s: BIG * s, lambda s: BIG * (1.0 - s))


def query_features(cut, count, rows, first_source, offset):
    second = second_clip(cut, *place_of((count, HEAD_DIM), rows, first_source, offset))
    return clip_columns(second, lambda s: 1.0 - s, lambda s: s)


def whole_kernel(cut, q, k, v, out, lse, k_wide, v_turned, q_wide):
    step = pl.program_id(0)
    keys = N_SEQ * ROWS
    sources = STEP_ROWS // ROWS

    @pl.when(step == 0)
    def _():
        k_wide[:, :HEAD_DIM] = k[...].reshape(keys, HEAD_DIM)
        k_wide[:, HEAD_DIM:] = key_features(cut, keys, ROWS, 0)
        v_turned[...] = jnp.swapaxes(v[...].reshape(keys, HEAD_DIM), 0, 1)

    q_wide[:, :HEAD_DIM] = q[...].reshape(STEP_ROWS, HEAD_DIM)
    q_wide[:, HEAD_DIM:] = query_features(cut, STEP_ROWS, ROWS, step * sources, 0)

    def write(block, result, log_total):
        count = Q_ROWS // ROWS
        out[block * count : (block + 1) * count] = result.reshape(count, ROWS, HEAD_DIM)
        for row in range(count):
            lse[block * count + row : block * count + row + 1, :] = log_total[
                :, row * HEAD_DIM : (row + 1) * HEAD_DIM
            ]

    attend(lambda block: q_wide[block * Q_ROWS : (block + 1) * Q_ROWS, :], k_wide, v_turned, write)


def shared_kernel(where, cut, q, own_kv, far_kv, whole, whole_lse, out, k_wide, v_turned, q_wide):
    core = where[2]
    keys = N_SEQ * HALF
    for place, (kv, offset) in enumerate(((own_kv, HALF * core), (far_kv, HALF * (1 - core)))):
        at = slice(place * keys, (place + 1) * keys)
        k_wide[at, :HEAD_DIM] = kv[:, :HALF].reshape(keys, HEAD_DIM)
        k_wide[at, HEAD_DIM:] = key_features(cut, keys, HALF, offset)
        v_turned[:, at] = jnp.swapaxes(kv[:, HALF:].reshape(keys, HEAD_DIM), 0, 1)
    q_wide[:, :HEAD_DIM] = q[...].reshape(STEP_ROWS, HEAD_DIM)
    q_wide[:, HEAD_DIM:] = query_features(cut, STEP_ROWS, HALF, 0, HALF * core)
    log_totals = []

    def write(block, result, log_total):
        count = Q_ROWS // HALF
        out[block * count : (block + 1) * count, ROWS:RET_ROWS, :] = result.reshape(count, HALF, HEAD_DIM)
        for row in range(Q_ROWS // HEAD_DIM):
            log_totals.append(log_total[:, row * HEAD_DIM : (row + 1) * HEAD_DIM])

    attend(lambda block: q_wide[block * Q_ROWS : (block + 1) * Q_ROWS, :], k_wide, v_turned, write)
    out[:, :ROWS, :] = whole[...]
    log_totals.append(jnp.zeros((RETURN - SHARED_LSE - len(log_totals), HEAD_DIM), jnp.float32))
    rows = jnp.concatenate([whole_lse[...], *log_totals], axis=0).astype(jnp.bfloat16)
    for device in range(N_SEQ):
        out[device, WHOLE_LSE:, :] = rows


Q_ROWS = 512
STEP_ROWS = 1024
VMEM = 32 * 2**20
PROJECT_VMEM = 50 * 2**20


def attention_scratch():
    keys = N_SEQ * ROWS
    return [
        pltpu.VMEM((keys, 2 * HEAD_DIM), jnp.bfloat16),
        pltpu.VMEM((HEAD_DIM, keys), jnp.bfloat16),
        pltpu.VMEM((STEP_ROWS, 2 * HEAD_DIM), jnp.bfloat16),
    ]


def attention_cost(queries, keys):
    return pl.CostEstimate(
        flops=queries * keys * HEAD_DIM // 4,
        bytes_accessed=4 * keys * HEAD_DIM * 2,
        transcendentals=0,
    )


def attend_whole(received):
    keys = N_SEQ * ROWS
    steps = keys // STEP_ROWS
    sources = STEP_ROWS // ROWS
    return pl.pallas_call(
        whole_kernel,
        grid=(steps,),
        in_specs=[
            pl.BlockSpec((N_SEQ, CUT_ROWS, HEAD_DIM), lambda i: (0, SEND_ROWS // CUT_ROWS, 0)),
            pl.BlockSpec((sources, ROWS, HEAD_DIM), lambda i: (i, 0, 0)),
            pl.BlockSpec((N_SEQ, ROWS, HEAD_DIM), lambda i: (0, 1, 0)),
            pl.BlockSpec((N_SEQ, ROWS, HEAD_DIM), lambda i: (0, 2, 0)),
        ],
        out_specs=[
            pl.BlockSpec((sources, ROWS, HEAD_DIM), lambda i: (i, 0, 0)),
            pl.BlockSpec((sources, ROWS), lambda i: (i, 0)),
        ],
        out_shape=[
            jax.ShapeDtypeStruct((N_SEQ, ROWS, HEAD_DIM), jnp.bfloat16),
            jax.ShapeDtypeStruct((N_SEQ, ROWS), jnp.float32),
        ],
        scratch_shapes=attention_scratch(),
        compiler_params=pltpu.CompilerParams(vmem_limit_bytes=VMEM),
        cost_estimate=attention_cost(keys, keys),
        name="attend_whole",
    )(*[received] * 4)


def attend_shared(where, received, own_kv, far_kv, whole, whole_lse):
    keys = N_SEQ * ROWS
    full = lambda *shape: pl.BlockSpec(shape, lambda i, c: (0,) * len(shape))
    return pl.pallas_call(
        shared_kernel,
        grid_spec=pltpu.PrefetchScalarGridSpec(
            num_scalar_prefetch=1,
            grid=(1,),
            in_specs=[
                pl.BlockSpec((N_SEQ, CUT_ROWS, HEAD_DIM), lambda i, c: (0, SEND_ROWS // CUT_ROWS, 0)),
                pl.BlockSpec((N_SEQ, HALF, HEAD_DIM), lambda i, c: (0, A_ROWS // HALF, 0)),
                full(N_SEQ, 2 * HALF, HEAD_DIM),
                full(N_SEQ, 2 * HALF, HEAD_DIM),
                full(N_SEQ, ROWS, HEAD_DIM),
                full(N_SEQ, ROWS),
            ],
            out_specs=full(N_SEQ, RETURN, HEAD_DIM),
            scratch_shapes=attention_scratch(),
        ),
        out_shape=jax.ShapeDtypeStruct((N_SEQ, RETURN, HEAD_DIM), jnp.bfloat16),
        compiler_params=pltpu.CompilerParams(vmem_limit_bytes=VMEM),
        cost_estimate=attention_cost(keys // 2, keys),
        name="attend_shared",
    )(where, received, received, own_kv, far_kv, whole, whole_lse)


def place_kernel(where, mine, near, near_far, part, part_far, out, sems):
    x, core = where[1], where[2]
    sign = 1 - 2 * core

    def copy(source, to, index):
        return pltpu.make_async_copy(source, out.at[(to + 4) % 4], sems.at[index])

    copies = [copy(mine, x, 0), copy(near, x - sign, 1), copy(near_far, x + sign, 2)]
    for item in copies:
        item.start()

    @pl.when(core == 0)
    def _():
        copy(part, x + 2, 3).start()

    @pl.when(core == 1)
    def _():
        copy(part_far, x + 2, 3).start()

    for item in copies + [copy(part, x + 2, 3)]:
        item.wait()


def place(where, mine, near, near_far, part, part_far):
    rows, columns = mine.shape
    return pl.pallas_call(
        place_kernel,
        grid_spec=pltpu.PrefetchScalarGridSpec(
            num_scalar_prefetch=1,
            grid=(),
            in_specs=[pl.BlockSpec(memory_space=pl.ANY)] * 5,
            out_specs=pl.BlockSpec(memory_space=pl.ANY),
            scratch_shapes=[pltpu.SemaphoreType.DMA((4,))],
        ),
        out_shape=jax.ShapeDtypeStruct((4, rows, columns), jnp.bfloat16),
        name="place",
    )(where, mine, near, near_far, part, part_far)


def slot_of(ret, head):
    chip, member = head // 3, head % 3
    low, high = ret.at[2 * chip], ret.at[2 * chip + 1]
    lane = lax.broadcasted_iota(jnp.int32, (1, HEAD_DIM), 1)
    rows = []
    for source in range(N_SEQ):
        whole = [ref[WHOLE_LSE : WHOLE_LSE + N_SEQ, :].astype(jnp.float32) for ref in (low, high)]
        shared = [ref[SHARED_LSE : SHARED_LSE + N_SEQ, :].astype(jnp.float32) for ref in (low, high)]
        left, right = (item[source // 2 : source // 2 + 1] for item in shared)
        if source % 2 == 0:
            right = pltpu.roll(right, HALF, 1)
        else:
            left = pltpu.roll(left, HALF, 1)
        both = jnp.where(lane < HALF, left, right)
        first, last = (item[source : source + 1] for item in whole)
        rows.append(jnp.where(member == 0, first, jnp.where(member == 1, both, last)))
    return rows


def stage_kernel(where, *refs):
    weights, out, sems = refs[:9], refs[9], refs[10]
    core = where[2]
    columns = out.shape[2] // 2
    copies = []
    for index in range(7):
        to = out.at[index // 2, pl.ds(index % 2 * TRIO, TRIO)]
        copies.append(pltpu.make_async_copy(weights[index], to, sems.at[index]))
    for index in range(2):
        at = core if index == 0 else 1 - core
        start = pl.multiple_of(at * columns, columns)
        to = out.at[3, pl.ds(TRIO, TRIO), pl.ds(start, columns)]
        copies.append(pltpu.make_async_copy(weights[7 + index], to, sems.at[7 + index]))
    for copy in copies:
        copy.start()
    for copy in copies:
        copy.wait()


def stage(where, chunks, far_chunks):
    columns = chunks[0].shape[1]
    return pl.pallas_call(
        stage_kernel,
        grid_spec=pltpu.PrefetchScalarGridSpec(
            num_scalar_prefetch=1,
            grid=(),
            in_specs=[pl.BlockSpec(memory_space=pl.ANY)] * 9,
            out_specs=pl.BlockSpec(memory_space=pl.ANY),
            scratch_shapes=[pltpu.SemaphoreType.DMA((9,))],
        ),
        out_shape=jax.ShapeDtypeStruct((4, 2 * TRIO, columns), jnp.bfloat16),
        name="stage",
    )(where, *chunks[:4], *far_chunks[:3], chunks[4], far_chunks[3])


HOPS = (0, 1, 2, 3, -1, -2, -3, 4)


def project_kernel(where, ret, weights, vis_out, txt_out, slots, held, sems):
    y, core = where[0], where[2]
    sign = 1 - 2 * core
    copies = [
        pltpu.make_async_copy(weights.at[block], held.at[block], sems.at[block])
        for block in range(weights.shape[0])
    ]
    for copy in copies:
        copy.start()
    total = jnp.zeros((ROWS, weights.shape[2]), jnp.float32)
    pieces = []
    for index, hops in enumerate(HOPS):
        chip = (y - hops * sign + 8) % 8
        low, high = ret[2 * chip], ret[2 * chip + 1]
        shared = jnp.concatenate([low[ROWS:RET_ROWS], high[ROWS:RET_ROWS]], axis=0)
        attention = jnp.concatenate([low[:ROWS], shared, high[:ROWS]], axis=1)
        txt_out[:, pl.ds(pl.multiple_of(chip * TRIO, TRIO), TRIO)] = attention[VIS_ROWS:]
        pieces.append(attention)
        if index % 2 == 1:
            both = jnp.concatenate(pieces[-2:], axis=1)
            copies[index // 2].wait()
            total += jnp.dot(both, held[index // 2], preferred_element_type=jnp.float32)
    vis_out[...] = total[:VIS_ROWS].astype(jnp.bfloat16)
    for slot in range(SLOTS):
        valid = where[5 + slot] > 0
        for source, row in enumerate(slot_of(ret, where[3 + slot])):
            row = jnp.where(valid, row, 0.0)
            at = source * VIS_ROWS
            slots[slot : slot + 1, at : at + VIS_ROWS] = row[:, :VIS_ROWS]
            at = VIS_SEQ + source * TXT_ROWS
            slots[slot : slot + 1, at : at + TXT_ROWS] = row[:, VIS_ROWS:]


def project(where, returned, weights):
    columns = weights.shape[2]
    return pl.pallas_call(
        project_kernel,
        grid_spec=pltpu.PrefetchScalarGridSpec(
            num_scalar_prefetch=1,
            grid=(),
            in_specs=[pl.BlockSpec(memory_space=pltpu.VMEM), pl.BlockSpec(memory_space=pl.ANY)],
            out_specs=[pl.BlockSpec(memory_space=pltpu.VMEM)] * 3,
            scratch_shapes=[
                pltpu.VMEM(weights.shape, jnp.bfloat16),
                pltpu.SemaphoreType.DMA((weights.shape[0],)),
            ],
        ),
        out_shape=[
            jax.ShapeDtypeStruct((VIS_ROWS, columns), jnp.bfloat16),
            jax.ShapeDtypeStruct((TXT_ROWS, HEADS * HEAD_DIM), jnp.bfloat16),
            jax.ShapeDtypeStruct((SLOTS, VIS_SEQ + TXT_SEQ), jnp.float32),
        ],
        compiler_params=pltpu.CompilerParams(vmem_limit_bytes=PROJECT_VMEM),
        name="project",
    )(where, returned, weights)


AXES = ("dp", "seq")
X_SIZE = 4
Y_SIZE = 8


def permute(operand, target, cores=(0, 1)):
    pairs = []
    for y in range(Y_SIZE):
        for x in range(X_SIZE):
            for s in range(N_SEQ):
                ty, tx, ts = target(y, x, s)
                there = (ty % Y_SIZE) * X_SIZE + tx % X_SIZE
                if s % 2 in cores:
                    pairs.append(((y * X_SIZE + x) * N_SEQ + s, there * N_SEQ + ts))
    return lax.ppermute(operand, AXES, pairs)


def swap(operand, cores=(0, 1)):
    return permute(operand, lambda y, x, s: (y, x, s ^ 1), cores)


def shift_x(operand, hops, cores=(0, 1)):
    return permute(operand, lambda y, x, s: (y, x + hops * (1 - 2 * (s % 2)), s), cores)


def shift_y(operand):
    return permute(operand, lambda y, x, s: (y + 1 - 2 * (s % 2), x, s))


def heads_of_slots(head_map, seq_index):
    mine = (head_map == seq_index).astype(jnp.int32)
    rank = jnp.cumsum(mine) - 1
    ids = jnp.arange(HEADS, dtype=jnp.int32)
    picked = mine[None] * (rank[None] == jnp.arange(SLOTS, dtype=jnp.int32)[:, None])
    return jnp.concatenate([jnp.sum(picked * ids[None], axis=1), jnp.sum(picked, axis=1)])


def on_device(qkv_vis, qkv_txt, vis_segments, txt_segments, head_map, w_out):
    seq_index = lax.axis_index("seq")
    dp_index = lax.axis_index("dp")
    core = seq_index % 2
    half = w_out.shape[1] // 2
    place_here = jnp.stack([dp_index // X_SIZE, dp_index % X_SIZE, core]).astype(jnp.int32)
    where = jnp.concatenate([place_here, heads_of_slots(head_map, seq_index)])

    near = shift_x(w_out, 1)
    part = shift_x(w_out, 2, cores=(0,))
    sending = pack(qkv_vis, qkv_txt, vis_segments, txt_segments)
    received = lax.all_to_all(sending, "seq", split_axis=0, concat_axis=0, tiled=True)
    chunks = [place(where, w_out, near, swap(near), part, swap(part, cores=(0,))).reshape(-1, 2 * half)]
    chunks.append(shift_y(chunks[0]))
    chunks.append(shift_y(chunks[1]))
    chunks.append(shift_y(chunks[2]))
    own_kv = received[:, A_ROWS + HALF : SEND_ROWS]
    far_kv = swap(own_kv)
    whole, whole_lse = attend_whole(received)
    returning = attend_shared(where, received, own_kv, far_kv, whole, whole_lse)
    returning, chunks[1], chunks[2], chunks[3] = lax.optimization_barrier((returning, *chunks[1:]))
    returned = lax.all_to_all(returning, "seq", split_axis=0, concat_axis=0, tiled=True)
    chunks.append(shift_y(lax.dynamic_slice_in_dim(chunks[3], core * half, half, 1)))
    far_chunks = [swap(chunk) for chunk in chunks[1:]]
    vis_out, txt_out, lse_slots = project(where, returned, stage(where, chunks, far_chunks))
    return vis_out, txt_out, lse_slots


def solution(mesh):
    in_specs = (
        P(("dp", "seq"), None),
        P(("dp", "seq"), None),
        P(("dp", "seq")),
        P(("dp", "seq")),
        P(),
        P("dp", None),
    )
    out_specs = (P(("dp", "seq"), None), P(("dp", "seq"), None), P("seq", "dp"))
    return jax.shard_map(
        on_device, mesh=mesh, in_specs=in_specs, out_specs=out_specs, check_vma=False
    )
```

```python
import functools

import jax
import jax.numpy as jnp
from jax import lax
from jax.experimental import pallas as pl
from jax.experimental.pallas import tpu as pltpu
from jax.sharding import PartitionSpec as P

HEADS = 24
HEAD_DIM = 128
N_SEQ = 16
VIS_ROWS = 112
TXT_ROWS = 16
ROWS = VIS_ROWS + TXT_ROWS
HALF = ROWS // 2
TRIO = 3 * HEAD_DIM
CHIPS = 8
A_ROWS = 3 * ROWS
SEND_ROWS = A_ROWS + 3 * HALF
CUT_ROWS = 16
PAYLOAD = SEND_ROWS + CUT_ROWS
RET_ROWS = ROWS + HALF
WHOLE_LSE = RET_ROWS
SHARED_LSE = WHOLE_LSE + N_SEQ
RETURN = SHARED_LSE + N_SEQ
PACK_CHIPS = 4
VIS_SEQ = VIS_ROWS * N_SEQ
TXT_SEQ = TXT_ROWS * N_SEQ
SLOTS = 2
LOG2E = 1.4426950408889634
LN2 = 0.6931471805599453
BIG = -1e30


def pack_kernel(seg_vis, seg_txt, vq, vk, vv, tq, tk, tv, out):
    def even(ref):
        parity = (ref[...] & 1).astype(jnp.float32)
        count = jnp.sum(1.0 - parity, axis=1, keepdims=True)
        return jnp.broadcast_to(count, (CUT_ROWS // 2, HEAD_DIM))

    cuts = jnp.concatenate([even(seg_vis), even(seg_txt)], axis=0).astype(jnp.bfloat16)
    for chip in range(PACK_CHIPS):
        low, high = 2 * chip, 2 * chip + 1
        for part, (vis, txt) in enumerate(((vq, tq), (vk, tk), (vv, tv))):
            row = part * ROWS
            for device, column in ((low, chip * TRIO), (high, chip * TRIO + 2 * HEAD_DIM)):
                columns = slice(column, column + HEAD_DIM)
                out[device, row : row + VIS_ROWS, :] = vis[:, columns]
                out[device, row + VIS_ROWS : row + ROWS, :] = txt[:, columns]
            row = A_ROWS + part * HALF
            columns = slice(chip * TRIO + HEAD_DIM, chip * TRIO + 2 * HEAD_DIM)
            out[low, row : row + HALF, :] = vis[:HALF, columns]
            out[high, row : row + VIS_ROWS - HALF, :] = vis[HALF:, columns]
            out[high, row + VIS_ROWS - HALF : row + HALF, :] = txt[:, columns]
        out[low, SEND_ROWS:PAYLOAD, :] = cuts
        out[high, SEND_ROWS:PAYLOAD, :] = cuts


def pack(qkv_vis, qkv_txt, vis_segments, txt_segments):
    steps = CHIPS // PACK_CHIPS

    def spec(rows, part):
        return pl.BlockSpec((rows, PACK_CHIPS * TRIO), lambda i: (0, part * steps + i))

    return pl.pallas_call(
        pack_kernel,
        grid=(steps,),
        in_specs=[
            pl.BlockSpec((1, VIS_ROWS), lambda i: (0, 0)),
            pl.BlockSpec((1, TXT_ROWS), lambda i: (0, 0)),
            *[spec(VIS_ROWS, part) for part in range(3)],
            *[spec(TXT_ROWS, part) for part in range(3)],
        ],
        out_specs=pl.BlockSpec((2 * PACK_CHIPS, PAYLOAD, HEAD_DIM), lambda i: (i, 0, 0)),
        out_shape=jax.ShapeDtypeStruct((N_SEQ, PAYLOAD, HEAD_DIM), jnp.bfloat16),
        name="pack",
    )(
        vis_segments.reshape(1, VIS_ROWS),
        txt_segments.reshape(1, TXT_ROWS),
        *[qkv_vis] * 3,
        *[qkv_txt] * 3,
    )


def second_clip(cut_ref, source, row):
    cuts = jnp.sum(cut_ref[...].astype(jnp.float32), axis=0)
    vis_cut, txt_cut = cuts[0:1, 0:1], cuts[CUT_ROWS // 2 : CUT_ROWS // 2 + 1, 0:1]
    vis_place = (source * VIS_ROWS + row).astype(jnp.float32)
    txt_place = (source * TXT_ROWS + row - VIS_ROWS).astype(jnp.float32)
    is_second = jnp.where(row < VIS_ROWS, vis_place - vis_cut, txt_place - txt_cut) >= 0.0
    return jnp.where(is_second, 1.0, 0.0)


def clip_columns(second, first_value, second_value):
    lane = lax.broadcasted_iota(jnp.int32, second.shape, 1)
    feature = jnp.where(lane == 0, first_value(second), second_value(second))
    return jnp.where(lane < 2, feature, 0.0).astype(jnp.bfloat16)


def attend(queries, k_wide, v_turned, write):
    factor = HEAD_DIM**-0.5 * LOG2E

    def score(block):
        return lax.dot_general(
            k_wide[...], queries(block), (((1,), (1,)), ((), ())), preferred_element_type=jnp.float32
        )

    blocks = STEP_ROWS // Q_ROWS
    scores = score(0)
    for block in range(blocks):
        upcoming = score(block + 1) if block + 1 < blocks else None
        highest = jnp.max(scores, axis=0, keepdims=True)
        exponent = jnp.exp2((scores - highest) * factor)
        total = jnp.sum(exponent, axis=0, keepdims=True)
        blended = jnp.dot(
            v_turned[...], exponent.astype(jnp.bfloat16), preferred_element_type=jnp.float32
        )
        result = jnp.swapaxes(blended * (1.0 / total), 0, 1).astype(jnp.bfloat16)
        write(block, result, highest * HEAD_DIM**-0.5 + jnp.log2(total) * LN2)
        scores = upcoming


def place_of(shape, rows, first_source, offset):
    index = lax.broadcasted_iota(jnp.int32, shape, 0)
    return first_source + index // rows, index % rows + offset


def key_features(cut, keys, rows, offset):
    second = second_clip(cut, *place_of((keys, HEAD_DIM), rows, 0, offset))
    return clip_columns(second, lambda s: BIG * s, lambda s: BIG * (1.0 - s))


def query_features(cut, count, rows, first_source, offset):
    second = second_clip(cut, *place_of((count, HEAD_DIM), rows, first_source, offset))
    return clip_columns(second, lambda s: 1.0 - s, lambda s: s)


def whole_kernel(cut, q, k, v, out, lse, k_wide, v_turned, q_wide):
    step = pl.program_id(0)
    keys = N_SEQ * ROWS
    sources = STEP_ROWS // ROWS

    @pl.when(step == 0)
    def _():
        k_wide[:, :HEAD_DIM] = k[...].reshape(keys, HEAD_DIM)
        k_wide[:, HEAD_DIM:] = key_features(cut, keys, ROWS, 0)
        v_turned[...] = jnp.swapaxes(v[...].reshape(keys, HEAD_DIM), 0, 1)

    q_wide[:, :HEAD_DIM] = q[...].reshape(STEP_ROWS, HEAD_DIM)
    q_wide[:, HEAD_DIM:] = query_features(cut, STEP_ROWS, ROWS, step * sources, 0)

    def write(block, result, log_total):
        count = Q_ROWS // ROWS
        out[block * count : (block + 1) * count] = result.reshape(count, ROWS, HEAD_DIM)
        for row in range(count):
            lse[block * count + row : block * count + row + 1, :] = log_total[
                :, row * HEAD_DIM : (row + 1) * HEAD_DIM
            ]

    attend(lambda block: q_wide[block * Q_ROWS : (block + 1) * Q_ROWS, :], k_wide, v_turned, write)


def shared_kernel(where, cut, q, own_kv, far_kv, whole, whole_lse, out, k_wide, v_turned, q_wide):
    core = where[2]
    keys = N_SEQ * HALF
    for place, (kv, offset) in enumerate(((own_kv, HALF * core), (far_kv, HALF * (1 - core)))):
        at = slice(place * keys, (place + 1) * keys)
        k_wide[at, :HEAD_DIM] = kv[:, :HALF].reshape(keys, HEAD_DIM)
        k_wide[at, HEAD_DIM:] = key_features(cut, keys, HALF, offset)
        v_turned[:, at] = jnp.swapaxes(kv[:, HALF:].reshape(keys, HEAD_DIM), 0, 1)
    q_wide[:, :HEAD_DIM] = q[...].reshape(STEP_ROWS, HEAD_DIM)
    q_wide[:, HEAD_DIM:] = query_features(cut, STEP_ROWS, HALF, 0, HALF * core)
    log_totals = []

    def write(block, result, log_total):
        count = Q_ROWS // HALF
        out[block * count : (block + 1) * count, ROWS:RET_ROWS, :] = result.reshape(count, HALF, HEAD_DIM)
        for row in range(Q_ROWS // HEAD_DIM):
            log_totals.append(log_total[:, row * HEAD_DIM : (row + 1) * HEAD_DIM])

    attend(lambda block: q_wide[block * Q_ROWS : (block + 1) * Q_ROWS, :], k_wide, v_turned, write)
    out[:, :ROWS, :] = whole[...]
    log_totals.append(jnp.zeros((RETURN - SHARED_LSE - len(log_totals), HEAD_DIM), jnp.float32))
    rows = jnp.concatenate([whole_lse[...], *log_totals], axis=0).astype(jnp.bfloat16)
    for device in range(N_SEQ):
        out[device, WHOLE_LSE:, :] = rows


Q_ROWS = 512
STEP_ROWS = 1024
VMEM = 32 * 2**20
PLACE_VMEM = 8 * 2**20
PROJECT_VMEM = 50 * 2**20


def attention_scratch():
    keys = N_SEQ * ROWS
    return [
        pltpu.VMEM((keys, 2 * HEAD_DIM), jnp.bfloat16),
        pltpu.VMEM((HEAD_DIM, keys), jnp.bfloat16),
        pltpu.VMEM((STEP_ROWS, 2 * HEAD_DIM), jnp.bfloat16),
    ]


def attention_cost(queries, keys):
    return pl.CostEstimate(
        flops=queries * keys * HEAD_DIM // 4,
        bytes_accessed=4 * keys * HEAD_DIM * 2,
        transcendentals=0,
    )


def attend_whole(received):
    keys = N_SEQ * ROWS
    steps = keys // STEP_ROWS
    sources = STEP_ROWS // ROWS
    return pl.pallas_call(
        whole_kernel,
        grid=(steps,),
        in_specs=[
            pl.BlockSpec((N_SEQ, CUT_ROWS, HEAD_DIM), lambda i: (0, SEND_ROWS // CUT_ROWS, 0)),
            pl.BlockSpec((sources, ROWS, HEAD_DIM), lambda i: (i, 0, 0)),
            pl.BlockSpec((N_SEQ, ROWS, HEAD_DIM), lambda i: (0, 1, 0)),
            pl.BlockSpec((N_SEQ, ROWS, HEAD_DIM), lambda i: (0, 2, 0)),
        ],
        out_specs=[
            pl.BlockSpec((sources, ROWS, HEAD_DIM), lambda i: (i, 0, 0)),
            pl.BlockSpec((sources, ROWS), lambda i: (i, 0)),
        ],
        out_shape=[
            jax.ShapeDtypeStruct((N_SEQ, ROWS, HEAD_DIM), jnp.bfloat16),
            jax.ShapeDtypeStruct((N_SEQ, ROWS), jnp.float32),
        ],
        scratch_shapes=attention_scratch(),
        compiler_params=pltpu.CompilerParams(vmem_limit_bytes=VMEM),
        cost_estimate=attention_cost(keys, keys),
        name="attend_whole",
    )(*[received] * 4)


def attend_shared(where, received, own_kv, far_kv, whole, whole_lse):
    keys = N_SEQ * ROWS
    full = lambda *shape: pl.BlockSpec(shape, lambda i, c: (0,) * len(shape))
    return pl.pallas_call(
        shared_kernel,
        grid_spec=pltpu.PrefetchScalarGridSpec(
            num_scalar_prefetch=1,
            grid=(1,),
            in_specs=[
                pl.BlockSpec((N_SEQ, CUT_ROWS, HEAD_DIM), lambda i, c: (0, SEND_ROWS // CUT_ROWS, 0)),
                pl.BlockSpec((N_SEQ, HALF, HEAD_DIM), lambda i, c: (0, A_ROWS // HALF, 0)),
                full(N_SEQ, 2 * HALF, HEAD_DIM),
                full(N_SEQ, 2 * HALF, HEAD_DIM),
                full(N_SEQ, ROWS, HEAD_DIM),
                full(N_SEQ, ROWS),
            ],
            out_specs=full(N_SEQ, RETURN, HEAD_DIM),
            scratch_shapes=attention_scratch(),
        ),
        out_shape=jax.ShapeDtypeStruct((N_SEQ, RETURN, HEAD_DIM), jnp.bfloat16),
        compiler_params=pltpu.CompilerParams(vmem_limit_bytes=VMEM),
        cost_estimate=attention_cost(keys // 2, keys),
        name="attend_shared",
    )(where, received, received, own_kv, far_kv, whole, whole_lse)


def place_kernel(where, mine, near, near_far, part, part_far, out):
    x, core = where[1], where[2]
    sign = 1 - 2 * core
    out[x] = mine[...]
    out[(x - sign + 4) % 4] = near[...]
    out[(x + sign + 4) % 4] = near_far[...]

    @pl.when(core == 0)
    def _():
        out[(x + 2) % 4] = part[...]

    @pl.when(core == 1)
    def _():
        out[(x + 2) % 4] = part_far[...]


def place(where, mine, near, near_far, part, part_far):
    rows, columns = mine.shape
    return pl.pallas_call(
        place_kernel,
        grid_spec=pltpu.PrefetchScalarGridSpec(
            num_scalar_prefetch=1,
            grid=(),
            in_specs=[pl.BlockSpec(memory_space=pltpu.VMEM)] * 5,
            out_specs=pl.BlockSpec(memory_space=pltpu.VMEM),
        ),
        out_shape=jax.ShapeDtypeStruct((4, rows, columns), jnp.bfloat16),
        compiler_params=pltpu.CompilerParams(vmem_limit_bytes=PLACE_VMEM),
        name="place",
    )(where, mine, near, near_far, part, part_far)


def slot_of(ret, head):
    chip, member = head // 3, head % 3
    low, high = ret.at[2 * chip], ret.at[2 * chip + 1]
    lane = lax.broadcasted_iota(jnp.int32, (1, HEAD_DIM), 1)
    rows = []
    for source in range(N_SEQ):
        whole = [ref[WHOLE_LSE : WHOLE_LSE + N_SEQ, :].astype(jnp.float32) for ref in (low, high)]
        shared = [ref[SHARED_LSE : SHARED_LSE + N_SEQ, :].astype(jnp.float32) for ref in (low, high)]
        left, right = (item[source // 2 : source // 2 + 1] for item in shared)
        if source % 2 == 0:
            right = pltpu.roll(right, HALF, 1)
        else:
            left = pltpu.roll(left, HALF, 1)
        both = jnp.where(lane < HALF, left, right)
        first, last = (item[source : source + 1] for item in whole)
        rows.append(jnp.where(member == 0, first, jnp.where(member == 1, both, last)))
    return rows


def project_kernel(where, ret, *refs):
    weights, (vis_out, txt_out, slots, held, sems) = refs[:9], refs[9:]
    y, core = where[0], where[2]
    sign = 1 - 2 * core
    columns = held.shape[2] // 2
    copies = []
    for index in range(7):
        to = held.at[index // 2, pl.ds(index % 2 * TRIO, TRIO)]
        copies.append(pltpu.make_async_copy(weights[index], to, sems.at[index]))
    for index in range(2):
        at = core if index == 0 else 1 - core
        start = pl.multiple_of(at * columns, columns)
        to = held.at[3, pl.ds(TRIO, TRIO), pl.ds(start, columns)]
        copies.append(pltpu.make_async_copy(weights[7 + index], to, sems.at[7 + index]))
    for copy in copies:
        copy.start()
    for slot in range(SLOTS):
        valid = where[5 + slot] > 0
        for source, row in enumerate(slot_of(ret, where[3 + slot])):
            row = jnp.where(valid, row, 0.0)
            at = source * VIS_ROWS
            slots[slot : slot + 1, at : at + VIS_ROWS] = row[:, :VIS_ROWS]
            at = VIS_SEQ + source * TXT_ROWS
            slots[slot : slot + 1, at : at + TXT_ROWS] = row[:, VIS_ROWS:]
    total = jnp.zeros((ROWS, 2 * columns), jnp.float32)
    pieces = []
    for index, hops in enumerate((0, 1, 2, 3, -1, -2, -3, 4)):
        chip = (y - hops * sign + 8) % 8
        low, high = ret[2 * chip], ret[2 * chip + 1]
        shared = jnp.concatenate([low[ROWS:RET_ROWS], high[ROWS:RET_ROWS]], axis=0)
        attention = jnp.concatenate([low[:ROWS], shared, high[:ROWS]], axis=1)
        txt_out[:, pl.ds(pl.multiple_of(chip * TRIO, TRIO), TRIO)] = attention[VIS_ROWS:]
        pieces.append(attention)
        copies[index].wait()
        if index % 2 == 1:
            if index == 7:
                copies[8].wait()
            both = jnp.concatenate(pieces[-2:], axis=1)
            total += jnp.dot(both, held[index // 2], preferred_element_type=jnp.float32)
    vis_out[...] = total[:VIS_ROWS].astype(jnp.bfloat16)


def project(where, returned, chunks, far_chunks):
    columns = chunks[0].shape[1]
    return pl.pallas_call(
        project_kernel,
        grid_spec=pltpu.PrefetchScalarGridSpec(
            num_scalar_prefetch=1,
            grid=(),
            in_specs=[pl.BlockSpec(memory_space=pltpu.VMEM)] + [pl.BlockSpec(memory_space=pltpu.HBM)] * 9,
            out_specs=[pl.BlockSpec(memory_space=pltpu.VMEM)] * 3,
            scratch_shapes=[
                pltpu.VMEM((4, 2 * TRIO, columns), jnp.bfloat16),
                pltpu.SemaphoreType.DMA((9,)),
            ],
        ),
        out_shape=[
            jax.ShapeDtypeStruct((VIS_ROWS, columns), jnp.bfloat16),
            jax.ShapeDtypeStruct((TXT_ROWS, HEADS * HEAD_DIM), jnp.bfloat16),
            jax.ShapeDtypeStruct((SLOTS, VIS_SEQ + TXT_SEQ), jnp.float32),
        ],
        compiler_params=pltpu.CompilerParams(vmem_limit_bytes=PROJECT_VMEM),
        name="project",
    )(where, returned, *chunks[:4], *far_chunks[:3], chunks[4], far_chunks[3])


AXES = ("dp", "seq")
X_SIZE = 4
Y_SIZE = 8


def permute(operand, target, cores=(0, 1)):
    pairs = []
    for y in range(Y_SIZE):
        for x in range(X_SIZE):
            for s in range(N_SEQ):
                ty, tx, ts = target(y, x, s)
                there = (ty % Y_SIZE) * X_SIZE + tx % X_SIZE
                if s % 2 in cores:
                    pairs.append(((y * X_SIZE + x) * N_SEQ + s, there * N_SEQ + ts))
    return lax.ppermute(operand, AXES, pairs)


def swap(operand, cores=(0, 1)):
    return permute(operand, lambda y, x, s: (y, x, s ^ 1), cores)


def shift_x(operand, hops, cores=(0, 1)):
    return permute(operand, lambda y, x, s: (y, x + hops * (1 - 2 * (s % 2)), s), cores)


def shift_y(operand):
    return permute(operand, lambda y, x, s: (y + 1 - 2 * (s % 2), x, s))


def heads_of_slots(head_map, seq_index):
    mine = (head_map == seq_index).astype(jnp.int32)
    rank = jnp.cumsum(mine) - 1
    ids = jnp.arange(HEADS, dtype=jnp.int32)
    picked = mine[None] * (rank[None] == jnp.arange(SLOTS, dtype=jnp.int32)[:, None])
    return jnp.concatenate([jnp.sum(picked * ids[None], axis=1), jnp.sum(picked, axis=1)])


def on_device(qkv_vis, qkv_txt, vis_segments, txt_segments, head_map, w_out):
    seq_index = lax.axis_index("seq")
    dp_index = lax.axis_index("dp")
    core = seq_index % 2
    half = w_out.shape[1] // 2
    place_here = jnp.stack([dp_index // X_SIZE, dp_index % X_SIZE, core]).astype(jnp.int32)
    where = jnp.concatenate([place_here, heads_of_slots(head_map, seq_index)])

    near = shift_x(w_out, 1)
    part = shift_x(w_out, 2, cores=(0,))
    sending = pack(qkv_vis, qkv_txt, vis_segments, txt_segments)
    received = lax.all_to_all(sending, "seq", split_axis=0, concat_axis=0, tiled=True)
    chunks = [place(where, w_out, near, swap(near), part, swap(part, cores=(0,))).reshape(-1, 2 * half)]
    chunks.append(shift_y(chunks[0]))
    chunks.append(shift_y(chunks[1]))
    chunks.append(shift_y(chunks[2]))
    own_kv = received[:, A_ROWS + HALF : SEND_ROWS]
    far_kv = swap(own_kv)
    whole, whole_lse = attend_whole(received)
    returning = attend_shared(where, received, own_kv, far_kv, whole, whole_lse)
    returning, chunks[1], chunks[2], chunks[3] = lax.optimization_barrier((returning, *chunks[1:]))
    returned = lax.all_to_all(returning, "seq", split_axis=0, concat_axis=0, tiled=True)
    chunks.append(shift_y(lax.dynamic_slice_in_dim(chunks[3], core * half, half, 1)))
    far_chunks = [swap(chunk) for chunk in chunks[1:]]
    vis_out, txt_out, lse_slots = project(where, returned, chunks, far_chunks)
    return vis_out, txt_out, lse_slots


def solution(mesh):
    in_specs = (
        P(("dp", "seq"), None),
        P(("dp", "seq"), None),
        P(("dp", "seq")),
        P(("dp", "seq")),
        P(),
        P("dp", None),
    )
    out_specs = (P(("dp", "seq"), None), P(("dp", "seq"), None), P("seq", "dp"))
    return jax.shard_map(
        on_device, mesh=mesh, in_specs=in_specs, out_specs=out_specs, check_vma=False
    )
```

```python
import functools

import jax
import jax.numpy as jnp
from jax import lax
from jax.experimental import pallas as pl
from jax.experimental.pallas import tpu as pltpu
from jax.sharding import PartitionSpec as P

HEADS = 24
HEAD_DIM = 128
N_SEQ = 16
VIS_ROWS = 112
TXT_ROWS = 16
ROWS = VIS_ROWS + TXT_ROWS
HALF = ROWS // 2
TRIO = 3 * HEAD_DIM
CHIPS = 8
A_ROWS = 3 * ROWS
SEND_ROWS = A_ROWS + 3 * HALF
CUT_ROWS = 16
PAYLOAD = SEND_ROWS + CUT_ROWS
RET_ROWS = ROWS + HALF
WHOLE_LSE = RET_ROWS
SHARED_LSE = WHOLE_LSE + N_SEQ
RETURN = SHARED_LSE + N_SEQ
PACK_CHIPS = 4
VIS_SEQ = VIS_ROWS * N_SEQ
TXT_SEQ = TXT_ROWS * N_SEQ
SLOTS = 2
LOG2E = 1.4426950408889634
LN2 = 0.6931471805599453
BIG = -1e30


def pack_kernel(seg_vis, seg_txt, vq, vk, vv, tq, tk, tv, out):
    def even(ref):
        parity = (ref[...] & 1).astype(jnp.float32)
        count = jnp.sum(1.0 - parity, axis=1, keepdims=True)
        return jnp.broadcast_to(count, (CUT_ROWS // 2, HEAD_DIM))

    cuts = jnp.concatenate([even(seg_vis), even(seg_txt)], axis=0).astype(jnp.bfloat16)
    for chip in range(PACK_CHIPS):
        low, high = 2 * chip, 2 * chip + 1
        for part, (vis, txt) in enumerate(((vq, tq), (vk, tk), (vv, tv))):
            row = part * ROWS
            for device, column in ((low, chip * TRIO), (high, chip * TRIO + 2 * HEAD_DIM)):
                columns = slice(column, column + HEAD_DIM)
                out[device, row : row + VIS_ROWS, :] = vis[:, columns]
                out[device, row + VIS_ROWS : row + ROWS, :] = txt[:, columns]
            row = A_ROWS + part * HALF
            columns = slice(chip * TRIO + HEAD_DIM, chip * TRIO + 2 * HEAD_DIM)
            out[low, row : row + HALF, :] = vis[:HALF, columns]
            out[high, row : row + VIS_ROWS - HALF, :] = vis[HALF:, columns]
            out[high, row + VIS_ROWS - HALF : row + HALF, :] = txt[:, columns]
        out[low, SEND_ROWS:PAYLOAD, :] = cuts
        out[high, SEND_ROWS:PAYLOAD, :] = cuts


def pack(qkv_vis, qkv_txt, vis_segments, txt_segments):
    steps = CHIPS // PACK_CHIPS

    def spec(rows, part):
        return pl.BlockSpec((rows, PACK_CHIPS * TRIO), lambda i: (0, part * steps + i))

    return pl.pallas_call(
        pack_kernel,
        grid=(steps,),
        in_specs=[
            pl.BlockSpec((1, VIS_ROWS), lambda i: (0, 0)),
            pl.BlockSpec((1, TXT_ROWS), lambda i: (0, 0)),
            *[spec(VIS_ROWS, part) for part in range(3)],
            *[spec(TXT_ROWS, part) for part in range(3)],
        ],
        out_specs=pl.BlockSpec((2 * PACK_CHIPS, PAYLOAD, HEAD_DIM), lambda i: (i, 0, 0)),
        out_shape=jax.ShapeDtypeStruct((N_SEQ, PAYLOAD, HEAD_DIM), jnp.bfloat16),
        name="pack",
    )(
        vis_segments.reshape(1, VIS_ROWS),
        txt_segments.reshape(1, TXT_ROWS),
        *[qkv_vis] * 3,
        *[qkv_txt] * 3,
    )


def second_clip(cut_ref, source, row):
    cuts = jnp.sum(cut_ref[...].astype(jnp.float32), axis=0)
    vis_cut, txt_cut = cuts[0:1, 0:1], cuts[CUT_ROWS // 2 : CUT_ROWS // 2 + 1, 0:1]
    vis_place = (source * VIS_ROWS + row).astype(jnp.float32)
    txt_place = (source * TXT_ROWS + row - VIS_ROWS).astype(jnp.float32)
    is_second = jnp.where(row < VIS_ROWS, vis_place - vis_cut, txt_place - txt_cut) >= 0.0
    return jnp.where(is_second, 1.0, 0.0)


def clip_columns(second, first_value, second_value):
    lane = lax.broadcasted_iota(jnp.int32, second.shape, 1)
    feature = jnp.where(lane == 0, first_value(second), second_value(second))
    return jnp.where(lane < 2, feature, 0.0).astype(jnp.bfloat16)


def attend(queries, k_wide, v_turned, write):
    factor = HEAD_DIM**-0.5 * LOG2E

    def score(block):
        return lax.dot_general(
            k_wide[...], queries(block), (((1,), (1,)), ((), ())), preferred_element_type=jnp.float32
        )

    blocks = STEP_ROWS // Q_ROWS
    scores = score(0)
    for block in range(blocks):
        upcoming = score(block + 1) if block + 1 < blocks else None
        highest = jnp.max(scores, axis=0, keepdims=True)
        exponent = jnp.exp2((scores - highest) * factor)
        total = jnp.sum(exponent, axis=0, keepdims=True)
        blended = jnp.dot(
            v_turned[...], exponent.astype(jnp.bfloat16), preferred_element_type=jnp.float32
        )
        result = jnp.swapaxes(blended * (1.0 / total), 0, 1).astype(jnp.bfloat16)
        write(block, result, highest * HEAD_DIM**-0.5 + jnp.log2(total) * LN2)
        scores = upcoming


def place_of(shape, rows, first_source, offset):
    index = lax.broadcasted_iota(jnp.int32, shape, 0)
    return first_source + index // rows, index % rows + offset


def key_features(cut, keys, rows, offset):
    second = second_clip(cut, *place_of((keys, HEAD_DIM), rows, 0, offset))
    return clip_columns(second, lambda s: BIG * s, lambda s: BIG * (1.0 - s))


def query_features(cut, count, rows, first_source, offset):
    second = second_clip(cut, *place_of((count, HEAD_DIM), rows, first_source, offset))
    return clip_columns(second, lambda s: 1.0 - s, lambda s: s)


def whole_kernel(cut, q, k, v, out, lse, k_wide, v_turned, q_wide):
    step = pl.program_id(0)
    keys = N_SEQ * ROWS
    sources = STEP_ROWS // ROWS

    @pl.when(step == 0)
    def _():
        k_wide[:, :HEAD_DIM] = k[...].reshape(keys, HEAD_DIM)
        k_wide[:, HEAD_DIM:] = key_features(cut, keys, ROWS, 0)
        v_turned[...] = jnp.swapaxes(v[...].reshape(keys, HEAD_DIM), 0, 1)

    q_wide[:, :HEAD_DIM] = q[...].reshape(STEP_ROWS, HEAD_DIM)
    q_wide[:, HEAD_DIM:] = query_features(cut, STEP_ROWS, ROWS, step * sources, 0)

    def write(block, result, log_total):
        count = Q_ROWS // ROWS
        out[block * count : (block + 1) * count] = result.reshape(count, ROWS, HEAD_DIM)
        for row in range(count):
            lse[block * count + row : block * count + row + 1, :] = log_total[
                :, row * HEAD_DIM : (row + 1) * HEAD_DIM
            ]

    attend(lambda block: q_wide[block * Q_ROWS : (block + 1) * Q_ROWS, :], k_wide, v_turned, write)


def shared_kernel(where, cut, q, own_kv, far_kv, whole, whole_lse, out, k_wide, v_turned, q_wide):
    core = where[2]
    keys = N_SEQ * HALF
    for place, (kv, offset) in enumerate(((own_kv, HALF * core), (far_kv, HALF * (1 - core)))):
        at = slice(place * keys, (place + 1) * keys)
        k_wide[at, :HEAD_DIM] = kv[:, :HALF].reshape(keys, HEAD_DIM)
        k_wide[at, HEAD_DIM:] = key_features(cut, keys, HALF, offset)
        v_turned[:, at] = jnp.swapaxes(kv[:, HALF:].reshape(keys, HEAD_DIM), 0, 1)
    q_wide[:, :HEAD_DIM] = q[...].reshape(STEP_ROWS, HEAD_DIM)
    q_wide[:, HEAD_DIM:] = query_features(cut, STEP_ROWS, HALF, 0, HALF * core)
    log_totals = []

    def write(block, result, log_total):
        count = Q_ROWS // HALF
        out[block * count : (block + 1) * count, ROWS:RET_ROWS, :] = result.reshape(count, HALF, HEAD_DIM)
        for row in range(Q_ROWS // HEAD_DIM):
            log_totals.append(log_total[:, row * HEAD_DIM : (row + 1) * HEAD_DIM])

    attend(lambda block: q_wide[block * Q_ROWS : (block + 1) * Q_ROWS, :], k_wide, v_turned, write)
    out[:, :ROWS, :] = whole[...]
    log_totals.append(jnp.zeros((RETURN - SHARED_LSE - len(log_totals), HEAD_DIM), jnp.float32))
    rows = jnp.concatenate([whole_lse[...], *log_totals], axis=0).astype(jnp.bfloat16)
    for device in range(N_SEQ):
        out[device, WHOLE_LSE:, :] = rows


Q_ROWS = 512
STEP_ROWS = 1024
VMEM = 32 * 2**20
PLACE_VMEM = 12 * 2**20
PROJECT_VMEM = 50 * 2**20


def attention_scratch():
    keys = N_SEQ * ROWS
    return [
        pltpu.VMEM((keys, 2 * HEAD_DIM), jnp.bfloat16),
        pltpu.VMEM((HEAD_DIM, keys), jnp.bfloat16),
        pltpu.VMEM((STEP_ROWS, 2 * HEAD_DIM), jnp.bfloat16),
    ]


def attention_cost(queries, keys):
    return pl.CostEstimate(
        flops=queries * keys * HEAD_DIM // 4,
        bytes_accessed=4 * keys * HEAD_DIM * 2,
        transcendentals=0,
    )


def attend_whole(received):
    keys = N_SEQ * ROWS
    steps = keys // STEP_ROWS
    sources = STEP_ROWS // ROWS
    return pl.pallas_call(
        whole_kernel,
        grid=(steps,),
        in_specs=[
            pl.BlockSpec((N_SEQ, CUT_ROWS, HEAD_DIM), lambda i: (0, SEND_ROWS // CUT_ROWS, 0)),
            pl.BlockSpec((sources, ROWS, HEAD_DIM), lambda i: (i, 0, 0)),
            pl.BlockSpec((N_SEQ, ROWS, HEAD_DIM), lambda i: (0, 1, 0)),
            pl.BlockSpec((N_SEQ, ROWS, HEAD_DIM), lambda i: (0, 2, 0)),
        ],
        out_specs=[
            pl.BlockSpec((sources, ROWS, HEAD_DIM), lambda i: (i, 0, 0)),
            pl.BlockSpec((sources, ROWS), lambda i: (i, 0)),
        ],
        out_shape=[
            jax.ShapeDtypeStruct((N_SEQ, ROWS, HEAD_DIM), jnp.bfloat16),
            jax.ShapeDtypeStruct((N_SEQ, ROWS), jnp.float32),
        ],
        scratch_shapes=attention_scratch(),
        compiler_params=pltpu.CompilerParams(vmem_limit_bytes=VMEM),
        cost_estimate=attention_cost(keys, keys),
        name="attend_whole",
    )(*[received] * 4)


def attend_shared(where, received, own_kv, far_kv, whole, whole_lse):
    keys = N_SEQ * ROWS
    full = lambda *shape: pl.BlockSpec(shape, lambda i, c: (0,) * len(shape))
    return pl.pallas_call(
        shared_kernel,
        grid_spec=pltpu.PrefetchScalarGridSpec(
            num_scalar_prefetch=1,
            grid=(1,),
            in_specs=[
                pl.BlockSpec((N_SEQ, CUT_ROWS, HEAD_DIM), lambda i, c: (0, SEND_ROWS // CUT_ROWS, 0)),
                pl.BlockSpec((N_SEQ, HALF, HEAD_DIM), lambda i, c: (0, A_ROWS // HALF, 0)),
                full(N_SEQ, 2 * HALF, HEAD_DIM),
                full(N_SEQ, 2 * HALF, HEAD_DIM),
                full(N_SEQ, ROWS, HEAD_DIM),
                full(N_SEQ, ROWS),
            ],
            out_specs=full(N_SEQ, RETURN, HEAD_DIM),
            scratch_shapes=attention_scratch(),
        ),
        out_shape=jax.ShapeDtypeStruct((N_SEQ, RETURN, HEAD_DIM), jnp.bfloat16),
        compiler_params=pltpu.CompilerParams(vmem_limit_bytes=VMEM),
        cost_estimate=attention_cost(keys // 2, keys),
        name="attend_shared",
    )(where, received, received, own_kv, far_kv, whole, whole_lse)


def place_kernel(where, mine, *refs):
    ring, far_ring, opposite, opposite_far, halves = refs[:3], refs[3:6], refs[6], refs[7], refs[8:]
    y, core = where[0], where[2]
    sign = 1 - 2 * core

    def put(to, shard):
        to = (to + Y_SIZE) % Y_SIZE
        for half, out in enumerate(halves):

            @pl.when(to // Y_HALF == half)
            def _():
                out[to % Y_HALF] = shard[...]

    put(y, mine)
    for index in range(3):
        hops = (index + 1) * sign
        put(y - hops, ring[index])
        put(y + hops, far_ring[index])

    @pl.when(core == 0)
    def _():
        put(y + 4, opposite)

    @pl.when(core == 1)
    def _():
        put(y + 4, opposite_far)


def place(where, shards):
    rows, columns = shards[0].shape
    return pl.pallas_call(
        place_kernel,
        grid_spec=pltpu.PrefetchScalarGridSpec(
            num_scalar_prefetch=1,
            grid=(),
            in_specs=[pl.BlockSpec(memory_space=pltpu.VMEM)] * len(shards),
            out_specs=[pl.BlockSpec(memory_space=pltpu.VMEM)] * 2,
        ),
        out_shape=[jax.ShapeDtypeStruct((Y_HALF, rows, columns), jnp.bfloat16)] * 2,
        compiler_params=pltpu.CompilerParams(vmem_limit_bytes=PLACE_VMEM),
        name="place",
    )(where, *shards)


def slot_of(ret, head):
    chip, member = head // 3, head % 3
    low, high = ret.at[2 * chip], ret.at[2 * chip + 1]
    lane = lax.broadcasted_iota(jnp.int32, (1, HEAD_DIM), 1)
    rows = []
    for source in range(N_SEQ):
        whole = [ref[WHOLE_LSE : WHOLE_LSE + N_SEQ, :].astype(jnp.float32) for ref in (low, high)]
        shared = [ref[SHARED_LSE : SHARED_LSE + N_SEQ, :].astype(jnp.float32) for ref in (low, high)]
        left, right = (item[source // 2 : source // 2 + 1] for item in shared)
        if source % 2 == 0:
            right = pltpu.roll(right, HALF, 1)
        else:
            left = pltpu.roll(left, HALF, 1)
        both = jnp.where(lane < HALF, left, right)
        first, last = (item[source : source + 1] for item in whole)
        rows.append(jnp.where(member == 0, first, jnp.where(member == 1, both, last)))
    return rows


def project_kernel(where, ret, *refs):
    weights, (vis_out, txt_out, slots, held, sems) = refs[:10], refs[10:]
    x, core = where[1], where[2]
    sign = 1 - 2 * core
    shard = weights[0].shape[1]

    def copies_of(index, to_x, first_y, count):
        column = (to_x + X_SIZE) % X_SIZE
        pieces = []
        for item in range(count):
            start = ((first_y + item) * X_SIZE + column) * shard
            to = held.at[pl.ds(pl.multiple_of(start, 32), shard)]
            pieces.append(pltpu.make_async_copy(weights[index].at[item], to, sems.at[index, item]))
        return pieces

    rounds = [[], []]
    for pair, to_x in enumerate((x, x - sign, x + sign)):
        for half in range(2):
            pieces = copies_of(2 * pair + half, to_x, half * Y_HALF, Y_HALF)
            for item in range(Y_HALF):
                rounds[item // 2].append(pieces[item])
    for pair, half in enumerate((core, 1 - core)):
        for item in range(2):
            rounds[item] += copies_of(6 + 2 * pair + item, x + 2, half * Y_HALF + 2 * item, 2)
    for copy in rounds[0] + rounds[1]:
        copy.start()
    for slot in range(SLOTS):
        valid = where[5 + slot] > 0
        for source, row in enumerate(slot_of(ret, where[3 + slot])):
            row = jnp.where(valid, row, 0.0)
            at = source * VIS_ROWS
            slots[slot : slot + 1, at : at + VIS_ROWS] = row[:, :VIS_ROWS]
            at = VIS_SEQ + source * TXT_ROWS
            slots[slot : slot + 1, at : at + TXT_ROWS] = row[:, VIS_ROWS:]
    total = jnp.zeros((ROWS, held.shape[1]), jnp.float32)
    depth = 2 * TRIO
    for item in range(2):
        for copy in rounds[item]:
            copy.wait()
        for first in (2 * item, 2 * item + Y_HALF):
            pieces = []
            for chip in (first, first + 1):
                low, high = ret[2 * chip], ret[2 * chip + 1]
                shared = jnp.concatenate([low[ROWS:RET_ROWS], high[ROWS:RET_ROWS]], axis=0)
                pieces += [low[:ROWS], shared, high[:ROWS]]
            attention = jnp.concatenate(pieces, axis=1)
            txt_out[:, first * TRIO : first * TRIO + depth] = attention[VIS_ROWS:]
            total += jnp.dot(
                attention, held[first * TRIO : first * TRIO + depth, :], preferred_element_type=jnp.float32
            )
    vis_out[...] = total[:VIS_ROWS].astype(jnp.bfloat16)


def project(where, returned, weights):
    columns = weights[0].shape[2]
    return pl.pallas_call(
        project_kernel,
        grid_spec=pltpu.PrefetchScalarGridSpec(
            num_scalar_prefetch=1,
            grid=(),
            in_specs=[pl.BlockSpec(memory_space=pltpu.VMEM)] + [pl.BlockSpec(memory_space=pl.ANY)] * 10,
            out_specs=[pl.BlockSpec(memory_space=pltpu.VMEM)] * 3,
            scratch_shapes=[
                pltpu.VMEM((HEADS * HEAD_DIM, columns), jnp.bfloat16),
                pltpu.SemaphoreType.DMA((10, Y_HALF)),
            ],
        ),
        out_shape=[
            jax.ShapeDtypeStruct((VIS_ROWS, columns), jnp.bfloat16),
            jax.ShapeDtypeStruct((TXT_ROWS, HEADS * HEAD_DIM), jnp.bfloat16),
            jax.ShapeDtypeStruct((SLOTS, VIS_SEQ + TXT_SEQ), jnp.float32),
        ],
        compiler_params=pltpu.CompilerParams(vmem_limit_bytes=PROJECT_VMEM),
        name="project",
    )(where, returned, *weights)


AXES = ("dp", "seq")
X_SIZE = 4
Y_SIZE = 8
Y_HALF = Y_SIZE // 2


def permute(operand, target, cores=(0, 1)):
    pairs = []
    for y in range(Y_SIZE):
        for x in range(X_SIZE):
            for s in range(N_SEQ):
                ty, tx, ts = target(y, x, s)
                there = (ty % Y_SIZE) * X_SIZE + tx % X_SIZE
                if s % 2 in cores:
                    pairs.append(((y * X_SIZE + x) * N_SEQ + s, there * N_SEQ + ts))
    return lax.ppermute(operand, AXES, pairs)


def swap(operand, cores=(0, 1)):
    return permute(operand, lambda y, x, s: (y, x, s ^ 1), cores)


def shift_x(operand):
    return permute(operand, lambda y, x, s: (y, x + 1 - 2 * (s % 2), s))


def shift_y(operand, hops=1, cores=(0, 1)):
    return permute(operand, lambda y, x, s: (y + hops * (1 - 2 * (s % 2)), x, s), cores)


def gather_along_y(where, w_out):
    ring = [shift_y(w_out)]
    opposite = shift_y(w_out, Y_SIZE // 2, cores=(0,))
    for _ in range(2):
        ring.append(shift_y(ring[-1]))
    far_ring = [swap(shard) for shard in ring]
    return place(where, [w_out, *ring, *far_ring, opposite, swap(opposite, cores=(0,))])


def heads_of_slots(head_map, seq_index):
    mine = (head_map == seq_index).astype(jnp.int32)
    rank = jnp.cumsum(mine) - 1
    ids = jnp.arange(HEADS, dtype=jnp.int32)
    picked = mine[None] * (rank[None] == jnp.arange(SLOTS, dtype=jnp.int32)[:, None])
    return jnp.concatenate([jnp.sum(picked * ids[None], axis=1), jnp.sum(picked, axis=1)])


def on_device(qkv_vis, qkv_txt, vis_segments, txt_segments, head_map, w_out):
    seq_index = lax.axis_index("seq")
    dp_index = lax.axis_index("dp")
    core = seq_index % 2
    place_here = jnp.stack([dp_index // X_SIZE, dp_index % X_SIZE, core]).astype(jnp.int32)
    where = jnp.concatenate([place_here, heads_of_slots(head_map, seq_index)])

    sending = pack(qkv_vis, qkv_txt, vis_segments, txt_segments)
    received = lax.all_to_all(sending, "seq", split_axis=0, concat_axis=0, tiled=True)
    own_x = gather_along_y(where, w_out)
    near = [shift_x(shards) for shards in own_x]
    own_kv = received[:, A_ROWS + HALF : SEND_ROWS]
    far_kv = swap(own_kv)
    whole, whole_lse = attend_whole(received)
    returning = attend_shared(where, received, own_kv, far_kv, whole, whole_lse)
    returning, near = lax.optimization_barrier((returning, near))
    returned = lax.all_to_all(returning, "seq", split_axis=0, concat_axis=0, tiled=True)
    opposite = [
        shift_x(jnp.where(core == 0, near[0][2 * part : 2 * part + 2], near[1][2 * part : 2 * part + 2]))
        for part in range(2)
    ]
    weights = [*own_x, *near, *map(swap, near), *opposite, *map(swap, opposite)]
    vis_out, txt_out, lse_slots = project(where, returned, weights)
    return vis_out, txt_out, lse_slots


def solution(mesh):
    in_specs = (
        P(("dp", "seq"), None),
        P(("dp", "seq"), None),
        P(("dp", "seq")),
        P(("dp", "seq")),
        P(),
        P("dp", None),
    )
    out_specs = (P(("dp", "seq"), None), P(("dp", "seq"), None), P("seq", "dp"))
    return jax.shard_map(
        on_device, mesh=mesh, in_specs=in_specs, out_specs=out_specs, check_vma=False
    )
```

```python
import functools

import jax
import jax.numpy as jnp
from jax import lax
from jax.experimental import pallas as pl
from jax.experimental.pallas import tpu as pltpu
from jax.sharding import PartitionSpec as P

HEADS = 24
HEAD_DIM = 128
N_SEQ = 16
VIS_ROWS = 112
TXT_ROWS = 16
ROWS = VIS_ROWS + TXT_ROWS
HALF = ROWS // 2
TRIO = 3 * HEAD_DIM
CHIPS = 8
A_ROWS = 3 * ROWS
SEND_ROWS = A_ROWS + 3 * HALF
CUT_ROWS = 16
PAYLOAD = SEND_ROWS + CUT_ROWS
RET_ROWS = ROWS + HALF
WHOLE_LSE = RET_ROWS
SHARED_LSE = WHOLE_LSE + N_SEQ
RETURN = SHARED_LSE + N_SEQ
PACK_CHIPS = 4
VIS_SEQ = VIS_ROWS * N_SEQ
TXT_SEQ = TXT_ROWS * N_SEQ
SLOTS = 2
LOG2E = 1.4426950408889634
LN2 = 0.6931471805599453
BIG = -1e30


def pack_kernel(seg_vis, seg_txt, vq, vk, vv, tq, tk, tv, out):
    def even(ref):
        parity = (ref[...] & 1).astype(jnp.float32)
        count = jnp.sum(1.0 - parity, axis=1, keepdims=True)
        return jnp.broadcast_to(count, (CUT_ROWS // 2, HEAD_DIM))

    cuts = jnp.concatenate([even(seg_vis), even(seg_txt)], axis=0).astype(jnp.bfloat16)
    for chip in range(PACK_CHIPS):
        low, high = 2 * chip, 2 * chip + 1
        for part, (vis, txt) in enumerate(((vq, tq), (vk, tk), (vv, tv))):
            row = part * ROWS
            for device, column in ((low, chip * TRIO), (high, chip * TRIO + 2 * HEAD_DIM)):
                columns = slice(column, column + HEAD_DIM)
                out[device, row : row + VIS_ROWS, :] = vis[:, columns]
                out[device, row + VIS_ROWS : row + ROWS, :] = txt[:, columns]
            row = A_ROWS + part * HALF
            columns = slice(chip * TRIO + HEAD_DIM, chip * TRIO + 2 * HEAD_DIM)
            out[low, row : row + HALF, :] = vis[:HALF, columns]
            out[high, row : row + VIS_ROWS - HALF, :] = vis[HALF:, columns]
            out[high, row + VIS_ROWS - HALF : row + HALF, :] = txt[:, columns]
        out[low, SEND_ROWS:PAYLOAD, :] = cuts
        out[high, SEND_ROWS:PAYLOAD, :] = cuts


def pack(qkv_vis, qkv_txt, vis_segments, txt_segments):
    steps = CHIPS // PACK_CHIPS

    def spec(rows, part):
        return pl.BlockSpec((rows, PACK_CHIPS * TRIO), lambda i: (0, part * steps + i))

    return pl.pallas_call(
        pack_kernel,
        grid=(steps,),
        in_specs=[
            pl.BlockSpec((1, VIS_ROWS), lambda i: (0, 0)),
            pl.BlockSpec((1, TXT_ROWS), lambda i: (0, 0)),
            *[spec(VIS_ROWS, part) for part in range(3)],
            *[spec(TXT_ROWS, part) for part in range(3)],
        ],
        out_specs=pl.BlockSpec((2 * PACK_CHIPS, PAYLOAD, HEAD_DIM), lambda i: (i, 0, 0)),
        out_shape=jax.ShapeDtypeStruct((N_SEQ, PAYLOAD, HEAD_DIM), jnp.bfloat16),
        name="pack",
    )(
        vis_segments.reshape(1, VIS_ROWS),
        txt_segments.reshape(1, TXT_ROWS),
        *[qkv_vis] * 3,
        *[qkv_txt] * 3,
    )


def second_clip(cut_ref, source, row):
    cuts = jnp.sum(cut_ref[...].astype(jnp.float32), axis=0)
    vis_cut, txt_cut = cuts[0:1, 0:1], cuts[CUT_ROWS // 2 : CUT_ROWS // 2 + 1, 0:1]
    vis_place = (source * VIS_ROWS + row).astype(jnp.float32)
    txt_place = (source * TXT_ROWS + row - VIS_ROWS).astype(jnp.float32)
    is_second = jnp.where(row < VIS_ROWS, vis_place - vis_cut, txt_place - txt_cut) >= 0.0
    return jnp.where(is_second, 1.0, 0.0)


def clip_columns(second, first_value, second_value):
    lane = lax.broadcasted_iota(jnp.int32, second.shape, 1)
    feature = jnp.where(lane == 0, first_value(second), second_value(second))
    return jnp.where(lane < 2, feature, 0.0).astype(jnp.bfloat16)


def attend(queries, k_wide, v_turned, write):
    factor = HEAD_DIM**-0.5 * LOG2E

    def score(block):
        return lax.dot_general(
            k_wide[...], queries(block), (((1,), (1,)), ((), ())), preferred_element_type=jnp.float32
        )

    blocks = STEP_ROWS // Q_ROWS
    scores = score(0)
    for block in range(blocks):
        upcoming = score(block + 1) if block + 1 < blocks else None
        highest = jnp.max(scores, axis=0, keepdims=True)
        exponent = jnp.exp2((scores - highest) * factor)
        total = jnp.sum(exponent, axis=0, keepdims=True)
        blended = jnp.dot(
            v_turned[...], exponent.astype(jnp.bfloat16), preferred_element_type=jnp.float32
        )
        result = jnp.swapaxes(blended * (1.0 / total), 0, 1).astype(jnp.bfloat16)
        write(block, result, highest * HEAD_DIM**-0.5 + jnp.log2(total) * LN2)
        scores = upcoming


def place_of(shape, rows, first_source, offset):
    index = lax.broadcasted_iota(jnp.int32, shape, 0)
    return first_source + index // rows, index % rows + offset


def key_features(cut, keys, rows, offset):
    second = second_clip(cut, *place_of((keys, HEAD_DIM), rows, 0, offset))
    return clip_columns(second, lambda s: BIG * s, lambda s: BIG * (1.0 - s))


def query_features(cut, count, rows, first_source, offset):
    second = second_clip(cut, *place_of((count, HEAD_DIM), rows, first_source, offset))
    return clip_columns(second, lambda s: 1.0 - s, lambda s: s)


def whole_kernel(cut, q, k, v, out, lse, k_wide, v_turned, q_wide):
    step = pl.program_id(0)
    keys = N_SEQ * ROWS
    sources = STEP_ROWS // ROWS

    @pl.when(step == 0)
    def _():
        k_wide[:, :HEAD_DIM] = k[...].reshape(keys, HEAD_DIM)
        k_wide[:, HEAD_DIM:] = key_features(cut, keys, ROWS, 0)
        v_turned[...] = jnp.swapaxes(v[...].reshape(keys, HEAD_DIM), 0, 1)

    q_wide[:, :HEAD_DIM] = q[...].reshape(STEP_ROWS, HEAD_DIM)
    q_wide[:, HEAD_DIM:] = query_features(cut, STEP_ROWS, ROWS, step * sources, 0)

    def write(block, result, log_total):
        count = Q_ROWS // ROWS
        out[block * count : (block + 1) * count] = result.reshape(count, ROWS, HEAD_DIM)
        for row in range(count):
            lse[block * count + row : block * count + row + 1, :] = log_total[
                :, row * HEAD_DIM : (row + 1) * HEAD_DIM
            ]

    attend(lambda block: q_wide[block * Q_ROWS : (block + 1) * Q_ROWS, :], k_wide, v_turned, write)


def shared_kernel(where, cut, q, own_kv, far_kv, whole, whole_lse, out, k_wide, v_turned, q_wide):
    core = where[2]
    keys = N_SEQ * HALF
    for place, (kv, offset) in enumerate(((own_kv, HALF * core), (far_kv, HALF * (1 - core)))):
        at = slice(place * keys, (place + 1) * keys)
        k_wide[at, :HEAD_DIM] = kv[:, :HALF].reshape(keys, HEAD_DIM)
        k_wide[at, HEAD_DIM:] = key_features(cut, keys, HALF, offset)
        v_turned[:, at] = jnp.swapaxes(kv[:, HALF:].reshape(keys, HEAD_DIM), 0, 1)
    q_wide[:, :HEAD_DIM] = q[...].reshape(STEP_ROWS, HEAD_DIM)
    q_wide[:, HEAD_DIM:] = query_features(cut, STEP_ROWS, HALF, 0, HALF * core)
    log_totals = []

    def write(block, result, log_total):
        count = Q_ROWS // HALF
        out[block * count : (block + 1) * count, ROWS:RET_ROWS, :] = result.reshape(count, HALF, HEAD_DIM)
        for row in range(Q_ROWS // HEAD_DIM):
            log_totals.append(log_total[:, row * HEAD_DIM : (row + 1) * HEAD_DIM])

    attend(lambda block: q_wide[block * Q_ROWS : (block + 1) * Q_ROWS, :], k_wide, v_turned, write)
    out[:, :ROWS, :] = whole[...]
    log_totals.append(jnp.zeros((RETURN - SHARED_LSE - len(log_totals), HEAD_DIM), jnp.float32))
    rows = jnp.concatenate([whole_lse[...], *log_totals], axis=0).astype(jnp.bfloat16)
    for device in range(N_SEQ):
        out[device, WHOLE_LSE:, :] = rows


Q_ROWS = 512
STEP_ROWS = 1024
VMEM = 32 * 2**20
PLACE_VMEM = 8 * 2**20
PROJECT_VMEM = 50 * 2**20


def attention_scratch():
    keys = N_SEQ * ROWS
    return [
        pltpu.VMEM((keys, 2 * HEAD_DIM), jnp.bfloat16),
        pltpu.VMEM((HEAD_DIM, keys), jnp.bfloat16),
        pltpu.VMEM((STEP_ROWS, 2 * HEAD_DIM), jnp.bfloat16),
    ]


def attention_cost(queries, keys):
    return pl.CostEstimate(
        flops=queries * keys * HEAD_DIM // 4,
        bytes_accessed=4 * keys * HEAD_DIM * 2,
        transcendentals=0,
    )


def attend_whole(received):
    keys = N_SEQ * ROWS
    steps = keys // STEP_ROWS
    sources = STEP_ROWS // ROWS
    return pl.pallas_call(
        whole_kernel,
        grid=(steps,),
        in_specs=[
            pl.BlockSpec((N_SEQ, CUT_ROWS, HEAD_DIM), lambda i: (0, SEND_ROWS // CUT_ROWS, 0)),
            pl.BlockSpec((sources, ROWS, HEAD_DIM), lambda i: (i, 0, 0)),
            pl.BlockSpec((N_SEQ, ROWS, HEAD_DIM), lambda i: (0, 1, 0)),
            pl.BlockSpec((N_SEQ, ROWS, HEAD_DIM), lambda i: (0, 2, 0)),
        ],
        out_specs=[
            pl.BlockSpec((sources, ROWS, HEAD_DIM), lambda i: (i, 0, 0)),
            pl.BlockSpec((sources, ROWS), lambda i: (i, 0)),
        ],
        out_shape=[
            jax.ShapeDtypeStruct((N_SEQ, ROWS, HEAD_DIM), jnp.bfloat16),
            jax.ShapeDtypeStruct((N_SEQ, ROWS), jnp.float32),
        ],
        scratch_shapes=attention_scratch(),
        compiler_params=pltpu.CompilerParams(vmem_limit_bytes=VMEM),
        cost_estimate=attention_cost(keys, keys),
        name="attend_whole",
    )(*[received] * 4)


def attend_shared(where, received, own_kv, far_kv, whole, whole_lse):
    keys = N_SEQ * ROWS
    full = lambda *shape: pl.BlockSpec(shape, lambda i, c: (0,) * len(shape))
    return pl.pallas_call(
        shared_kernel,
        grid_spec=pltpu.PrefetchScalarGridSpec(
            num_scalar_prefetch=1,
            grid=(1,),
            in_specs=[
                pl.BlockSpec((N_SEQ, CUT_ROWS, HEAD_DIM), lambda i, c: (0, SEND_ROWS // CUT_ROWS, 0)),
                pl.BlockSpec((N_SEQ, HALF, HEAD_DIM), lambda i, c: (0, A_ROWS // HALF, 0)),
                full(N_SEQ, 2 * HALF, HEAD_DIM),
                full(N_SEQ, 2 * HALF, HEAD_DIM),
                full(N_SEQ, ROWS, HEAD_DIM),
                full(N_SEQ, ROWS),
            ],
            out_specs=full(N_SEQ, RETURN, HEAD_DIM),
            scratch_shapes=attention_scratch(),
        ),
        out_shape=jax.ShapeDtypeStruct((N_SEQ, RETURN, HEAD_DIM), jnp.bfloat16),
        compiler_params=pltpu.CompilerParams(vmem_limit_bytes=VMEM),
        cost_estimate=attention_cost(keys // 2, keys),
        name="attend_shared",
    )(where, received, received, own_kv, far_kv, whole, whole_lse)


def place_kernel(where, mine, near, near_far, part, part_far, out):
    x, core = where[1], where[2]
    sign = 1 - 2 * core
    out[x] = mine[...]
    out[(x - sign + 4) % 4] = near[...]
    out[(x + sign + 4) % 4] = near_far[...]

    @pl.when(core == 0)
    def _():
        out[(x + 2) % 4] = part[...]

    @pl.when(core == 1)
    def _():
        out[(x + 2) % 4] = part_far[...]


def place(where, mine, near, near_far, part, part_far):
    rows, columns = mine.shape
    return pl.pallas_call(
        place_kernel,
        grid_spec=pltpu.PrefetchScalarGridSpec(
            num_scalar_prefetch=1,
            grid=(),
            in_specs=[pl.BlockSpec(memory_space=pltpu.VMEM)] * 5,
            out_specs=pl.BlockSpec(memory_space=pltpu.VMEM),
        ),
        out_shape=jax.ShapeDtypeStruct((4, rows, columns), jnp.bfloat16),
        compiler_params=pltpu.CompilerParams(vmem_limit_bytes=PLACE_VMEM),
        name="place",
    )(where, mine, near, near_far, part, part_far)


def slot_of(ret, head):
    chip, member = head // 3, head % 3
    low, high = ret.at[2 * chip], ret.at[2 * chip + 1]
    lane = lax.broadcasted_iota(jnp.int32, (1, HEAD_DIM), 1)
    rows = []
    for source in range(N_SEQ):
        whole = [ref[WHOLE_LSE : WHOLE_LSE + N_SEQ, :].astype(jnp.float32) for ref in (low, high)]
        shared = [ref[SHARED_LSE : SHARED_LSE + N_SEQ, :].astype(jnp.float32) for ref in (low, high)]
        left, right = (item[source // 2 : source // 2 + 1] for item in shared)
        if source % 2 == 0:
            right = pltpu.roll(right, HALF, 1)
        else:
            left = pltpu.roll(left, HALF, 1)
        both = jnp.where(lane < HALF, left, right)
        first, last = (item[source : source + 1] for item in whole)
        rows.append(jnp.where(member == 0, first, jnp.where(member == 1, both, last)))
    return rows


def project_kernel(where, ret, *refs):
    weights, (vis_out, txt_out, slots, held, sems) = refs[:9], refs[9:]
    y, core = where[0], where[2]
    sign = 1 - 2 * core
    columns = held.shape[2] // 2
    copies = []
    for index in range(7):
        to = held.at[index // 2, pl.ds(index % 2 * TRIO, TRIO)]
        copies.append(pltpu.make_async_copy(weights[index], to, sems.at[index]))
    for index in range(2):
        at = core if index == 0 else 1 - core
        start = pl.multiple_of(at * columns, columns)
        to = held.at[3, pl.ds(TRIO, TRIO), pl.ds(start, columns)]
        copies.append(pltpu.make_async_copy(weights[7 + index], to, sems.at[7 + index]))
    for copy in copies:
        copy.start()
    for slot in range(SLOTS):
        valid = where[5 + slot] > 0
        for source, row in enumerate(slot_of(ret, where[3 + slot])):
            row = jnp.where(valid, row, 0.0)
            at = source * VIS_ROWS
            slots[slot : slot + 1, at : at + VIS_ROWS] = row[:, :VIS_ROWS]
            at = VIS_SEQ + source * TXT_ROWS
            slots[slot : slot + 1, at : at + TXT_ROWS] = row[:, VIS_ROWS:]
    total = jnp.zeros((ROWS, 2 * columns), jnp.float32)
    pieces = []
    for index, hops in enumerate((0, 1, 2, 3, -1, -2, -3, 4)):
        chip = (y - hops * sign + 8) % 8
        low, high = ret[2 * chip], ret[2 * chip + 1]
        shared = jnp.concatenate([low[ROWS:RET_ROWS], high[ROWS:RET_ROWS]], axis=0)
        attention = jnp.concatenate([low[:ROWS], shared, high[:ROWS]], axis=1)
        txt_out[:, pl.ds(pl.multiple_of(chip * TRIO, TRIO), TRIO)] = attention[VIS_ROWS:]
        pieces.append(attention)
        copies[index].wait()
        if index % 2 == 1:
            if index == 7:
                copies[8].wait()
            both = jnp.concatenate(pieces[-2:], axis=1)
            total += jnp.dot(both, held[index // 2], preferred_element_type=jnp.float32)
    vis_out[...] = total[:VIS_ROWS].astype(jnp.bfloat16)


def project(where, returned, chunks, far_chunks):
    columns = chunks[0].shape[1]
    return pl.pallas_call(
        project_kernel,
        grid_spec=pltpu.PrefetchScalarGridSpec(
            num_scalar_prefetch=1,
            grid=(),
            in_specs=[pl.BlockSpec(memory_space=pltpu.VMEM)] + [pl.BlockSpec(memory_space=pltpu.HBM)] * 9,
            out_specs=[pl.BlockSpec(memory_space=pltpu.VMEM)] * 3,
            scratch_shapes=[
                pltpu.VMEM((4, 2 * TRIO, columns), jnp.bfloat16),
                pltpu.SemaphoreType.DMA((9,)),
            ],
        ),
        out_shape=[
            jax.ShapeDtypeStruct((VIS_ROWS, columns), jnp.bfloat16),
            jax.ShapeDtypeStruct((TXT_ROWS, HEADS * HEAD_DIM), jnp.bfloat16),
            jax.ShapeDtypeStruct((SLOTS, VIS_SEQ + TXT_SEQ), jnp.float32),
        ],
        compiler_params=pltpu.CompilerParams(vmem_limit_bytes=PROJECT_VMEM),
        name="project",
    )(where, returned, *chunks[:4], *far_chunks[:3], chunks[4], far_chunks[3])


AXES = ("dp", "seq")
X_SIZE = 4
Y_SIZE = 8


def permute(operand, target, cores=(0, 1)):
    pairs = []
    for y in range(Y_SIZE):
        for x in range(X_SIZE):
            for s in range(N_SEQ):
                ty, tx, ts = target(y, x, s)
                there = (ty % Y_SIZE) * X_SIZE + tx % X_SIZE
                if s % 2 in cores:
                    pairs.append(((y * X_SIZE + x) * N_SEQ + s, there * N_SEQ + ts))
    return lax.ppermute(operand, AXES, pairs)


def swap(operand, cores=(0, 1)):
    return permute(operand, lambda y, x, s: (y, x, s ^ 1), cores)


def shift_x(operand, hops, cores=(0, 1)):
    return permute(operand, lambda y, x, s: (y, x + hops * (1 - 2 * (s % 2)), s), cores)


def shift_y(operand):
    return permute(operand, lambda y, x, s: (y + 1 - 2 * (s % 2), x, s))


def heads_of_slots(head_map, seq_index):
    mine = (head_map == seq_index).astype(jnp.int32)
    rank = jnp.cumsum(mine) - 1
    ids = jnp.arange(HEADS, dtype=jnp.int32)
    picked = mine[None] * (rank[None] == jnp.arange(SLOTS, dtype=jnp.int32)[:, None])
    return jnp.concatenate([jnp.sum(picked * ids[None], axis=1), jnp.sum(picked, axis=1)])


def on_device(qkv_vis, qkv_txt, vis_segments, txt_segments, head_map, w_out):
    seq_index = lax.axis_index("seq")
    dp_index = lax.axis_index("dp")
    core = seq_index % 2
    half = w_out.shape[1] // 2
    place_here = jnp.stack([dp_index // X_SIZE, dp_index % X_SIZE, core]).astype(jnp.int32)
    where = jnp.concatenate([place_here, heads_of_slots(head_map, seq_index)])

    near = shift_x(w_out, 1)
    part = shift_x(w_out, 2, cores=(0,))
    sending = pack(qkv_vis, qkv_txt, vis_segments, txt_segments)
    received = lax.all_to_all(sending, "seq", split_axis=0, concat_axis=0, tiled=True)
    chunks = [place(where, w_out, near, swap(near), part, swap(part, cores=(0,))).reshape(-1, 2 * half)]
    chunks.append(shift_y(chunks[0]))
    chunks.append(shift_y(chunks[1]))
    far_chunks = [swap(chunks[1])]
    received, far_chunks[0] = lax.optimization_barrier((received, far_chunks[0]))
    own_kv = received[:, A_ROWS + HALF : SEND_ROWS]
    far_kv = swap(own_kv)
    whole, whole_lse = attend_whole(received)
    whole, far_kv, chunks[2] = lax.optimization_barrier((whole, far_kv, chunks[2]))
    chunks.append(shift_y(chunks[2]))
    returning = attend_shared(where, received, own_kv, far_kv, whole, whole_lse)
    returning, chunks[2] = lax.optimization_barrier((returning, chunks[2]))
    returned = lax.all_to_all(returning, "seq", split_axis=0, concat_axis=0, tiled=True)
    chunks.append(shift_y(lax.dynamic_slice_in_dim(chunks[3], core * half, half, 1)))
    far_chunks += [swap(chunk) for chunk in chunks[2:]]
    vis_out, txt_out, lse_slots = project(where, returned, chunks, far_chunks)
    return vis_out, txt_out, lse_slots


def solution(mesh):
    in_specs = (
        P(("dp", "seq"), None),
        P(("dp", "seq"), None),
        P(("dp", "seq")),
        P(("dp", "seq")),
        P(),
        P("dp", None),
    )
    out_specs = (P(("dp", "seq"), None), P(("dp", "seq"), None), P("seq", "dp"))
    return jax.shard_map(
        on_device, mesh=mesh, in_specs=in_specs, out_specs=out_specs, check_vma=False
    )
```

```python
import functools

import jax
import jax.numpy as jnp
from jax import lax
from jax.experimental import pallas as pl
from jax.experimental.pallas import tpu as pltpu
from jax.sharding import PartitionSpec as P

HEADS = 24
HEAD_DIM = 128
N_SEQ = 16
VIS_ROWS = 112
TXT_ROWS = 16
ROWS = VIS_ROWS + TXT_ROWS
HALF = ROWS // 2
TRIO = 3 * HEAD_DIM
CHIPS = 8
A_ROWS = 3 * ROWS
SEND_ROWS = A_ROWS + 3 * HALF
CUT_ROWS = 8
PAYLOAD = SEND_ROWS + CUT_ROWS
RET_ROWS = ROWS + HALF
WHOLE_LSE = RET_ROWS
SHARED_LSE = WHOLE_LSE + N_SEQ
RETURN = SHARED_LSE + N_SEQ
PACK_CHIPS = 4
VIS_SEQ = VIS_ROWS * N_SEQ
TXT_SEQ = TXT_ROWS * N_SEQ
SLOTS = 2
LOG2E = 1.4426950408889634
LN2 = 0.6931471805599453
BIG = -1e30


def pack_kernel(seg_vis, seg_txt, vq, vk, vv, tq, tk, tv, out):
    def even(ref):
        parity = (ref[...] & 1).astype(jnp.float32)
        count = jnp.sum(1.0 - parity, axis=1, keepdims=True)
        return jnp.broadcast_to(count, (CUT_ROWS // 2, HEAD_DIM))

    cuts = jnp.concatenate([even(seg_vis), even(seg_txt)], axis=0).astype(jnp.bfloat16)
    for chip in range(PACK_CHIPS):
        low, high = 2 * chip, 2 * chip + 1
        for part, (vis, txt) in enumerate(((vq, tq), (vk, tk), (vv, tv))):
            row = part * ROWS
            for device, column in ((low, chip * TRIO), (high, chip * TRIO + 2 * HEAD_DIM)):
                columns = slice(column, column + HEAD_DIM)
                out[device, row : row + VIS_ROWS, :] = vis[:, columns]
                out[device, row + VIS_ROWS : row + ROWS, :] = txt[:, columns]
            row = A_ROWS + part * HALF
            columns = slice(chip * TRIO + HEAD_DIM, chip * TRIO + 2 * HEAD_DIM)
            out[low, row : row + HALF, :] = vis[:HALF, columns]
            out[high, row : row + VIS_ROWS - HALF, :] = vis[HALF:, columns]
            out[high, row + VIS_ROWS - HALF : row + HALF, :] = txt[:, columns]
        out[low, SEND_ROWS:PAYLOAD, :] = cuts
        out[high, SEND_ROWS:PAYLOAD, :] = cuts


def pack(qkv_vis, qkv_txt, vis_segments, txt_segments):
    steps = CHIPS // PACK_CHIPS

    def spec(rows, part):
        return pl.BlockSpec((rows, PACK_CHIPS * TRIO), lambda i: (0, part * steps + i))

    return pl.pallas_call(
        pack_kernel,
        grid=(steps,),
        in_specs=[
            pl.BlockSpec((1, VIS_ROWS), lambda i: (0, 0)),
            pl.BlockSpec((1, TXT_ROWS), lambda i: (0, 0)),
            *[spec(VIS_ROWS, part) for part in range(3)],
            *[spec(TXT_ROWS, part) for part in range(3)],
        ],
        out_specs=pl.BlockSpec((2 * PACK_CHIPS, PAYLOAD, HEAD_DIM), lambda i: (i, 0, 0)),
        out_shape=jax.ShapeDtypeStruct((N_SEQ, PAYLOAD, HEAD_DIM), jnp.bfloat16),
        name="pack",
    )(
        vis_segments.reshape(1, VIS_ROWS),
        txt_segments.reshape(1, TXT_ROWS),
        *[qkv_vis] * 3,
        *[qkv_txt] * 3,
    )


def clip_features(cut, first_source, count, rows, offset, value, second_lane):
    cuts = jnp.sum(cut[...].astype(jnp.float32), axis=0)
    vis_cut, txt_cut = cuts[0:1], cuts[CUT_ROWS // 2 : CUT_ROWS // 2 + 1]
    row = lax.broadcasted_iota(jnp.int32, (rows, HEAD_DIM), 0) + offset
    is_vis, row = row < VIS_ROWS, row.astype(jnp.float32)
    behind = jnp.where(is_vis, row - vis_cut, row - VIS_ROWS - txt_cut)
    stride = jnp.where(is_vis, float(VIS_ROWS), float(TXT_ROWS))
    lane = lax.broadcasted_iota(jnp.int32, (1, HEAD_DIM), 1)
    second = jnp.where(lane == second_lane, value, 0.0)
    first = jnp.where(lane == 1 - second_lane, value, 0.0)
    behind = behind + stride * first_source
    pieces = []
    for _ in range(count):
        pieces.append(jnp.where(behind >= 0.0, second, first).astype(jnp.bfloat16))
        behind = behind + stride
    return jnp.concatenate(pieces, axis=0)


def attend(queries, k_wide, v_turned, write):
    factor = HEAD_DIM**-0.5 * LOG2E

    def score(block):
        return lax.dot_general(
            k_wide[...], queries(block), (((1,), (1,)), ((), ())), preferred_element_type=jnp.float32
        )

    blocks = STEP_ROWS // Q_ROWS
    scores = score(0)
    for block in range(blocks):
        upcoming = score(block + 1) if block + 1 < blocks else None
        highest = jnp.max(scores, axis=0, keepdims=True)
        exponent = jnp.exp2((scores - highest) * factor)
        total = jnp.sum(exponent, axis=0, keepdims=True)
        blended = jnp.dot(
            v_turned[...], exponent.astype(jnp.bfloat16), preferred_element_type=jnp.float32
        )
        result = jnp.swapaxes(blended * (1.0 / total), 0, 1).astype(jnp.bfloat16)
        write(block, result, highest * HEAD_DIM**-0.5 + jnp.log2(total) * LN2)
        scores = upcoming


def key_features(cut, rows, offset):
    return clip_features(cut, 0.0, N_SEQ, rows, offset, BIG, 0)


def query_features(cut, first_source, rows, offset):
    return clip_features(cut, first_source, STEP_ROWS // rows, rows, offset, 1.0, 1)


def whole_kernel(cut, q, k, v, out, lse, k_wide, v_turned, q_wide):
    step = pl.program_id(0)
    keys = N_SEQ * ROWS
    sources = STEP_ROWS // ROWS

    @pl.when(step == 0)
    def _():
        k_wide[:, :HEAD_DIM] = k[...].reshape(keys, HEAD_DIM)
        k_wide[:, HEAD_DIM:] = key_features(cut, ROWS, 0)
        v_turned[...] = jnp.swapaxes(v[...].reshape(keys, HEAD_DIM), 0, 1)

    q_wide[:, :HEAD_DIM] = q[...].reshape(STEP_ROWS, HEAD_DIM)
    q_wide[:, HEAD_DIM:] = query_features(cut, (step * sources).astype(jnp.float32), ROWS, 0)

    def write(block, result, log_total):
        count = Q_ROWS // ROWS
        out[block * count : (block + 1) * count] = result.reshape(count, ROWS, HEAD_DIM)
        for row in range(count):
            lse[block * count + row : block * count + row + 1, :] = log_total[
                :, row * HEAD_DIM : (row + 1) * HEAD_DIM
            ]

    attend(lambda block: q_wide[block * Q_ROWS : (block + 1) * Q_ROWS, :], k_wide, v_turned, write)


def shared_kernel(where, cut, q, own_kv, far_kv, whole, whole_lse, out, k_wide, v_turned, q_wide):
    core = where[2]
    keys = N_SEQ * HALF
    for place, (kv, offset) in enumerate(((own_kv, HALF * core), (far_kv, HALF * (1 - core)))):
        at = slice(place * keys, (place + 1) * keys)
        k_wide[at, :HEAD_DIM] = kv[:, :HALF].reshape(keys, HEAD_DIM)
        k_wide[at, HEAD_DIM:] = key_features(cut, HALF, offset)
        v_turned[:, at] = jnp.swapaxes(kv[:, HALF:].reshape(keys, HEAD_DIM), 0, 1)
    q_wide[:, :HEAD_DIM] = q[...].reshape(STEP_ROWS, HEAD_DIM)
    q_wide[:, HEAD_DIM:] = query_features(cut, 0.0, HALF, HALF * core)
    log_totals = []

    def write(block, result, log_total):
        count = Q_ROWS // HALF
        out[block * count : (block + 1) * count, ROWS:RET_ROWS, :] = result.reshape(count, HALF, HEAD_DIM)
        for row in range(Q_ROWS // HEAD_DIM):
            log_totals.append(log_total[:, row * HEAD_DIM : (row + 1) * HEAD_DIM])

    attend(lambda block: q_wide[block * Q_ROWS : (block + 1) * Q_ROWS, :], k_wide, v_turned, write)
    out[:, :ROWS, :] = whole[...]
    log_totals.append(jnp.zeros((RETURN - SHARED_LSE - len(log_totals), HEAD_DIM), jnp.float32))
    rows = jnp.concatenate([whole_lse[...], *log_totals], axis=0).astype(jnp.bfloat16)
    for device in range(N_SEQ):
        out[device, WHOLE_LSE:, :] = rows


Q_ROWS = 512
STEP_ROWS = 1024
VMEM = 32 * 2**20
PLACE_VMEM = 8 * 2**20
PROJECT_VMEM = 50 * 2**20


def attention_scratch():
    keys = N_SEQ * ROWS
    return [
        pltpu.VMEM((keys, 2 * HEAD_DIM), jnp.bfloat16),
        pltpu.VMEM((HEAD_DIM, keys), jnp.bfloat16),
        pltpu.VMEM((STEP_ROWS, 2 * HEAD_DIM), jnp.bfloat16),
    ]


def attention_cost(queries, keys):
    return pl.CostEstimate(
        flops=queries * keys * HEAD_DIM // 4,
        bytes_accessed=4 * keys * HEAD_DIM * 2,
        transcendentals=0,
    )


def attend_whole(received):
    keys = N_SEQ * ROWS
    steps = keys // STEP_ROWS
    sources = STEP_ROWS // ROWS
    return pl.pallas_call(
        whole_kernel,
        grid=(steps,),
        in_specs=[
            pl.BlockSpec((N_SEQ, CUT_ROWS, HEAD_DIM), lambda i: (0, SEND_ROWS // CUT_ROWS, 0)),
            pl.BlockSpec((sources, ROWS, HEAD_DIM), lambda i: (i, 0, 0)),
            pl.BlockSpec((N_SEQ, ROWS, HEAD_DIM), lambda i: (0, 1, 0)),
            pl.BlockSpec((N_SEQ, ROWS, HEAD_DIM), lambda i: (0, 2, 0)),
        ],
        out_specs=[
            pl.BlockSpec((sources, ROWS, HEAD_DIM), lambda i: (i, 0, 0)),
            pl.BlockSpec((sources, ROWS), lambda i: (i, 0)),
        ],
        out_shape=[
            jax.ShapeDtypeStruct((N_SEQ, ROWS, HEAD_DIM), jnp.bfloat16),
            jax.ShapeDtypeStruct((N_SEQ, ROWS), jnp.float32),
        ],
        scratch_shapes=attention_scratch(),
        compiler_params=pltpu.CompilerParams(vmem_limit_bytes=VMEM),
        cost_estimate=attention_cost(keys, keys),
        name="attend_whole",
    )(*[received] * 4)


def attend_shared(where, received, own_kv, far_kv, whole, whole_lse):
    keys = N_SEQ * ROWS
    full = lambda *shape: pl.BlockSpec(shape, lambda i, c: (0,) * len(shape))
    return pl.pallas_call(
        shared_kernel,
        grid_spec=pltpu.PrefetchScalarGridSpec(
            num_scalar_prefetch=1,
            grid=(1,),
            in_specs=[
                pl.BlockSpec((N_SEQ, CUT_ROWS, HEAD_DIM), lambda i, c: (0, SEND_ROWS // CUT_ROWS, 0)),
                pl.BlockSpec((N_SEQ, HALF, HEAD_DIM), lambda i, c: (0, A_ROWS // HALF, 0)),
                full(N_SEQ, 2 * HALF, HEAD_DIM),
                full(N_SEQ, 2 * HALF, HEAD_DIM),
                full(N_SEQ, ROWS, HEAD_DIM),
                full(N_SEQ, ROWS),
            ],
            out_specs=full(N_SEQ, RETURN, HEAD_DIM),
            scratch_shapes=attention_scratch(),
        ),
        out_shape=jax.ShapeDtypeStruct((N_SEQ, RETURN, HEAD_DIM), jnp.bfloat16),
        compiler_params=pltpu.CompilerParams(vmem_limit_bytes=VMEM),
        cost_estimate=attention_cost(keys // 2, keys),
        name="attend_shared",
    )(where, received, received, own_kv, far_kv, whole, whole_lse)


def place_kernel(where, mine, near, near_far, part, part_far, out):
    x, core = where[1], where[2]
    sign = 1 - 2 * core
    out[x] = mine[...]
    out[(x - sign + 4) % 4] = near[...]
    out[(x + sign + 4) % 4] = near_far[...]

    @pl.when(core == 0)
    def _():
        out[(x + 2) % 4] = part[...]

    @pl.when(core == 1)
    def _():
        out[(x + 2) % 4] = part_far[...]


def place(where, mine, near, near_far, part, part_far):
    rows, columns = mine.shape
    return pl.pallas_call(
        place_kernel,
        grid_spec=pltpu.PrefetchScalarGridSpec(
            num_scalar_prefetch=1,
            grid=(),
            in_specs=[pl.BlockSpec(memory_space=pltpu.VMEM)] * 5,
            out_specs=pl.BlockSpec(memory_space=pltpu.VMEM),
        ),
        out_shape=jax.ShapeDtypeStruct((4, rows, columns), jnp.bfloat16),
        compiler_params=pltpu.CompilerParams(vmem_limit_bytes=PLACE_VMEM),
        name="place",
    )(where, mine, near, near_far, part, part_far)


def slot_of(ret, head):
    chip, member = head // 3, head % 3
    low, high = ret.at[2 * chip], ret.at[2 * chip + 1]
    lane = lax.broadcasted_iota(jnp.int32, (1, HEAD_DIM), 1)
    rows = []
    for source in range(N_SEQ):
        whole = [ref[WHOLE_LSE : WHOLE_LSE + N_SEQ, :].astype(jnp.float32) for ref in (low, high)]
        shared = [ref[SHARED_LSE : SHARED_LSE + N_SEQ, :].astype(jnp.float32) for ref in (low, high)]
        left, right = (item[source // 2 : source // 2 + 1] for item in shared)
        if source % 2 == 0:
            right = pltpu.roll(right, HALF, 1)
        else:
            left = pltpu.roll(left, HALF, 1)
        both = jnp.where(lane < HALF, left, right)
        first, last = (item[source : source + 1] for item in whole)
        rows.append(jnp.where(member == 0, first, jnp.where(member == 1, both, last)))
    return rows


def project_kernel(where, ret, *refs):
    weights, (vis_out, txt_out, slots, held, sems) = refs[:9], refs[9:]
    y, core = where[0], where[2]
    sign = 1 - 2 * core
    columns = held.shape[2] // 2
    copies = []
    for index in range(7):
        to = held.at[index // 2, pl.ds(index % 2 * TRIO, TRIO)]
        copies.append(pltpu.make_async_copy(weights[index], to, sems.at[index]))
    for index in range(2):
        at = core if index == 0 else 1 - core
        start = pl.multiple_of(at * columns, columns)
        to = held.at[3, pl.ds(TRIO, TRIO), pl.ds(start, columns)]
        copies.append(pltpu.make_async_copy(weights[7 + index], to, sems.at[7 + index]))
    for copy in copies:
        copy.start()
    for slot in range(SLOTS):
        valid = where[5 + slot] > 0
        for source, row in enumerate(slot_of(ret, where[3 + slot])):
            row = jnp.where(valid, row, 0.0)
            at = source * VIS_ROWS
            slots[slot : slot + 1, at : at + VIS_ROWS] = row[:, :VIS_ROWS]
            at = VIS_SEQ + source * TXT_ROWS
            slots[slot : slot + 1, at : at + TXT_ROWS] = row[:, VIS_ROWS:]
    total = jnp.zeros((ROWS, 2 * columns), jnp.float32)
    pieces = []
    for index, hops in enumerate((0, 1, 2, 3, -1, -2, -3, 4)):
        chip = (y - hops * sign + 8) % 8
        low, high = ret[2 * chip], ret[2 * chip + 1]
        shared = jnp.concatenate([low[ROWS:RET_ROWS], high[ROWS:RET_ROWS]], axis=0)
        attention = jnp.concatenate([low[:ROWS], shared, high[:ROWS]], axis=1)
        txt_out[:, pl.ds(pl.multiple_of(chip * TRIO, TRIO), TRIO)] = attention[VIS_ROWS:]
        pieces.append(attention)
        copies[index].wait()
        if index % 2 == 1:
            if index == 7:
                copies[8].wait()
            both = jnp.concatenate(pieces[-2:], axis=1)
            total += jnp.dot(both, held[index // 2], preferred_element_type=jnp.float32)
    vis_out[...] = total[:VIS_ROWS].astype(jnp.bfloat16)


def project(where, returned, chunks, far_chunks):
    columns = chunks[0].shape[1]
    return pl.pallas_call(
        project_kernel,
        grid_spec=pltpu.PrefetchScalarGridSpec(
            num_scalar_prefetch=1,
            grid=(),
            in_specs=[pl.BlockSpec(memory_space=pltpu.VMEM)] + [pl.BlockSpec(memory_space=pltpu.HBM)] * 9,
            out_specs=[pl.BlockSpec(memory_space=pltpu.VMEM)] * 3,
            scratch_shapes=[
                pltpu.VMEM((4, 2 * TRIO, columns), jnp.bfloat16),
                pltpu.SemaphoreType.DMA((9,)),
            ],
        ),
        out_shape=[
            jax.ShapeDtypeStruct((VIS_ROWS, columns), jnp.bfloat16),
            jax.ShapeDtypeStruct((TXT_ROWS, HEADS * HEAD_DIM), jnp.bfloat16),
            jax.ShapeDtypeStruct((SLOTS, VIS_SEQ + TXT_SEQ), jnp.float32),
        ],
        compiler_params=pltpu.CompilerParams(vmem_limit_bytes=PROJECT_VMEM),
        name="project",
    )(where, returned, *chunks[:4], *far_chunks[:3], chunks[4], far_chunks[3])


AXES = ("dp", "seq")
X_SIZE = 4
Y_SIZE = 8


def permute(operand, target, cores=(0, 1)):
    pairs = []
    for y in range(Y_SIZE):
        for x in range(X_SIZE):
            for s in range(N_SEQ):
                ty, tx, ts = target(y, x, s)
                there = (ty % Y_SIZE) * X_SIZE + tx % X_SIZE
                if s % 2 in cores:
                    pairs.append(((y * X_SIZE + x) * N_SEQ + s, there * N_SEQ + ts))
    return lax.ppermute(operand, AXES, pairs)


def swap(operand, cores=(0, 1)):
    return permute(operand, lambda y, x, s: (y, x, s ^ 1), cores)


def shift_x(operand, hops, cores=(0, 1)):
    return permute(operand, lambda y, x, s: (y, x + hops * (1 - 2 * (s % 2)), s), cores)


def shift_y(operand):
    return permute(operand, lambda y, x, s: (y + 1 - 2 * (s % 2), x, s))


def heads_of_slots(head_map, seq_index):
    mine = (head_map == seq_index).astype(jnp.int32)
    rank = jnp.cumsum(mine) - 1
    ids = jnp.arange(HEADS, dtype=jnp.int32)
    picked = mine[None] * (rank[None] == jnp.arange(SLOTS, dtype=jnp.int32)[:, None])
    return jnp.concatenate([jnp.sum(picked * ids[None], axis=1), jnp.sum(picked, axis=1)])


def on_device(qkv_vis, qkv_txt, vis_segments, txt_segments, head_map, w_out):
    seq_index = lax.axis_index("seq")
    dp_index = lax.axis_index("dp")
    core = seq_index % 2
    half = w_out.shape[1] // 2
    place_here = jnp.stack([dp_index // X_SIZE, dp_index % X_SIZE, core]).astype(jnp.int32)
    where = jnp.concatenate([place_here, heads_of_slots(head_map, seq_index)])

    near = shift_x(w_out, 1)
    part = shift_x(w_out, 2, cores=(0,))
    sending = pack(qkv_vis, qkv_txt, vis_segments, txt_segments)
    received = lax.all_to_all(sending, "seq", split_axis=0, concat_axis=0, tiled=True)
    chunks = [place(where, w_out, near, swap(near), part, swap(part, cores=(0,))).reshape(-1, 2 * half)]
    chunks.append(shift_y(chunks[0]))
    chunks.append(shift_y(chunks[1]))
    far_chunks = [swap(chunks[1])]
    received, far_chunks[0] = lax.optimization_barrier((received, far_chunks[0]))
    own_kv = received[:, A_ROWS + HALF : SEND_ROWS]
    far_kv = swap(own_kv)
    whole, whole_lse = attend_whole(received)
    whole, far_kv, chunks[2] = lax.optimization_barrier((whole, far_kv, chunks[2]))
    chunks.append(shift_y(chunks[2]))
    returning = attend_shared(where, received, own_kv, far_kv, whole, whole_lse)
    returning, chunks[2] = lax.optimization_barrier((returning, chunks[2]))
    returned = lax.all_to_all(returning, "seq", split_axis=0, concat_axis=0, tiled=True)
    chunks.append(shift_y(lax.dynamic_slice_in_dim(chunks[3], core * half, half, 1)))
    far_chunks += [swap(chunk) for chunk in chunks[2:]]
    vis_out, txt_out, lse_slots = project(where, returned, chunks, far_chunks)
    return vis_out, txt_out, lse_slots


def solution(mesh):
    in_specs = (
        P(("dp", "seq"), None),
        P(("dp", "seq"), None),
        P(("dp", "seq")),
        P(("dp", "seq")),
        P(),
        P("dp", None),
    )
    out_specs = (P(("dp", "seq"), None), P(("dp", "seq"), None), P("seq", "dp"))
    return jax.shard_map(
        on_device, mesh=mesh, in_specs=in_specs, out_specs=out_specs, check_vma=False
    )
```

```python
import functools

import jax
import jax.numpy as jnp
from jax import lax
from jax.experimental import pallas as pl
from jax.experimental.pallas import tpu as pltpu
from jax.sharding import PartitionSpec as P

HEADS = 24
HEAD_DIM = 128
N_SEQ = 16
VIS_ROWS = 112
TXT_ROWS = 16
ROWS = VIS_ROWS + TXT_ROWS
HALF = ROWS // 2
TRIO = 3 * HEAD_DIM
CHIPS = 8
A_ROWS = 3 * ROWS
SEND_ROWS = A_ROWS + 3 * HALF
CUT_ROWS = 8
PAYLOAD = SEND_ROWS + CUT_ROWS
RET_ROWS = ROWS + HALF
WHOLE_LSE = RET_ROWS
SHARED_LSE = WHOLE_LSE + N_SEQ
RETURN = SHARED_LSE + N_SEQ
PACK_CHIPS = 4
VIS_SEQ = VIS_ROWS * N_SEQ
TXT_SEQ = TXT_ROWS * N_SEQ
SLOTS = 2
LOG2E = 1.4426950408889634
LN2 = 0.6931471805599453
BIG = -1e30


def pack_kernel(seg_vis, seg_txt, vq, vk, vv, tq, tk, tv, out):
    def even(ref):
        parity = (ref[...] & 1).astype(jnp.float32)
        count = jnp.sum(1.0 - parity, axis=1, keepdims=True)
        return jnp.broadcast_to(count, (CUT_ROWS // 2, HEAD_DIM))

    cuts = jnp.concatenate([even(seg_vis), even(seg_txt)], axis=0).astype(jnp.bfloat16)
    for chip in range(PACK_CHIPS):
        low, high = 2 * chip, 2 * chip + 1
        for part, (vis, txt) in enumerate(((vq, tq), (vk, tk), (vv, tv))):
            row = part * ROWS
            for device, column in ((low, chip * TRIO), (high, chip * TRIO + 2 * HEAD_DIM)):
                columns = slice(column, column + HEAD_DIM)
                out[device, row : row + VIS_ROWS, :] = vis[:, columns]
                out[device, row + VIS_ROWS : row + ROWS, :] = txt[:, columns]
            row = A_ROWS + part * HALF
            columns = slice(chip * TRIO + HEAD_DIM, chip * TRIO + 2 * HEAD_DIM)
            out[low, row : row + HALF, :] = vis[:HALF, columns]
            out[high, row : row + VIS_ROWS - HALF, :] = vis[HALF:, columns]
            out[high, row + VIS_ROWS - HALF : row + HALF, :] = txt[:, columns]
        out[low, SEND_ROWS:PAYLOAD, :] = cuts
        out[high, SEND_ROWS:PAYLOAD, :] = cuts


def pack(qkv_vis, qkv_txt, vis_segments, txt_segments):
    steps = CHIPS // PACK_CHIPS

    def spec(rows, part):
        return pl.BlockSpec((rows, PACK_CHIPS * TRIO), lambda i: (0, part * steps + i))

    return pl.pallas_call(
        pack_kernel,
        grid=(steps,),
        in_specs=[
            pl.BlockSpec((1, VIS_ROWS), lambda i: (0, 0)),
            pl.BlockSpec((1, TXT_ROWS), lambda i: (0, 0)),
            *[spec(VIS_ROWS, part) for part in range(3)],
            *[spec(TXT_ROWS, part) for part in range(3)],
        ],
        out_specs=pl.BlockSpec((2 * PACK_CHIPS, PAYLOAD, HEAD_DIM), lambda i: (i, 0, 0)),
        out_shape=jax.ShapeDtypeStruct((N_SEQ, PAYLOAD, HEAD_DIM), jnp.bfloat16),
        name="pack",
    )(
        vis_segments.reshape(1, VIS_ROWS),
        txt_segments.reshape(1, TXT_ROWS),
        *[qkv_vis] * 3,
        *[qkv_txt] * 3,
    )


def clip_features(cut, first_source, count, rows, offset, value, second_lane):
    cuts = jnp.sum(cut[...].astype(jnp.float32), axis=0)
    vis_cut, txt_cut = cuts[0:1], cuts[CUT_ROWS // 2 : CUT_ROWS // 2 + 1]
    row = lax.broadcasted_iota(jnp.int32, (rows, HEAD_DIM), 0) + offset
    is_vis, row = row < VIS_ROWS, row.astype(jnp.float32)
    behind = jnp.where(is_vis, row - vis_cut, row - VIS_ROWS - txt_cut)
    stride = jnp.where(is_vis, float(VIS_ROWS), float(TXT_ROWS))
    lane = lax.broadcasted_iota(jnp.int32, (1, HEAD_DIM), 1)
    second = jnp.where(lane == second_lane, value, 0.0)
    first = jnp.where(lane == 1 - second_lane, value, 0.0)
    behind = behind + stride * first_source
    pieces = []
    for _ in range(count):
        pieces.append(jnp.where(behind >= 0.0, second, first).astype(jnp.bfloat16))
        behind = behind + stride
    return jnp.concatenate(pieces, axis=0)


def attend(queries, k_wide, v_turned, write):
    factor = HEAD_DIM**-0.5 * LOG2E

    def score(block):
        return lax.dot_general(
            k_wide[...], queries(block), (((1,), (1,)), ((), ())), preferred_element_type=jnp.float32
        )

    blocks = STEP_ROWS // Q_ROWS
    scores = score(0)
    for block in range(blocks):
        upcoming = score(block + 1) if block + 1 < blocks else None
        highest = jnp.max(scores, axis=0, keepdims=True)
        exponent = jnp.exp2((scores - highest) * factor)
        total = jnp.sum(exponent, axis=0, keepdims=True)
        blended = jnp.dot(
            v_turned[...], exponent.astype(jnp.bfloat16), preferred_element_type=jnp.float32
        )
        result = jnp.swapaxes(blended * (1.0 / total), 0, 1).astype(jnp.bfloat16)
        write(block, result, highest * HEAD_DIM**-0.5 + jnp.log2(total) * LN2)
        scores = upcoming


def key_features(cut, rows, offset):
    return clip_features(cut, 0.0, N_SEQ, rows, offset, BIG, 0)


def query_features(cut, first_source, rows, offset):
    return clip_features(cut, first_source, STEP_ROWS // rows, rows, offset, 1.0, 1)


def whole_kernel(cut, q, k, v, out, lse, k_wide, v_turned, q_wide):
    step = pl.program_id(0)
    keys = N_SEQ * ROWS
    sources = STEP_ROWS // ROWS

    @pl.when(step == 0)
    def _():
        k_wide[:, :HEAD_DIM] = k[...].reshape(keys, HEAD_DIM)
        k_wide[:, HEAD_DIM:] = key_features(cut, ROWS, 0)
        v_turned[...] = jnp.swapaxes(v[...].reshape(keys, HEAD_DIM), 0, 1)

    q_wide[:, :HEAD_DIM] = q[...].reshape(STEP_ROWS, HEAD_DIM)
    q_wide[:, HEAD_DIM:] = query_features(cut, (step * sources).astype(jnp.float32), ROWS, 0)

    def write(block, result, log_total):
        count = Q_ROWS // ROWS
        out[block * count : (block + 1) * count] = result.reshape(count, ROWS, HEAD_DIM)
        for row in range(count):
            lse[block * count + row : block * count + row + 1, :] = log_total[
                :, row * HEAD_DIM : (row + 1) * HEAD_DIM
            ]

    attend(lambda block: q_wide[block * Q_ROWS : (block + 1) * Q_ROWS, :], k_wide, v_turned, write)


def shared_kernel(where, cut, q, own_kv, far_kv, whole, whole_lse, out, k_wide, v_turned, q_wide):
    core = where[2]
    keys = N_SEQ * HALF
    for place, (kv, offset) in enumerate(((own_kv, HALF * core), (far_kv, HALF * (1 - core)))):
        at = slice(place * keys, (place + 1) * keys)
        k_wide[at, :HEAD_DIM] = kv[:, :HALF].reshape(keys, HEAD_DIM)
        k_wide[at, HEAD_DIM:] = key_features(cut, HALF, offset)
        v_turned[:, at] = jnp.swapaxes(kv[:, HALF:].reshape(keys, HEAD_DIM), 0, 1)
    q_wide[:, :HEAD_DIM] = q[...].reshape(STEP_ROWS, HEAD_DIM)
    q_wide[:, HEAD_DIM:] = query_features(cut, 0.0, HALF, HALF * core)
    log_totals = []

    def write(block, result, log_total):
        count = Q_ROWS // HALF
        out[block * count : (block + 1) * count, ROWS:RET_ROWS, :] = result.reshape(count, HALF, HEAD_DIM)
        for row in range(Q_ROWS // HEAD_DIM):
            log_totals.append(log_total[:, row * HEAD_DIM : (row + 1) * HEAD_DIM])

    attend(lambda block: q_wide[block * Q_ROWS : (block + 1) * Q_ROWS, :], k_wide, v_turned, write)
    out[:, :ROWS, :] = whole[...]
    log_totals.append(jnp.zeros((RETURN - SHARED_LSE - len(log_totals), HEAD_DIM), jnp.float32))
    rows = jnp.concatenate([whole_lse[...], *log_totals], axis=0).astype(jnp.bfloat16)
    for device in range(N_SEQ):
        out[device, WHOLE_LSE:, :] = rows


Q_ROWS = 512
STEP_ROWS = 1024
VMEM = 32 * 2**20
PLACE_VMEM = 8 * 2**20
PROJECT_VMEM = 50 * 2**20


def attention_scratch():
    keys = N_SEQ * ROWS
    return [
        pltpu.VMEM((keys, 2 * HEAD_DIM), jnp.bfloat16),
        pltpu.VMEM((HEAD_DIM, keys), jnp.bfloat16),
        pltpu.VMEM((STEP_ROWS, 2 * HEAD_DIM), jnp.bfloat16),
    ]


def attention_cost(queries, keys):
    return pl.CostEstimate(
        flops=queries * keys * HEAD_DIM // 4,
        bytes_accessed=4 * keys * HEAD_DIM * 2,
        transcendentals=0,
    )


def attend_whole(received):
    keys = N_SEQ * ROWS
    steps = keys // STEP_ROWS
    sources = STEP_ROWS // ROWS
    return pl.pallas_call(
        whole_kernel,
        grid=(steps,),
        in_specs=[
            pl.BlockSpec((N_SEQ, CUT_ROWS, HEAD_DIM), lambda i: (0, SEND_ROWS // CUT_ROWS, 0)),
            pl.BlockSpec((sources, ROWS, HEAD_DIM), lambda i: (i, 0, 0)),
            pl.BlockSpec((N_SEQ, ROWS, HEAD_DIM), lambda i: (0, 1, 0)),
            pl.BlockSpec((N_SEQ, ROWS, HEAD_DIM), lambda i: (0, 2, 0)),
        ],
        out_specs=[
            pl.BlockSpec((sources, ROWS, HEAD_DIM), lambda i: (i, 0, 0)),
            pl.BlockSpec((sources, ROWS), lambda i: (i, 0)),
        ],
        out_shape=[
            jax.ShapeDtypeStruct((N_SEQ, ROWS, HEAD_DIM), jnp.bfloat16),
            jax.ShapeDtypeStruct((N_SEQ, ROWS), jnp.float32),
        ],
        scratch_shapes=attention_scratch(),
        compiler_params=pltpu.CompilerParams(vmem_limit_bytes=VMEM),
        cost_estimate=attention_cost(keys, keys),
        name="attend_whole",
    )(*[received] * 4)


def attend_shared(where, received, own_kv, far_kv, whole, whole_lse):
    keys = N_SEQ * ROWS
    full = lambda *shape: pl.BlockSpec(shape, lambda i, c: (0,) * len(shape))
    return pl.pallas_call(
        shared_kernel,
        grid_spec=pltpu.PrefetchScalarGridSpec(
            num_scalar_prefetch=1,
            grid=(1,),
            in_specs=[
                pl.BlockSpec((N_SEQ, CUT_ROWS, HEAD_DIM), lambda i, c: (0, SEND_ROWS // CUT_ROWS, 0)),
                pl.BlockSpec((N_SEQ, HALF, HEAD_DIM), lambda i, c: (0, A_ROWS // HALF, 0)),
                full(N_SEQ, 2 * HALF, HEAD_DIM),
                full(N_SEQ, 2 * HALF, HEAD_DIM),
                full(N_SEQ, ROWS, HEAD_DIM),
                full(N_SEQ, ROWS),
            ],
            out_specs=full(N_SEQ, RETURN, HEAD_DIM),
            scratch_shapes=attention_scratch(),
        ),
        out_shape=jax.ShapeDtypeStruct((N_SEQ, RETURN, HEAD_DIM), jnp.bfloat16),
        compiler_params=pltpu.CompilerParams(vmem_limit_bytes=VMEM),
        cost_estimate=attention_cost(keys // 2, keys),
        name="attend_shared",
    )(where, received, received, own_kv, far_kv, whole, whole_lse)


def place_kernel(where, mine, near, near_far, part, part_far, *halves):
    x, core = where[1], where[2]
    sign = 1 - 2 * core

    def put(to, shard):
        to = (to + X_SIZE) % X_SIZE
        for half, out in enumerate(halves):

            @pl.when(to // 2 == half)
            def _():
                out[to % 2] = shard[...]

    put(x, mine)
    put(x - sign, near)
    put(x + sign, near_far)

    @pl.when(core == 0)
    def _():
        put(x + 2, part)

    @pl.when(core == 1)
    def _():
        put(x + 2, part_far)


def place(where, mine, near, near_far, part, part_far):
    rows, columns = mine.shape
    return pl.pallas_call(
        place_kernel,
        grid_spec=pltpu.PrefetchScalarGridSpec(
            num_scalar_prefetch=1,
            grid=(),
            in_specs=[pl.BlockSpec(memory_space=pltpu.VMEM)] * 5,
            out_specs=[pl.BlockSpec(memory_space=pltpu.VMEM)] * 2,
        ),
        out_shape=[jax.ShapeDtypeStruct((2, rows, columns), jnp.bfloat16)] * 2,
        compiler_params=pltpu.CompilerParams(vmem_limit_bytes=PLACE_VMEM),
        name="place",
    )(where, mine, near, near_far, part, part_far)


def slot_of(ret, head):
    chip, member = head // 3, head % 3
    low, high = ret.at[2 * chip], ret.at[2 * chip + 1]
    lane = lax.broadcasted_iota(jnp.int32, (1, HEAD_DIM), 1)
    rows = []
    for source in range(N_SEQ):
        whole = [ref[WHOLE_LSE : WHOLE_LSE + N_SEQ, :].astype(jnp.float32) for ref in (low, high)]
        shared = [ref[SHARED_LSE : SHARED_LSE + N_SEQ, :].astype(jnp.float32) for ref in (low, high)]
        left, right = (item[source // 2 : source // 2 + 1] for item in shared)
        if source % 2 == 0:
            right = pltpu.roll(right, HALF, 1)
        else:
            left = pltpu.roll(left, HALF, 1)
        both = jnp.where(lane < HALF, left, right)
        first, last = (item[source : source + 1] for item in whole)
        rows.append(jnp.where(member == 0, first, jnp.where(member == 1, both, last)))
    return rows


HOPS = (0, 1, 2, 3, -1, -2, -3)
PIECES = 2 * len(HOPS) + 2


def project_kernel(where, ret, *refs):
    weights, (vis_out, txt_out, slots, held, sems) = refs[:PIECES], refs[PIECES:]
    y, core = where[0], where[2]
    sign = 1 - 2 * core
    half_rows = TRIO // 2
    copies = []
    for index in range(PIECES):
        chunk, half = index // 2, index % 2
        if chunk == len(HOPS):
            half = core if half == 0 else 1 - core
        start = chunk % 2 * TRIO + half * half_rows
        to = held.at[chunk // 2, pl.ds(pl.multiple_of(start, 64), half_rows)]
        copies.append(pltpu.make_async_copy(weights[index], to, sems.at[index]))
    for copy in copies:
        copy.start()
    for slot in range(SLOTS):
        valid = where[5 + slot] > 0
        for source, row in enumerate(slot_of(ret, where[3 + slot])):
            row = jnp.where(valid, row, 0.0)
            at = source * VIS_ROWS
            slots[slot : slot + 1, at : at + VIS_ROWS] = row[:, :VIS_ROWS]
            at = VIS_SEQ + source * TXT_ROWS
            slots[slot : slot + 1, at : at + TXT_ROWS] = row[:, VIS_ROWS:]
    total = jnp.zeros((ROWS, held.shape[2]), jnp.float32)
    pieces = []
    for index, hops in enumerate((*HOPS, 4)):
        chip = (y - hops * sign + Y_SIZE) % Y_SIZE
        low, high = ret[2 * chip], ret[2 * chip + 1]
        shared = jnp.concatenate([low[ROWS:RET_ROWS], high[ROWS:RET_ROWS]], axis=0)
        attention = jnp.concatenate([low[:ROWS], shared, high[:ROWS]], axis=1)
        txt_out[:, pl.ds(pl.multiple_of(chip * TRIO, TRIO), TRIO)] = attention[VIS_ROWS:]
        pieces.append(attention)
        copies[2 * index].wait()
        copies[2 * index + 1].wait()
        if index % 2 == 1:
            both = jnp.concatenate(pieces[-2:], axis=1)
            total += jnp.dot(both, held[index // 2], preferred_element_type=jnp.float32)
    vis_out[...] = total[:VIS_ROWS].astype(jnp.bfloat16)


def project(where, returned, weights):
    columns = weights[0].shape[1]
    return pl.pallas_call(
        project_kernel,
        grid_spec=pltpu.PrefetchScalarGridSpec(
            num_scalar_prefetch=1,
            grid=(),
            in_specs=[pl.BlockSpec(memory_space=pltpu.VMEM)] + [pl.BlockSpec(memory_space=pltpu.HBM)] * PIECES,
            out_specs=[pl.BlockSpec(memory_space=pltpu.VMEM)] * 3,
            scratch_shapes=[
                pltpu.VMEM((Y_SIZE // 2, 2 * TRIO, columns), jnp.bfloat16),
                pltpu.SemaphoreType.DMA((PIECES,)),
            ],
        ),
        out_shape=[
            jax.ShapeDtypeStruct((VIS_ROWS, columns), jnp.bfloat16),
            jax.ShapeDtypeStruct((TXT_ROWS, HEADS * HEAD_DIM), jnp.bfloat16),
            jax.ShapeDtypeStruct((SLOTS, VIS_SEQ + TXT_SEQ), jnp.float32),
        ],
        compiler_params=pltpu.CompilerParams(vmem_limit_bytes=PROJECT_VMEM),
        name="project",
    )(where, returned, *weights)


AXES = ("dp", "seq")
X_SIZE = 4
Y_SIZE = 8


def permute(operand, target, cores=(0, 1)):
    pairs = []
    for y in range(Y_SIZE):
        for x in range(X_SIZE):
            for s in range(N_SEQ):
                ty, tx, ts = target(y, x, s)
                there = (ty % Y_SIZE) * X_SIZE + tx % X_SIZE
                if s % 2 in cores:
                    pairs.append(((y * X_SIZE + x) * N_SEQ + s, there * N_SEQ + ts))
    return lax.ppermute(operand, AXES, pairs)


def swap(operand, cores=(0, 1)):
    return permute(operand, lambda y, x, s: (y, x, s ^ 1), cores)


def shift_x(operand, hops, cores=(0, 1)):
    return permute(operand, lambda y, x, s: (y, x + hops * (1 - 2 * (s % 2)), s), cores)


def shift_y(operand):
    return permute(operand, lambda y, x, s: (y + 1 - 2 * (s % 2), x, s))


def heads_of_slots(head_map, seq_index):
    mine = (head_map == seq_index).astype(jnp.int32)
    rank = jnp.cumsum(mine) - 1
    ids = jnp.arange(HEADS, dtype=jnp.int32)
    picked = mine[None] * (rank[None] == jnp.arange(SLOTS, dtype=jnp.int32)[:, None])
    return jnp.concatenate([jnp.sum(picked * ids[None], axis=1), jnp.sum(picked, axis=1)])


def on_device(qkv_vis, qkv_txt, vis_segments, txt_segments, head_map, w_out):
    seq_index = lax.axis_index("seq")
    dp_index = lax.axis_index("dp")
    core = seq_index % 2
    place_here = jnp.stack([dp_index // X_SIZE, dp_index % X_SIZE, core]).astype(jnp.int32)
    where = jnp.concatenate([place_here, heads_of_slots(head_map, seq_index)])

    near = shift_x(w_out, 1)
    part = shift_x(w_out, 2, cores=(0,))
    sending = pack(qkv_vis, qkv_txt, vis_segments, txt_segments)
    received = lax.all_to_all(sending, "seq", split_axis=0, concat_axis=0, tiled=True)
    halves = place(where, w_out, near, swap(near), part, swap(part, cores=(0,)))
    chunks = [[half.reshape(-1, half.shape[2]) for half in halves]]
    for _ in range(3):
        chunks.append([shift_y(half) for half in chunks[-1]])
    own_kv = received[:, A_ROWS + HALF : SEND_ROWS]
    far_kv = swap(own_kv)
    whole, whole_lse = attend_whole(received)
    returning = attend_shared(where, received, own_kv, far_kv, whole, whole_lse)
    returning, chunks[1:] = lax.optimization_barrier((returning, chunks[1:]))
    returned = lax.all_to_all(returning, "seq", split_axis=0, concat_axis=0, tiled=True)
    opposite = shift_y(jnp.where(core == 0, *chunks[3]))
    far_chunks = [[swap(half) for half in chunk] for chunk in chunks[1:]]
    weights = [half for chunk in chunks + far_chunks for half in chunk] + [opposite, swap(opposite)]
    vis_out, txt_out, lse_slots = project(where, returned, weights)
    return vis_out, txt_out, lse_slots


def solution(mesh):
    in_specs = (
        P(("dp", "seq"), None),
        P(("dp", "seq"), None),
        P(("dp", "seq")),
        P(("dp", "seq")),
        P(),
        P("dp", None),
    )
    out_specs = (P(("dp", "seq"), None), P(("dp", "seq"), None), P("seq", "dp"))
    return jax.shard_map(
        on_device, mesh=mesh, in_specs=in_specs, out_specs=out_specs, check_vma=False
    )
```

```python
import functools

import jax
import jax.numpy as jnp
from jax import lax
from jax.experimental import pallas as pl
from jax.experimental.pallas import tpu as pltpu
from jax.sharding import PartitionSpec as P

HEADS = 24
HEAD_DIM = 128
N_SEQ = 16
VIS_ROWS = 112
TXT_ROWS = 16
ROWS = VIS_ROWS + TXT_ROWS
HALF = ROWS // 2
TRIO = 3 * HEAD_DIM
CHIPS = 8
A_ROWS = 3 * ROWS
SEND_ROWS = A_ROWS + 3 * HALF
CUT_ROWS = 8
PAYLOAD = SEND_ROWS + CUT_ROWS
RET_ROWS = ROWS + HALF
WHOLE_LSE = RET_ROWS
SHARED_LSE = WHOLE_LSE + N_SEQ
RETURN = SHARED_LSE + N_SEQ
PACK_CHIPS = 4
VIS_SEQ = VIS_ROWS * N_SEQ
TXT_SEQ = TXT_ROWS * N_SEQ
SLOTS = 2
LOG2E = 1.4426950408889634
LN2 = 0.6931471805599453
BIG = -1e30


def pack_kernel(seg_vis, seg_txt, vq, vk, vv, tq, tk, tv, out):
    def even(ref):
        parity = (ref[...] & 1).astype(jnp.float32)
        count = jnp.sum(1.0 - parity, axis=1, keepdims=True)
        return jnp.broadcast_to(count, (CUT_ROWS // 2, HEAD_DIM))

    cuts = jnp.concatenate([even(seg_vis), even(seg_txt)], axis=0).astype(jnp.bfloat16)
    for chip in range(PACK_CHIPS):
        low, high = 2 * chip, 2 * chip + 1
        for part, (vis, txt) in enumerate(((vq, tq), (vk, tk), (vv, tv))):
            row = part * ROWS
            for device, column in ((low, chip * TRIO), (high, chip * TRIO + 2 * HEAD_DIM)):
                columns = slice(column, column + HEAD_DIM)
                out[device, row : row + VIS_ROWS, :] = vis[:, columns]
                out[device, row + VIS_ROWS : row + ROWS, :] = txt[:, columns]
            row = A_ROWS + part * HALF
            columns = slice(chip * TRIO + HEAD_DIM, chip * TRIO + 2 * HEAD_DIM)
            out[low, row : row + HALF, :] = vis[:HALF, columns]
            out[high, row : row + VIS_ROWS - HALF, :] = vis[HALF:, columns]
            out[high, row + VIS_ROWS - HALF : row + HALF, :] = txt[:, columns]
        out[low, SEND_ROWS:PAYLOAD, :] = cuts
        out[high, SEND_ROWS:PAYLOAD, :] = cuts


def pack(qkv_vis, qkv_txt, vis_segments, txt_segments):
    steps = CHIPS // PACK_CHIPS

    def spec(rows, part):
        return pl.BlockSpec((rows, PACK_CHIPS * TRIO), lambda i: (0, part * steps + i))

    return pl.pallas_call(
        pack_kernel,
        grid=(steps,),
        in_specs=[
            pl.BlockSpec((1, VIS_ROWS), lambda i: (0, 0)),
            pl.BlockSpec((1, TXT_ROWS), lambda i: (0, 0)),
            *[spec(VIS_ROWS, part) for part in range(3)],
            *[spec(TXT_ROWS, part) for part in range(3)],
        ],
        out_specs=pl.BlockSpec((2 * PACK_CHIPS, PAYLOAD, HEAD_DIM), lambda i: (i, 0, 0)),
        out_shape=jax.ShapeDtypeStruct((N_SEQ, PAYLOAD, HEAD_DIM), jnp.bfloat16),
        name="pack",
    )(
        vis_segments.reshape(1, VIS_ROWS),
        txt_segments.reshape(1, TXT_ROWS),
        *[qkv_vis] * 3,
        *[qkv_txt] * 3,
    )


def clip_features(cut, first_source, count, rows, offset, value, second_lane):
    cuts = jnp.sum(cut[...].astype(jnp.float32), axis=0)
    vis_cut, txt_cut = cuts[0:1], cuts[CUT_ROWS // 2 : CUT_ROWS // 2 + 1]
    row = lax.broadcasted_iota(jnp.int32, (rows, HEAD_DIM), 0) + offset
    is_vis, row = row < VIS_ROWS, row.astype(jnp.float32)
    behind = jnp.where(is_vis, row - vis_cut, row - VIS_ROWS - txt_cut)
    stride = jnp.where(is_vis, float(VIS_ROWS), float(TXT_ROWS))
    lane = lax.broadcasted_iota(jnp.int32, (1, HEAD_DIM), 1)
    second = jnp.where(lane == second_lane, value, 0.0)
    first = jnp.where(lane == 1 - second_lane, value, 0.0)
    behind = behind + stride * first_source
    pieces = []
    for _ in range(count):
        pieces.append(jnp.where(behind >= 0.0, second, first).astype(jnp.bfloat16))
        behind = behind + stride
    return jnp.concatenate(pieces, axis=0)


def attend(queries, k_wide, v_turned, write):
    factor = HEAD_DIM**-0.5 * LOG2E

    def score(block):
        return lax.dot_general(
            k_wide[...], queries(block), (((1,), (1,)), ((), ())), preferred_element_type=jnp.float32
        )

    blocks = STEP_ROWS // Q_ROWS
    scores = score(0)
    for block in range(blocks):
        upcoming = score(block + 1) if block + 1 < blocks else None
        highest = jnp.max(scores, axis=0, keepdims=True)
        exponent = jnp.exp2((scores - highest) * factor)
        total = jnp.sum(exponent, axis=0, keepdims=True)
        blended = jnp.dot(
            v_turned[...], exponent.astype(jnp.bfloat16), preferred_element_type=jnp.float32
        )
        result = jnp.swapaxes(blended * (1.0 / total), 0, 1).astype(jnp.bfloat16)
        write(block, result, highest * HEAD_DIM**-0.5 + jnp.log2(total) * LN2)
        scores = upcoming


def key_features(cut, rows, offset):
    return clip_features(cut, 0.0, N_SEQ, rows, offset, BIG, 0)


def query_features(cut, first_source, rows, offset):
    return clip_features(cut, first_source, STEP_ROWS // rows, rows, offset, 1.0, 1)


def whole_kernel(cut, q, k, v, out, lse, k_wide, v_turned, q_wide):
    step = pl.program_id(0)
    keys = N_SEQ * ROWS
    sources = STEP_ROWS // ROWS

    @pl.when(step == 0)
    def _():
        k_wide[:, :HEAD_DIM] = k[...].reshape(keys, HEAD_DIM)
        k_wide[:, HEAD_DIM:] = key_features(cut, ROWS, 0)
        v_turned[...] = jnp.swapaxes(v[...].reshape(keys, HEAD_DIM), 0, 1)

    q_wide[:, :HEAD_DIM] = q[...].reshape(STEP_ROWS, HEAD_DIM)
    q_wide[:, HEAD_DIM:] = query_features(cut, (step * sources).astype(jnp.float32), ROWS, 0)

    def write(block, result, log_total):
        count = Q_ROWS // ROWS
        out[block * count : (block + 1) * count] = result.reshape(count, ROWS, HEAD_DIM)
        for row in range(count):
            lse[block * count + row : block * count + row + 1, :] = log_total[
                :, row * HEAD_DIM : (row + 1) * HEAD_DIM
            ]

    attend(lambda block: q_wide[block * Q_ROWS : (block + 1) * Q_ROWS, :], k_wide, v_turned, write)


def shared_kernel(where, cut, q, own_kv, far_kv, whole, whole_lse, out, k_wide, v_turned, q_wide):
    core = where[2]
    keys = N_SEQ * HALF
    for place, (kv, offset) in enumerate(((own_kv, HALF * core), (far_kv, HALF * (1 - core)))):
        at = slice(place * keys, (place + 1) * keys)
        k_wide[at, :HEAD_DIM] = kv[:, :HALF].reshape(keys, HEAD_DIM)
        k_wide[at, HEAD_DIM:] = key_features(cut, HALF, offset)
        v_turned[:, at] = jnp.swapaxes(kv[:, HALF:].reshape(keys, HEAD_DIM), 0, 1)
    q_wide[:, :HEAD_DIM] = q[...].reshape(STEP_ROWS, HEAD_DIM)
    q_wide[:, HEAD_DIM:] = query_features(cut, 0.0, HALF, HALF * core)
    log_totals = []

    def write(block, result, log_total):
        count = Q_ROWS // HALF
        out[block * count : (block + 1) * count, ROWS:RET_ROWS, :] = result.reshape(count, HALF, HEAD_DIM)
        for row in range(Q_ROWS // HEAD_DIM):
            log_totals.append(log_total[:, row * HEAD_DIM : (row + 1) * HEAD_DIM])

    attend(lambda block: q_wide[block * Q_ROWS : (block + 1) * Q_ROWS, :], k_wide, v_turned, write)
    out[:, :ROWS, :] = whole[...]
    log_totals.append(jnp.zeros((RETURN - SHARED_LSE - len(log_totals), HEAD_DIM), jnp.float32))
    rows = jnp.concatenate([whole_lse[...], *log_totals], axis=0).astype(jnp.bfloat16)
    for device in range(N_SEQ):
        out[device, WHOLE_LSE:, :] = rows


Q_ROWS = 512
STEP_ROWS = 1024
VMEM = 32 * 2**20
PLACE_VMEM = 60 * 2**20
JOIN_VMEM = 60 * 2**20
PROJECT_VMEM = 50 * 2**20


def attention_scratch():
    keys = N_SEQ * ROWS
    return [
        pltpu.VMEM((keys, 2 * HEAD_DIM), jnp.bfloat16),
        pltpu.VMEM((HEAD_DIM, keys), jnp.bfloat16),
        pltpu.VMEM((STEP_ROWS, 2 * HEAD_DIM), jnp.bfloat16),
    ]


def attention_cost(queries, keys):
    return pl.CostEstimate(
        flops=queries * keys * HEAD_DIM // 4,
        bytes_accessed=4 * keys * HEAD_DIM * 2,
        transcendentals=0,
    )


def attend_whole(received):
    keys = N_SEQ * ROWS
    steps = keys // STEP_ROWS
    sources = STEP_ROWS // ROWS
    return pl.pallas_call(
        whole_kernel,
        grid=(steps,),
        in_specs=[
            pl.BlockSpec((N_SEQ, CUT_ROWS, HEAD_DIM), lambda i: (0, SEND_ROWS // CUT_ROWS, 0)),
            pl.BlockSpec((sources, ROWS, HEAD_DIM), lambda i: (i, 0, 0)),
            pl.BlockSpec((N_SEQ, ROWS, HEAD_DIM), lambda i: (0, 1, 0)),
            pl.BlockSpec((N_SEQ, ROWS, HEAD_DIM), lambda i: (0, 2, 0)),
        ],
        out_specs=[
            pl.BlockSpec((sources, ROWS, HEAD_DIM), lambda i: (i, 0, 0)),
            pl.BlockSpec((sources, ROWS), lambda i: (i, 0)),
        ],
        out_shape=[
            jax.ShapeDtypeStruct((N_SEQ, ROWS, HEAD_DIM), jnp.bfloat16),
            jax.ShapeDtypeStruct((N_SEQ, ROWS), jnp.float32),
        ],
        scratch_shapes=attention_scratch(),
        compiler_params=pltpu.CompilerParams(vmem_limit_bytes=VMEM),
        cost_estimate=attention_cost(keys, keys),
        name="attend_whole",
    )(*[received] * 4)


def attend_shared(where, received, own_kv, far_kv, whole, whole_lse):
    keys = N_SEQ * ROWS
    full = lambda *shape: pl.BlockSpec(shape, lambda i, c: (0,) * len(shape))
    return pl.pallas_call(
        shared_kernel,
        grid_spec=pltpu.PrefetchScalarGridSpec(
            num_scalar_prefetch=1,
            grid=(1,),
            in_specs=[
                pl.BlockSpec((N_SEQ, CUT_ROWS, HEAD_DIM), lambda i, c: (0, SEND_ROWS // CUT_ROWS, 0)),
                pl.BlockSpec((N_SEQ, HALF, HEAD_DIM), lambda i, c: (0, A_ROWS // HALF, 0)),
                full(N_SEQ, 2 * HALF, HEAD_DIM),
                full(N_SEQ, 2 * HALF, HEAD_DIM),
                full(N_SEQ, ROWS, HEAD_DIM),
                full(N_SEQ, ROWS),
            ],
            out_specs=full(N_SEQ, RETURN, HEAD_DIM),
            scratch_shapes=attention_scratch(),
        ),
        out_shape=jax.ShapeDtypeStruct((N_SEQ, RETURN, HEAD_DIM), jnp.bfloat16),
        compiler_params=pltpu.CompilerParams(vmem_limit_bytes=VMEM),
        cost_estimate=attention_cost(keys // 2, keys),
        name="attend_shared",
    )(where, received, received, own_kv, far_kv, whole, whole_lse)


def place_kernel(where, mine, near, near_far, part, part_far, *halves):
    x, core = where[1], where[2]
    sign = 1 - 2 * core

    def put(to, shard):
        to = (to + X_SIZE) % X_SIZE
        for half, out in enumerate(halves):

            @pl.when(to // 2 == half)
            def _():
                out[to % 2] = shard[...]

    put(x, mine)
    put(x - sign, near)
    put(x + sign, near_far)

    @pl.when(core == 0)
    def _():
        put(x + 2, part)

    @pl.when(core == 1)
    def _():
        put(x + 2, part_far)


def place(where, mine, near, near_far, part, part_far):
    rows, columns = mine.shape
    return pl.pallas_call(
        place_kernel,
        grid_spec=pltpu.PrefetchScalarGridSpec(
            num_scalar_prefetch=1,
            grid=(),
            in_specs=[pl.BlockSpec(memory_space=pltpu.VMEM)] * 5,
            out_specs=[pl.BlockSpec(memory_space=pltpu.VMEM)] * 2,
        ),
        out_shape=[jax.ShapeDtypeStruct((2, rows, columns), jnp.bfloat16)] * 2,
        compiler_params=pltpu.CompilerParams(vmem_limit_bytes=PLACE_VMEM),
        name="place",
    )(where, mine, near, near_far, part, part_far)


def join_kernel(*refs):
    halves, wholes, (held, in_sems, out_sems) = refs[:6], refs[6:9], refs[9:]
    rows = halves[0].shape[0]
    loads = [
        pltpu.make_async_copy(half, held.at[index // 2, pl.ds(index % 2 * rows, rows)], in_sems.at[index])
        for index, half in enumerate(halves)
    ]
    for load in loads:
        load.start()
    stores = []
    for index, whole in enumerate(wholes):
        loads[2 * index].wait()
        loads[2 * index + 1].wait()
        stores.append(pltpu.make_async_copy(held.at[index], whole, out_sems.at[index]))
        stores[-1].start()
    for store in stores:
        store.wait()


def join(chunks):
    rows, columns = chunks[0][0].shape
    return pl.pallas_call(
        join_kernel,
        in_specs=[pl.BlockSpec(memory_space=pl.ANY)] * 6,
        out_specs=[pl.BlockSpec(memory_space=pl.ANY)] * 3,
        out_shape=[jax.ShapeDtypeStruct((2 * rows, columns), jnp.bfloat16)] * 3,
        scratch_shapes=[
            pltpu.VMEM((3, 2 * rows, columns), jnp.bfloat16),
            pltpu.SemaphoreType.DMA((6,)),
            pltpu.SemaphoreType.DMA((3,)),
        ],
        compiler_params=pltpu.CompilerParams(vmem_limit_bytes=JOIN_VMEM),
        name="join",
    )(*[half for chunk in chunks for half in chunk])


def slot_of(ret, head):
    chip, member = head // 3, head % 3
    low, high = ret.at[2 * chip], ret.at[2 * chip + 1]
    lane = lax.broadcasted_iota(jnp.int32, (1, HEAD_DIM), 1)
    rows = []
    for source in range(N_SEQ):
        whole = [ref[WHOLE_LSE : WHOLE_LSE + N_SEQ, :].astype(jnp.float32) for ref in (low, high)]
        shared = [ref[SHARED_LSE : SHARED_LSE + N_SEQ, :].astype(jnp.float32) for ref in (low, high)]
        left, right = (item[source // 2 : source // 2 + 1] for item in shared)
        if source % 2 == 0:
            right = pltpu.roll(right, HALF, 1)
        else:
            left = pltpu.roll(left, HALF, 1)
        both = jnp.where(lane < HALF, left, right)
        first, last = (item[source : source + 1] for item in whole)
        rows.append(jnp.where(member == 0, first, jnp.where(member == 1, both, last)))
    return rows


HOPS = (0, 1, 2, 3, -1, -2, -3)
PIECES = 2 + 6 + 2


def project_kernel(where, ret, *refs):
    weights, (vis_out, txt_out, slots, held, sems) = refs[:PIECES], refs[PIECES:]
    y, core = where[0], where[2]
    sign = 1 - 2 * core
    places = [(0, 0, 1), (0, 1, 1)] + [(chunk, 0, 2) for chunk in range(1, 7)] + [(7, core, 1), (7, 1 - core, 1)]
    copies = []
    for index, (chunk, half, count) in enumerate(places):
        start = chunk % 2 * TRIO + half * (TRIO // 2)
        to = held.at[chunk // 2, pl.ds(pl.multiple_of(start, 64), count * (TRIO // 2))]
        copies.append(pltpu.make_async_copy(weights[index], to, sems.at[index]))
    for copy in copies:
        copy.start()
    arrivals = [copies[:2]] + [[copy] for copy in copies[2:8]] + [copies[8:]]
    for slot in range(SLOTS):
        valid = where[5 + slot] > 0
        for source, row in enumerate(slot_of(ret, where[3 + slot])):
            row = jnp.where(valid, row, 0.0)
            at = source * VIS_ROWS
            slots[slot : slot + 1, at : at + VIS_ROWS] = row[:, :VIS_ROWS]
            at = VIS_SEQ + source * TXT_ROWS
            slots[slot : slot + 1, at : at + TXT_ROWS] = row[:, VIS_ROWS:]
    total = jnp.zeros((ROWS, held.shape[2]), jnp.float32)
    pieces = []
    for index, hops in enumerate((*HOPS, 4)):
        chip = (y - hops * sign + Y_SIZE) % Y_SIZE
        low, high = ret[2 * chip], ret[2 * chip + 1]
        shared = jnp.concatenate([low[ROWS:RET_ROWS], high[ROWS:RET_ROWS]], axis=0)
        attention = jnp.concatenate([low[:ROWS], shared, high[:ROWS]], axis=1)
        txt_out[:, pl.ds(pl.multiple_of(chip * TRIO, TRIO), TRIO)] = attention[VIS_ROWS:]
        pieces.append(attention)
        for copy in arrivals[index]:
            copy.wait()
        if index % 2 == 1:
            both = jnp.concatenate(pieces[-2:], axis=1)
            total += jnp.dot(both, held[index // 2], preferred_element_type=jnp.float32)
    vis_out[...] = total[:VIS_ROWS].astype(jnp.bfloat16)


def project(where, returned, weights):
    columns = weights[0].shape[1]
    return pl.pallas_call(
        project_kernel,
        grid_spec=pltpu.PrefetchScalarGridSpec(
            num_scalar_prefetch=1,
            grid=(),
            in_specs=[pl.BlockSpec(memory_space=pltpu.VMEM)] + [pl.BlockSpec(memory_space=pltpu.HBM)] * PIECES,
            out_specs=[pl.BlockSpec(memory_space=pltpu.VMEM)] * 3,
            scratch_shapes=[
                pltpu.VMEM((Y_SIZE // 2, 2 * TRIO, columns), jnp.bfloat16),
                pltpu.SemaphoreType.DMA((PIECES,)),
            ],
        ),
        out_shape=[
            jax.ShapeDtypeStruct((VIS_ROWS, columns), jnp.bfloat16),
            jax.ShapeDtypeStruct((TXT_ROWS, HEADS * HEAD_DIM), jnp.bfloat16),
            jax.ShapeDtypeStruct((SLOTS, VIS_SEQ + TXT_SEQ), jnp.float32),
        ],
        compiler_params=pltpu.CompilerParams(vmem_limit_bytes=PROJECT_VMEM),
        name="project",
    )(where, returned, *weights)


AXES = ("dp", "seq")
X_SIZE = 4
Y_SIZE = 8


def permute(operand, target, cores=(0, 1)):
    pairs = []
    for y in range(Y_SIZE):
        for x in range(X_SIZE):
            for s in range(N_SEQ):
                ty, tx, ts = target(y, x, s)
                there = (ty % Y_SIZE) * X_SIZE + tx % X_SIZE
                if s % 2 in cores:
                    pairs.append(((y * X_SIZE + x) * N_SEQ + s, there * N_SEQ + ts))
    return lax.ppermute(operand, AXES, pairs)


def swap(operand, cores=(0, 1)):
    return permute(operand, lambda y, x, s: (y, x, s ^ 1), cores)


def shift_x(operand, hops, cores=(0, 1)):
    return permute(operand, lambda y, x, s: (y, x + hops * (1 - 2 * (s % 2)), s), cores)


def shift_y(operand):
    return permute(operand, lambda y, x, s: (y + 1 - 2 * (s % 2), x, s))


def heads_of_slots(head_map, seq_index):
    mine = (head_map == seq_index).astype(jnp.int32)
    rank = jnp.cumsum(mine) - 1
    ids = jnp.arange(HEADS, dtype=jnp.int32)
    picked = mine[None] * (rank[None] == jnp.arange(SLOTS, dtype=jnp.int32)[:, None])
    return jnp.concatenate([jnp.sum(picked * ids[None], axis=1), jnp.sum(picked, axis=1)])


def on_device(qkv_vis, qkv_txt, vis_segments, txt_segments, head_map, w_out):
    seq_index = lax.axis_index("seq")
    dp_index = lax.axis_index("dp")
    core = seq_index % 2
    place_here = jnp.stack([dp_index // X_SIZE, dp_index % X_SIZE, core]).astype(jnp.int32)
    where = jnp.concatenate([place_here, heads_of_slots(head_map, seq_index)])

    near = shift_x(w_out, 1)
    part = shift_x(w_out, 2, cores=(0,))
    sending = pack(qkv_vis, qkv_txt, vis_segments, txt_segments)
    received = lax.all_to_all(sending, "seq", split_axis=0, concat_axis=0, tiled=True)
    halves = place(where, w_out, near, swap(near), part, swap(part, cores=(0,)))
    chunks = [[half.reshape(-1, half.shape[2]) for half in halves]]
    for _ in range(3):
        chunks.append([shift_y(half) for half in chunks[-1]])
    own_kv = received[:, A_ROWS + HALF : SEND_ROWS]
    far_kv = swap(own_kv)
    whole, whole_lse = attend_whole(received)
    returning = attend_shared(where, received, own_kv, far_kv, whole, whole_lse)
    returning, chunks[1:] = lax.optimization_barrier((returning, chunks[1:]))
    returned = lax.all_to_all(returning, "seq", split_axis=0, concat_axis=0, tiled=True)
    opposite = shift_y(jnp.where(core == 0, *chunks[3]))
    hops = join(chunks[1:])
    weights = [*chunks[0], *hops, *map(swap, hops), opposite, swap(opposite)]
    vis_out, txt_out, lse_slots = project(where, returned, weights)
    return vis_out, txt_out, lse_slots


def solution(mesh):
    in_specs = (
        P(("dp", "seq"), None),
        P(("dp", "seq"), None),
        P(("dp", "seq")),
        P(("dp", "seq")),
        P(),
        P("dp", None),
    )
    out_specs = (P(("dp", "seq"), None), P(("dp", "seq"), None), P("seq", "dp"))
    return jax.shard_map(
        on_device, mesh=mesh, in_specs=in_specs, out_specs=out_specs, check_vma=False
    )
```

```python
import functools

import jax
import jax.numpy as jnp
from jax import lax
from jax.experimental import pallas as pl
from jax.experimental.pallas import tpu as pltpu
from jax.sharding import PartitionSpec as P

HEADS = 24
HEAD_DIM = 128
N_SEQ = 16
VIS_ROWS = 112
TXT_ROWS = 16
ROWS = VIS_ROWS + TXT_ROWS
HALF = ROWS // 2
TRIO = 3 * HEAD_DIM
CHIPS = 8
A_ROWS = 3 * ROWS
SEND_ROWS = A_ROWS + 3 * HALF
CUT_ROWS = 8
PAYLOAD = SEND_ROWS + CUT_ROWS
RET_ROWS = ROWS + HALF
WHOLE_LSE = RET_ROWS
SHARED_LSE = WHOLE_LSE + N_SEQ
RETURN = SHARED_LSE + N_SEQ // 2
PACK_CHIPS = 4
VIS_SEQ = VIS_ROWS * N_SEQ
TXT_SEQ = TXT_ROWS * N_SEQ
SLOTS = 2
LOG2E = 1.4426950408889634
LN2 = 0.6931471805599453
BIG = -1e30


def pack_kernel(seg_vis, seg_txt, vq, vk, vv, tq, tk, tv, out):
    def even(ref):
        parity = (ref[...] & 1).astype(jnp.float32)
        count = jnp.sum(1.0 - parity, axis=1, keepdims=True)
        return jnp.broadcast_to(count, (CUT_ROWS // 2, HEAD_DIM))

    cuts = jnp.concatenate([even(seg_vis), even(seg_txt)], axis=0).astype(jnp.bfloat16)
    for chip in range(PACK_CHIPS):
        low, high = 2 * chip, 2 * chip + 1
        for part, (vis, txt) in enumerate(((vq, tq), (vk, tk), (vv, tv))):
            row = part * ROWS
            for device, column in ((low, chip * TRIO), (high, chip * TRIO + 2 * HEAD_DIM)):
                columns = slice(column, column + HEAD_DIM)
                out[device, row : row + VIS_ROWS, :] = vis[:, columns]
                out[device, row + VIS_ROWS : row + ROWS, :] = txt[:, columns]
            row = A_ROWS + part * HALF
            columns = slice(chip * TRIO + HEAD_DIM, chip * TRIO + 2 * HEAD_DIM)
            out[low, row : row + HALF, :] = vis[:HALF, columns]
            out[high, row : row + VIS_ROWS - HALF, :] = vis[HALF:, columns]
            out[high, row + VIS_ROWS - HALF : row + HALF, :] = txt[:, columns]
        out[low, SEND_ROWS:PAYLOAD, :] = cuts
        out[high, SEND_ROWS:PAYLOAD, :] = cuts


def pack(qkv_vis, qkv_txt, vis_segments, txt_segments):
    steps = CHIPS // PACK_CHIPS

    def spec(rows, part):
        return pl.BlockSpec((rows, PACK_CHIPS * TRIO), lambda i: (0, part * steps + i))

    return pl.pallas_call(
        pack_kernel,
        grid=(steps,),
        in_specs=[
            pl.BlockSpec((1, VIS_ROWS), lambda i: (0, 0)),
            pl.BlockSpec((1, TXT_ROWS), lambda i: (0, 0)),
            *[spec(VIS_ROWS, part) for part in range(3)],
            *[spec(TXT_ROWS, part) for part in range(3)],
        ],
        out_specs=pl.BlockSpec((2 * PACK_CHIPS, PAYLOAD, HEAD_DIM), lambda i: (i, 0, 0)),
        out_shape=jax.ShapeDtypeStruct((N_SEQ, PAYLOAD, HEAD_DIM), jnp.bfloat16),
        name="pack",
    )(
        vis_segments.reshape(1, VIS_ROWS),
        txt_segments.reshape(1, TXT_ROWS),
        *[qkv_vis] * 3,
        *[qkv_txt] * 3,
    )


def clip_features(cut, first_source, count, rows, offset, value, second_lane):
    cuts = jnp.sum(cut[...].astype(jnp.float32), axis=0)
    vis_cut, txt_cut = cuts[0:1], cuts[CUT_ROWS // 2 : CUT_ROWS // 2 + 1]
    row = lax.broadcasted_iota(jnp.int32, (rows, HEAD_DIM), 0) + offset
    is_vis, row = row < VIS_ROWS, row.astype(jnp.float32)
    behind = jnp.where(is_vis, row - vis_cut, row - VIS_ROWS - txt_cut)
    stride = jnp.where(is_vis, float(VIS_ROWS), float(TXT_ROWS))
    lane = lax.broadcasted_iota(jnp.int32, (1, HEAD_DIM), 1)
    second = jnp.where(lane == second_lane, value, 0.0)
    first = jnp.where(lane == 1 - second_lane, value, 0.0)
    behind = behind + stride * first_source
    pieces = []
    for _ in range(count):
        pieces.append(jnp.where(behind >= 0.0, second, first).astype(jnp.bfloat16))
        behind = behind + stride
    return jnp.concatenate(pieces, axis=0)


def attend(queries, k_wide, v_turned, write):
    factor = HEAD_DIM**-0.5 * LOG2E

    def score(block):
        return lax.dot_general(
            k_wide[...], queries(block), (((1,), (1,)), ((), ())), preferred_element_type=jnp.float32
        )

    blocks = STEP_ROWS // Q_ROWS
    scores = score(0)
    for block in range(blocks):
        upcoming = score(block + 1) if block + 1 < blocks else None
        highest = jnp.max(scores, axis=0, keepdims=True)
        exponent = jnp.exp2((scores - highest) * factor)
        total = jnp.sum(exponent, axis=0, keepdims=True)
        blended = jnp.dot(
            v_turned[...], exponent.astype(jnp.bfloat16), preferred_element_type=jnp.float32
        )
        result = jnp.swapaxes(blended * (1.0 / total), 0, 1).astype(jnp.bfloat16)
        write(block, result, highest * HEAD_DIM**-0.5 + jnp.log2(total) * LN2)
        scores = upcoming


def key_features(cut, rows, offset):
    return clip_features(cut, 0.0, N_SEQ, rows, offset, BIG, 0)


def query_features(cut, first_source, rows, offset):
    return clip_features(cut, first_source, STEP_ROWS // rows, rows, offset, 1.0, 1)


def whole_kernel(cut, q, k, v, out, lse, k_wide, v_turned, q_wide):
    step = pl.program_id(0)
    keys = N_SEQ * ROWS
    sources = STEP_ROWS // ROWS

    @pl.when(step == 0)
    def _():
        k_wide[:, :HEAD_DIM] = k[...].reshape(keys, HEAD_DIM)
        k_wide[:, HEAD_DIM:] = key_features(cut, ROWS, 0)
        v_turned[...] = jnp.swapaxes(v[...].reshape(keys, HEAD_DIM), 0, 1)

    q_wide[:, :HEAD_DIM] = q[...].reshape(STEP_ROWS, HEAD_DIM)
    q_wide[:, HEAD_DIM:] = query_features(cut, (step * sources).astype(jnp.float32), ROWS, 0)

    def write(block, result, log_total):
        count = Q_ROWS // ROWS
        out[block * count : (block + 1) * count] = result.reshape(count, ROWS, HEAD_DIM)
        for row in range(count):
            lse[block * count + row : block * count + row + 1, :] = log_total[
                :, row * HEAD_DIM : (row + 1) * HEAD_DIM
            ]

    attend(lambda block: q_wide[block * Q_ROWS : (block + 1) * Q_ROWS, :], k_wide, v_turned, write)


def shared_kernel(where, cut, q, own_kv, far_kv, whole, whole_lse, out, k_wide, v_turned, q_wide):
    core = where[2]
    keys = N_SEQ * HALF
    for place, (kv, offset) in enumerate(((own_kv, HALF * core), (far_kv, HALF * (1 - core)))):
        at = slice(place * keys, (place + 1) * keys)
        k_wide[at, :HEAD_DIM] = kv[:, :HALF].reshape(keys, HEAD_DIM)
        k_wide[at, HEAD_DIM:] = key_features(cut, HALF, offset)
        v_turned[:, at] = jnp.swapaxes(kv[:, HALF:].reshape(keys, HEAD_DIM), 0, 1)
    q_wide[:, :HEAD_DIM] = q[...].reshape(STEP_ROWS, HEAD_DIM)
    q_wide[:, HEAD_DIM:] = query_features(cut, 0.0, HALF, HALF * core)
    log_totals = []

    def write(block, result, log_total):
        count = Q_ROWS // HALF
        out[block * count : (block + 1) * count, ROWS:RET_ROWS, :] = result.reshape(count, HALF, HEAD_DIM)
        for row in range(Q_ROWS // HEAD_DIM):
            log_totals.append(log_total[:, row * HEAD_DIM : (row + 1) * HEAD_DIM])

    attend(lambda block: q_wide[block * Q_ROWS : (block + 1) * Q_ROWS, :], k_wide, v_turned, write)
    out[:, :ROWS, :] = whole[...]
    rows = jnp.concatenate([whole_lse[...], *log_totals], axis=0).astype(jnp.bfloat16)
    for device in range(N_SEQ):
        out[device, WHOLE_LSE:, :] = rows


Q_ROWS = 512
STEP_ROWS = 1024
VMEM = 32 * 2**20
PLACE_VMEM = 60 * 2**20
JOIN_VMEM = 60 * 2**20
PROJECT_VMEM = 50 * 2**20


def attention_scratch():
    keys = N_SEQ * ROWS
    return [
        pltpu.VMEM((keys, 2 * HEAD_DIM), jnp.bfloat16),
        pltpu.VMEM((HEAD_DIM, keys), jnp.bfloat16),
        pltpu.VMEM((STEP_ROWS, 2 * HEAD_DIM), jnp.bfloat16),
    ]


def attention_cost(queries, keys):
    return pl.CostEstimate(
        flops=queries * keys * HEAD_DIM // 4,
        bytes_accessed=4 * keys * HEAD_DIM * 2,
        transcendentals=0,
    )


def attend_whole(received):
    keys = N_SEQ * ROWS
    steps = keys // STEP_ROWS
    sources = STEP_ROWS // ROWS
    return pl.pallas_call(
        whole_kernel,
        grid=(steps,),
        in_specs=[
            pl.BlockSpec((N_SEQ, CUT_ROWS, HEAD_DIM), lambda i: (0, SEND_ROWS // CUT_ROWS, 0)),
            pl.BlockSpec((sources, ROWS, HEAD_DIM), lambda i: (i, 0, 0)),
            pl.BlockSpec((N_SEQ, ROWS, HEAD_DIM), lambda i: (0, 1, 0)),
            pl.BlockSpec((N_SEQ, ROWS, HEAD_DIM), lambda i: (0, 2, 0)),
        ],
        out_specs=[
            pl.BlockSpec((sources, ROWS, HEAD_DIM), lambda i: (i, 0, 0)),
            pl.BlockSpec((sources, ROWS), lambda i: (i, 0)),
        ],
        out_shape=[
            jax.ShapeDtypeStruct((N_SEQ, ROWS, HEAD_DIM), jnp.bfloat16),
            jax.ShapeDtypeStruct((N_SEQ, ROWS), jnp.float32),
        ],
        scratch_shapes=attention_scratch(),
        compiler_params=pltpu.CompilerParams(vmem_limit_bytes=VMEM),
        cost_estimate=attention_cost(keys, keys),
        name="attend_whole",
    )(*[received] * 4)


def attend_shared(where, received, own_kv, far_kv, whole, whole_lse):
    keys = N_SEQ * ROWS
    full = lambda *shape: pl.BlockSpec(shape, lambda i, c: (0,) * len(shape))
    return pl.pallas_call(
        shared_kernel,
        grid_spec=pltpu.PrefetchScalarGridSpec(
            num_scalar_prefetch=1,
            grid=(1,),
            in_specs=[
                pl.BlockSpec((N_SEQ, CUT_ROWS, HEAD_DIM), lambda i, c: (0, SEND_ROWS // CUT_ROWS, 0)),
                pl.BlockSpec((N_SEQ, HALF, HEAD_DIM), lambda i, c: (0, A_ROWS // HALF, 0)),
                full(N_SEQ, 2 * HALF, HEAD_DIM),
                full(N_SEQ, 2 * HALF, HEAD_DIM),
                full(N_SEQ, ROWS, HEAD_DIM),
                full(N_SEQ, ROWS),
            ],
            out_specs=full(N_SEQ, RETURN, HEAD_DIM),
            scratch_shapes=attention_scratch(),
        ),
        out_shape=jax.ShapeDtypeStruct((N_SEQ, RETURN, HEAD_DIM), jnp.bfloat16),
        compiler_params=pltpu.CompilerParams(vmem_limit_bytes=VMEM),
        cost_estimate=attention_cost(keys // 2, keys),
        name="attend_shared",
    )(where, received, received, own_kv, far_kv, whole, whole_lse)


def place_kernel(where, mine, near, near_far, part, part_far, *halves):
    x, core = where[1], where[2]
    sign = 1 - 2 * core

    def put(to, shard):
        to = (to + X_SIZE) % X_SIZE
        for half, out in enumerate(halves):

            @pl.when(to // 2 == half)
            def _():
                out[to % 2] = shard[...]

    put(x, mine)
    put(x - sign, near)
    put(x + sign, near_far)

    @pl.when(core == 0)
    def _():
        put(x + 2, part)

    @pl.when(core == 1)
    def _():
        put(x + 2, part_far)


def place(where, mine, near, near_far, part, part_far):
    rows, columns = mine.shape
    return pl.pallas_call(
        place_kernel,
        grid_spec=pltpu.PrefetchScalarGridSpec(
            num_scalar_prefetch=1,
            grid=(),
            in_specs=[pl.BlockSpec(memory_space=pltpu.VMEM)] * 5,
            out_specs=[pl.BlockSpec(memory_space=pltpu.VMEM)] * 2,
        ),
        out_shape=[jax.ShapeDtypeStruct((2, rows, columns), jnp.bfloat16)] * 2,
        compiler_params=pltpu.CompilerParams(vmem_limit_bytes=PLACE_VMEM),
        name="place",
    )(where, mine, near, near_far, part, part_far)


def join_kernel(*refs):
    halves, wholes, (held, in_sems, out_sems) = refs[:6], refs[6:9], refs[9:]
    rows = halves[0].shape[0]
    loads = [
        pltpu.make_async_copy(half, held.at[index // 2, pl.ds(index % 2 * rows, rows)], in_sems.at[index])
        for index, half in enumerate(halves)
    ]
    for load in loads:
        load.start()
    stores = []
    for index, whole in enumerate(wholes):
        loads[2 * index].wait()
        loads[2 * index + 1].wait()
        stores.append(pltpu.make_async_copy(held.at[index], whole, out_sems.at[index]))
        stores[-1].start()
    for store in stores:
        store.wait()


def join(chunks):
    rows, columns = chunks[0][0].shape
    return pl.pallas_call(
        join_kernel,
        in_specs=[pl.BlockSpec(memory_space=pl.ANY)] * 6,
        out_specs=[pl.BlockSpec(memory_space=pl.ANY)] * 3,
        out_shape=[jax.ShapeDtypeStruct((2 * rows, columns), jnp.bfloat16)] * 3,
        scratch_shapes=[
            pltpu.VMEM((3, 2 * rows, columns), jnp.bfloat16),
            pltpu.SemaphoreType.DMA((6,)),
            pltpu.SemaphoreType.DMA((3,)),
        ],
        compiler_params=pltpu.CompilerParams(vmem_limit_bytes=JOIN_VMEM),
        name="join",
    )(*[half for chunk in chunks for half in chunk])


def slot_of(ret, head):
    chip, member = head // 3, head % 3
    low, high = ret.at[2 * chip], ret.at[2 * chip + 1]
    lane = lax.broadcasted_iota(jnp.int32, (1, HEAD_DIM), 1)
    rows = []
    for source in range(N_SEQ):
        whole = [ref[WHOLE_LSE : WHOLE_LSE + N_SEQ, :].astype(jnp.float32) for ref in (low, high)]
        shared = [ref[SHARED_LSE:RETURN, :].astype(jnp.float32) for ref in (low, high)]
        left, right = (item[source // 2 : source // 2 + 1] for item in shared)
        if source % 2 == 0:
            right = pltpu.roll(right, HALF, 1)
        else:
            left = pltpu.roll(left, HALF, 1)
        both = jnp.where(lane < HALF, left, right)
        first, last = (item[source : source + 1] for item in whole)
        rows.append(jnp.where(member == 0, first, jnp.where(member == 1, both, last)))
    return rows


HOPS = (0, 1, 2, 3, -1, -2, -3)
PIECES = 2 + 6 + 2


def project_kernel(where, ret, *refs):
    weights, (vis_out, txt_out, slots, held, sems) = refs[:PIECES], refs[PIECES:]
    y, core = where[0], where[2]
    sign = 1 - 2 * core
    places = [(0, 0, 1), (0, 1, 1)] + [(chunk, 0, 2) for chunk in range(1, 7)] + [(7, core, 1), (7, 1 - core, 1)]
    copies = []
    for index, (chunk, half, count) in enumerate(places):
        start = chunk % 2 * TRIO + half * (TRIO // 2)
        to = held.at[chunk // 2, pl.ds(pl.multiple_of(start, 64), count * (TRIO // 2))]
        copies.append(pltpu.make_async_copy(weights[index], to, sems.at[index]))
    for copy in copies:
        copy.start()
    arrivals = [copies[:2]] + [[copy] for copy in copies[2:8]] + [copies[8:]]
    for slot in range(SLOTS):
        valid = where[5 + slot] > 0
        for source, row in enumerate(slot_of(ret, where[3 + slot])):
            row = jnp.where(valid, row, 0.0)
            at = source * VIS_ROWS
            slots[slot : slot + 1, at : at + VIS_ROWS] = row[:, :VIS_ROWS]
            at = VIS_SEQ + source * TXT_ROWS
            slots[slot : slot + 1, at : at + TXT_ROWS] = row[:, VIS_ROWS:]
    total = jnp.zeros((ROWS, held.shape[2]), jnp.float32)
    pieces = []
    for index, hops in enumerate((*HOPS, 4)):
        chip = (y - hops * sign + Y_SIZE) % Y_SIZE
        low, high = ret[2 * chip], ret[2 * chip + 1]
        shared = jnp.concatenate([low[ROWS:RET_ROWS], high[ROWS:RET_ROWS]], axis=0)
        attention = jnp.concatenate([low[:ROWS], shared, high[:ROWS]], axis=1)
        txt_out[:, pl.ds(pl.multiple_of(chip * TRIO, TRIO), TRIO)] = attention[VIS_ROWS:]
        pieces.append(attention)
        for copy in arrivals[index]:
            copy.wait()
        if index % 2 == 1:
            both = jnp.concatenate(pieces[-2:], axis=1)
            total += jnp.dot(both, held[index // 2], preferred_element_type=jnp.float32)
    vis_out[...] = total[:VIS_ROWS].astype(jnp.bfloat16)


def project(where, returned, weights):
    columns = weights[0].shape[1]
    return pl.pallas_call(
        project_kernel,
        grid_spec=pltpu.PrefetchScalarGridSpec(
            num_scalar_prefetch=1,
            grid=(),
            in_specs=[pl.BlockSpec(memory_space=pltpu.VMEM)] + [pl.BlockSpec(memory_space=pltpu.HBM)] * PIECES,
            out_specs=[pl.BlockSpec(memory_space=pltpu.VMEM)] * 3,
            scratch_shapes=[
                pltpu.VMEM((Y_SIZE // 2, 2 * TRIO, columns), jnp.bfloat16),
                pltpu.SemaphoreType.DMA((PIECES,)),
            ],
        ),
        out_shape=[
            jax.ShapeDtypeStruct((VIS_ROWS, columns), jnp.bfloat16),
            jax.ShapeDtypeStruct((TXT_ROWS, HEADS * HEAD_DIM), jnp.bfloat16),
            jax.ShapeDtypeStruct((SLOTS, VIS_SEQ + TXT_SEQ), jnp.float32),
        ],
        compiler_params=pltpu.CompilerParams(vmem_limit_bytes=PROJECT_VMEM),
        name="project",
    )(where, returned, *weights)


AXES = ("dp", "seq")
X_SIZE = 4
Y_SIZE = 8


def permute(operand, target, cores=(0, 1)):
    pairs = []
    for y in range(Y_SIZE):
        for x in range(X_SIZE):
            for s in range(N_SEQ):
                ty, tx, ts = target(y, x, s)
                there = (ty % Y_SIZE) * X_SIZE + tx % X_SIZE
                if s % 2 in cores:
                    pairs.append(((y * X_SIZE + x) * N_SEQ + s, there * N_SEQ + ts))
    return lax.ppermute(operand, AXES, pairs)


def swap(operand, cores=(0, 1)):
    return permute(operand, lambda y, x, s: (y, x, s ^ 1), cores)


def shift_x(operand, hops, cores=(0, 1)):
    return permute(operand, lambda y, x, s: (y, x + hops * (1 - 2 * (s % 2)), s), cores)


def shift_y(operand):
    return permute(operand, lambda y, x, s: (y + 1 - 2 * (s % 2), x, s))


def heads_of_slots(head_map, seq_index):
    mine = (head_map == seq_index).astype(jnp.int32)
    rank = jnp.cumsum(mine) - 1
    ids = jnp.arange(HEADS, dtype=jnp.int32)
    picked = mine[None] * (rank[None] == jnp.arange(SLOTS, dtype=jnp.int32)[:, None])
    return jnp.concatenate([jnp.sum(picked * ids[None], axis=1), jnp.sum(picked, axis=1)])


def on_device(qkv_vis, qkv_txt, vis_segments, txt_segments, head_map, w_out):
    seq_index = lax.axis_index("seq")
    dp_index = lax.axis_index("dp")
    core = seq_index % 2
    place_here = jnp.stack([dp_index // X_SIZE, dp_index % X_SIZE, core]).astype(jnp.int32)
    where = jnp.concatenate([place_here, heads_of_slots(head_map, seq_index)])

    near = shift_x(w_out, 1)
    part = shift_x(w_out, 2, cores=(0,))
    sending = pack(qkv_vis, qkv_txt, vis_segments, txt_segments)
    received = lax.all_to_all(sending, "seq", split_axis=0, concat_axis=0, tiled=True)
    halves = place(where, w_out, near, swap(near), part, swap(part, cores=(0,)))
    chunks = [[half.reshape(-1, half.shape[2]) for half in halves]]
    for _ in range(3):
        chunks.append([shift_y(half) for half in chunks[-1]])
    own_kv = received[:, A_ROWS + HALF : SEND_ROWS]
    far_kv = swap(own_kv)
    whole, whole_lse = attend_whole(received)
    returning = attend_shared(where, received, own_kv, far_kv, whole, whole_lse)
    returning, chunks[1:] = lax.optimization_barrier((returning, chunks[1:]))
    returned = lax.all_to_all(returning, "seq", split_axis=0, concat_axis=0, tiled=True)
    opposite = shift_y(jnp.where(core == 0, *chunks[3]))
    hops = join(chunks[1:])
    weights = [*chunks[0], *hops, *map(swap, hops), opposite, swap(opposite)]
    vis_out, txt_out, lse_slots = project(where, returned, weights)
    return vis_out, txt_out, lse_slots


def solution(mesh):
    in_specs = (
        P(("dp", "seq"), None),
        P(("dp", "seq"), None),
        P(("dp", "seq")),
        P(("dp", "seq")),
        P(),
        P("dp", None),
    )
    out_specs = (P(("dp", "seq"), None), P(("dp", "seq"), None), P("seq", "dp"))
    return jax.shard_map(
        on_device, mesh=mesh, in_specs=in_specs, out_specs=out_specs, check_vma=False
    )
```

```python
import functools

import jax
import jax.numpy as jnp
from jax import lax
from jax.experimental import pallas as pl
from jax.experimental.pallas import tpu as pltpu
from jax.sharding import PartitionSpec as P

HEADS = 24
HEAD_DIM = 128
N_SEQ = 16
VIS_ROWS = 112
TXT_ROWS = 16
ROWS = VIS_ROWS + TXT_ROWS
HALF = ROWS // 2
TRIO = 3 * HEAD_DIM
CHIPS = 8
A_ROWS = 3 * ROWS
SEND_ROWS = A_ROWS + 3 * HALF
CUT_ROWS = 8
PAYLOAD = SEND_ROWS + CUT_ROWS
RET_ROWS = ROWS + HALF
WHOLE_LSE = RET_ROWS
SHARED_LSE = WHOLE_LSE + N_SEQ
RETURN = SHARED_LSE + N_SEQ // 2
PACK_CHIPS = 4
VIS_SEQ = VIS_ROWS * N_SEQ
TXT_SEQ = TXT_ROWS * N_SEQ
SLOTS = 2
LOG2E = 1.4426950408889634
LN2 = 0.6931471805599453
BIG = -1e30


def pack_kernel(seg_vis, seg_txt, vq, vk, vv, tq, tk, tv, out):
    def even(ref):
        parity = (ref[...] & 1).astype(jnp.float32)
        count = jnp.sum(1.0 - parity, axis=1, keepdims=True)
        return jnp.broadcast_to(count, (CUT_ROWS // 2, HEAD_DIM))

    cuts = jnp.concatenate([even(seg_vis), even(seg_txt)], axis=0).astype(jnp.bfloat16)
    for chip in range(PACK_CHIPS):
        low, high = 2 * chip, 2 * chip + 1
        for part, (vis, txt) in enumerate(((vq, tq), (vk, tk), (vv, tv))):
            row = part * ROWS
            for device, column in ((low, chip * TRIO), (high, chip * TRIO + 2 * HEAD_DIM)):
                columns = slice(column, column + HEAD_DIM)
                out[device, row : row + VIS_ROWS, :] = vis[:, columns]
                out[device, row + VIS_ROWS : row + ROWS, :] = txt[:, columns]
            row = A_ROWS + part * HALF
            columns = slice(chip * TRIO + HEAD_DIM, chip * TRIO + 2 * HEAD_DIM)
            out[low, row : row + HALF, :] = vis[:HALF, columns]
            out[high, row : row + VIS_ROWS - HALF, :] = vis[HALF:, columns]
            out[high, row + VIS_ROWS - HALF : row + HALF, :] = txt[:, columns]
        out[low, SEND_ROWS:PAYLOAD, :] = cuts
        out[high, SEND_ROWS:PAYLOAD, :] = cuts


def pack(qkv_vis, qkv_txt, vis_segments, txt_segments):
    steps = CHIPS // PACK_CHIPS

    def spec(rows, part):
        return pl.BlockSpec((rows, PACK_CHIPS * TRIO), lambda i: (0, part * steps + i))

    return pl.pallas_call(
        pack_kernel,
        grid=(steps,),
        in_specs=[
            pl.BlockSpec((1, VIS_ROWS), lambda i: (0, 0)),
            pl.BlockSpec((1, TXT_ROWS), lambda i: (0, 0)),
            *[spec(VIS_ROWS, part) for part in range(3)],
            *[spec(TXT_ROWS, part) for part in range(3)],
        ],
        out_specs=pl.BlockSpec((2 * PACK_CHIPS, PAYLOAD, HEAD_DIM), lambda i: (i, 0, 0)),
        out_shape=jax.ShapeDtypeStruct((N_SEQ, PAYLOAD, HEAD_DIM), jnp.bfloat16),
        name="pack",
    )(
        vis_segments.reshape(1, VIS_ROWS),
        txt_segments.reshape(1, TXT_ROWS),
        *[qkv_vis] * 3,
        *[qkv_txt] * 3,
    )


def clip_features(cut, first_source, count, rows, offset, value, second_lane):
    cuts = jnp.sum(cut[...].astype(jnp.float32), axis=0)
    vis_cut, txt_cut = cuts[0:1], cuts[CUT_ROWS // 2 : CUT_ROWS // 2 + 1]
    row = lax.broadcasted_iota(jnp.int32, (rows, HEAD_DIM), 0) + offset
    is_vis, row = row < VIS_ROWS, row.astype(jnp.float32)
    behind = jnp.where(is_vis, row - vis_cut, row - VIS_ROWS - txt_cut)
    stride = jnp.where(is_vis, float(VIS_ROWS), float(TXT_ROWS))
    lane = lax.broadcasted_iota(jnp.int32, (1, HEAD_DIM), 1)
    second = jnp.where(lane == second_lane, value, 0.0)
    first = jnp.where(lane == 1 - second_lane, value, 0.0)
    behind = behind + stride * first_source
    pieces = []
    for _ in range(count):
        pieces.append(jnp.where(behind >= 0.0, second, first).astype(jnp.bfloat16))
        behind = behind + stride
    return jnp.concatenate(pieces, axis=0)


def attend(queries, k_wide, v_turned, write):
    factor = HEAD_DIM**-0.5 * LOG2E

    def score(block):
        return lax.dot_general(
            k_wide[...], queries(block), (((1,), (1,)), ((), ())), preferred_element_type=jnp.float32
        )

    blocks = STEP_ROWS // Q_ROWS
    scores = score(0)
    for block in range(blocks):
        upcoming = score(block + 1) if block + 1 < blocks else None
        highest = jnp.max(scores, axis=0, keepdims=True)
        exponent = jnp.exp2((scores - highest) * factor)
        total = jnp.sum(exponent, axis=0, keepdims=True)
        blended = jnp.dot(
            v_turned[...], exponent.astype(jnp.bfloat16), preferred_element_type=jnp.float32
        )
        result = jnp.swapaxes(blended * (1.0 / total), 0, 1).astype(jnp.bfloat16)
        write(block, result, highest * HEAD_DIM**-0.5 + jnp.log2(total) * LN2)
        scores = upcoming


def key_features(cut, rows, offset):
    return clip_features(cut, 0.0, N_SEQ, rows, offset, BIG, 0)


def query_features(cut, first_source, rows, offset):
    return clip_features(cut, first_source, STEP_ROWS // rows, rows, offset, 1.0, 1)


def whole_kernel(cut, q, k, v, out, lse, k_wide, v_turned, q_wide):
    step = pl.program_id(0)
    keys = N_SEQ * ROWS
    sources = STEP_ROWS // ROWS

    @pl.when(step == 0)
    def _():
        k_wide[:, :HEAD_DIM] = k[...].reshape(keys, HEAD_DIM)
        k_wide[:, HEAD_DIM:] = key_features(cut, ROWS, 0)
        v_turned[...] = jnp.swapaxes(v[...].reshape(keys, HEAD_DIM), 0, 1)

    q_wide[:, :HEAD_DIM] = q[...].reshape(STEP_ROWS, HEAD_DIM)
    q_wide[:, HEAD_DIM:] = query_features(cut, (step * sources).astype(jnp.float32), ROWS, 0)

    def write(block, result, log_total):
        count = Q_ROWS // ROWS
        out[block * count : (block + 1) * count] = result.reshape(count, ROWS, HEAD_DIM)
        for row in range(count):
            lse[block * count + row : block * count + row + 1, :] = log_total[
                :, row * HEAD_DIM : (row + 1) * HEAD_DIM
            ]

    attend(lambda block: q_wide[block * Q_ROWS : (block + 1) * Q_ROWS, :], k_wide, v_turned, write)


def shared_kernel(where, cut, q, own_kv, far_kv, whole, whole_lse, out, k_wide, v_turned, q_wide):
    core = where[2]
    keys = N_SEQ * HALF
    for place, (kv, offset) in enumerate(((own_kv, HALF * core), (far_kv, HALF * (1 - core)))):
        at = slice(place * keys, (place + 1) * keys)
        k_wide[at, :HEAD_DIM] = kv[:, :HALF].reshape(keys, HEAD_DIM)
        k_wide[at, HEAD_DIM:] = key_features(cut, HALF, offset)
        v_turned[:, at] = jnp.swapaxes(kv[:, HALF:].reshape(keys, HEAD_DIM), 0, 1)
    q_wide[:, :HEAD_DIM] = q[...].reshape(STEP_ROWS, HEAD_DIM)
    q_wide[:, HEAD_DIM:] = query_features(cut, 0.0, HALF, HALF * core)
    log_totals = []

    def write(block, result, log_total):
        count = Q_ROWS // HALF
        out[block * count : (block + 1) * count, ROWS:RET_ROWS, :] = result.reshape(count, HALF, HEAD_DIM)
        for row in range(Q_ROWS // HEAD_DIM):
            log_totals.append(log_total[:, row * HEAD_DIM : (row + 1) * HEAD_DIM])

    attend(lambda block: q_wide[block * Q_ROWS : (block + 1) * Q_ROWS, :], k_wide, v_turned, write)
    out[:, :ROWS, :] = whole[...]
    rows = jnp.concatenate([whole_lse[...], *log_totals], axis=0).astype(jnp.bfloat16)
    for device in range(N_SEQ):
        out[device, WHOLE_LSE:, :] = rows


Q_ROWS = 512
STEP_ROWS = 1024
VMEM = 32 * 2**20
PLACE_VMEM = 60 * 2**20
JOIN_VMEM = 60 * 2**20
PROJECT_VMEM = 51 * 2**20


def attention_scratch():
    keys = N_SEQ * ROWS
    return [
        pltpu.VMEM((keys, 2 * HEAD_DIM), jnp.bfloat16),
        pltpu.VMEM((HEAD_DIM, keys), jnp.bfloat16),
        pltpu.VMEM((STEP_ROWS, 2 * HEAD_DIM), jnp.bfloat16),
    ]


def attention_cost(queries, keys):
    return pl.CostEstimate(
        flops=queries * keys * HEAD_DIM // 4,
        bytes_accessed=4 * keys * HEAD_DIM * 2,
        transcendentals=0,
    )


def attend_whole(received):
    keys = N_SEQ * ROWS
    steps = keys // STEP_ROWS
    sources = STEP_ROWS // ROWS
    return pl.pallas_call(
        whole_kernel,
        grid=(steps,),
        in_specs=[
            pl.BlockSpec((N_SEQ, CUT_ROWS, HEAD_DIM), lambda i: (0, SEND_ROWS // CUT_ROWS, 0)),
            pl.BlockSpec((sources, ROWS, HEAD_DIM), lambda i: (i, 0, 0)),
            pl.BlockSpec((N_SEQ, ROWS, HEAD_DIM), lambda i: (0, 1, 0)),
            pl.BlockSpec((N_SEQ, ROWS, HEAD_DIM), lambda i: (0, 2, 0)),
        ],
        out_specs=[
            pl.BlockSpec((sources, ROWS, HEAD_DIM), lambda i: (i, 0, 0)),
            pl.BlockSpec((sources, ROWS), lambda i: (i, 0)),
        ],
        out_shape=[
            jax.ShapeDtypeStruct((N_SEQ, ROWS, HEAD_DIM), jnp.bfloat16),
            jax.ShapeDtypeStruct((N_SEQ, ROWS), jnp.float32),
        ],
        scratch_shapes=attention_scratch(),
        compiler_params=pltpu.CompilerParams(vmem_limit_bytes=VMEM),
        cost_estimate=attention_cost(keys, keys),
        name="attend_whole",
    )(*[received] * 4)


def attend_shared(where, received, own_kv, far_kv, whole, whole_lse):
    keys = N_SEQ * ROWS
    full = lambda *shape: pl.BlockSpec(shape, lambda i, c: (0,) * len(shape))
    return pl.pallas_call(
        shared_kernel,
        grid_spec=pltpu.PrefetchScalarGridSpec(
            num_scalar_prefetch=1,
            grid=(1,),
            in_specs=[
                pl.BlockSpec((N_SEQ, CUT_ROWS, HEAD_DIM), lambda i, c: (0, SEND_ROWS // CUT_ROWS, 0)),
                pl.BlockSpec((N_SEQ, HALF, HEAD_DIM), lambda i, c: (0, A_ROWS // HALF, 0)),
                full(N_SEQ, 2 * HALF, HEAD_DIM),
                full(N_SEQ, 2 * HALF, HEAD_DIM),
                full(N_SEQ, ROWS, HEAD_DIM),
                full(N_SEQ, ROWS),
            ],
            out_specs=full(N_SEQ, RETURN, HEAD_DIM),
            scratch_shapes=attention_scratch(),
        ),
        out_shape=jax.ShapeDtypeStruct((N_SEQ, RETURN, HEAD_DIM), jnp.bfloat16),
        compiler_params=pltpu.CompilerParams(vmem_limit_bytes=VMEM),
        cost_estimate=attention_cost(keys // 2, keys),
        name="attend_shared",
    )(where, received, received, own_kv, far_kv, whole, whole_lse)


def place_kernel(where, mine, near, near_far, part, part_far, low, high, held, sems):
    x, core = where[1], where[2]
    sign = 1 - 2 * core

    def load(shard, to, index):
        return pltpu.make_async_copy(shard, held.at[(to + X_SIZE) % X_SIZE], sems.at[index])

    loads = [load(mine, x, 0), load(near, x - sign, 1), load(near_far, x + sign, 2)]
    for copy in loads:
        copy.start()

    @pl.when(core == 0)
    def _():
        load(part, x + 2, 3).start()

    @pl.when(core == 1)
    def _():
        load(part_far, x + 2, 3).start()

    for copy in loads + [load(part, x + 2, 3)]:
        copy.wait()
    stores = [
        pltpu.make_async_copy(held.at[pl.ds(2 * half, 2)], out, sems.at[4 + half])
        for half, out in enumerate((low, high))
    ]
    for store in stores:
        store.start()
    for store in stores:
        store.wait()


def place(where, mine, near, near_far, part, part_far):
    rows, columns = mine.shape
    return pl.pallas_call(
        place_kernel,
        grid_spec=pltpu.PrefetchScalarGridSpec(
            num_scalar_prefetch=1,
            grid=(),
            in_specs=[pl.BlockSpec(memory_space=pl.ANY)] * 5,
            out_specs=[pl.BlockSpec(memory_space=pl.ANY)] * 2,
            scratch_shapes=[
                pltpu.VMEM((X_SIZE, rows, columns), jnp.bfloat16),
                pltpu.SemaphoreType.DMA((6,)),
            ],
        ),
        out_shape=[jax.ShapeDtypeStruct((2, rows, columns), jnp.bfloat16)] * 2,
        compiler_params=pltpu.CompilerParams(vmem_limit_bytes=PLACE_VMEM),
        name="place",
    )(where, mine, near, near_far, part, part_far)


def join_kernel(*refs):
    halves, wholes, (held, in_sems, out_sems) = refs[:8], refs[8:12], refs[12:]
    rows = halves[0].shape[0]
    loads = [
        pltpu.make_async_copy(half, held.at[index // 2, pl.ds(index % 2 * rows, rows)], in_sems.at[index])
        for index, half in enumerate(halves)
    ]
    for load in loads:
        load.start()
    stores = []
    for index, whole in enumerate(wholes):
        loads[2 * index].wait()
        loads[2 * index + 1].wait()
        stores.append(pltpu.make_async_copy(held.at[index], whole, out_sems.at[index]))
        stores[-1].start()
    for store in stores:
        store.wait()


def join(chunks):
    rows, columns = chunks[0][0].shape
    return pl.pallas_call(
        join_kernel,
        in_specs=[pl.BlockSpec(memory_space=pl.ANY)] * 8,
        out_specs=[pl.BlockSpec(memory_space=pl.ANY)] * 4,
        out_shape=[jax.ShapeDtypeStruct((2 * rows, columns), jnp.bfloat16)] * 4,
        scratch_shapes=[
            pltpu.VMEM((4, 2 * rows, columns), jnp.bfloat16),
            pltpu.SemaphoreType.DMA((8,)),
            pltpu.SemaphoreType.DMA((4,)),
        ],
        compiler_params=pltpu.CompilerParams(vmem_limit_bytes=JOIN_VMEM),
        name="join",
    )(*[half for chunk in chunks for half in chunk])


def slot_of(ret, head):
    chip, member = head // 3, head % 3
    low, high = ret.at[2 * chip], ret.at[2 * chip + 1]
    lane = lax.broadcasted_iota(jnp.int32, (1, HEAD_DIM), 1)
    rows = []
    for source in range(N_SEQ):
        whole = [ref[WHOLE_LSE : WHOLE_LSE + N_SEQ, :].astype(jnp.float32) for ref in (low, high)]
        shared = [ref[SHARED_LSE:RETURN, :].astype(jnp.float32) for ref in (low, high)]
        left, right = (item[source // 2 : source // 2 + 1] for item in shared)
        if source % 2 == 0:
            right = pltpu.roll(right, HALF, 1)
        else:
            left = pltpu.roll(left, HALF, 1)
        both = jnp.where(lane < HALF, left, right)
        first, last = (item[source : source + 1] for item in whole)
        rows.append(jnp.where(member == 0, first, jnp.where(member == 1, both, last)))
    return rows


HOPS = (0, 1, 2, 3, -1, -2, -3)
PIECES = 7 + 2


def project_kernel(where, ret, *refs):
    weights, (vis_out, txt_out, slots, held, sems) = refs[:PIECES], refs[PIECES:]
    y, core = where[0], where[2]
    sign = 1 - 2 * core
    places = [(chunk, 0, 2) for chunk in range(7)] + [(7, core, 1), (7, 1 - core, 1)]
    copies = []
    for index, (chunk, half, count) in enumerate(places):
        start = chunk % 2 * TRIO + half * (TRIO // 2)
        to = held.at[chunk // 2, pl.ds(pl.multiple_of(start, 64), count * (TRIO // 2))]
        copies.append(pltpu.make_async_copy(weights[index], to, sems.at[index]))
    for copy in copies:
        copy.start()
    arrivals = [[copy] for copy in copies[:7]] + [copies[7:]]
    for slot in range(SLOTS):
        valid = where[5 + slot] > 0
        for source, row in enumerate(slot_of(ret, where[3 + slot])):
            row = jnp.where(valid, row, 0.0)
            at = source * VIS_ROWS
            slots[slot : slot + 1, at : at + VIS_ROWS] = row[:, :VIS_ROWS]
            at = VIS_SEQ + source * TXT_ROWS
            slots[slot : slot + 1, at : at + TXT_ROWS] = row[:, VIS_ROWS:]
    total = jnp.zeros((ROWS, held.shape[2]), jnp.float32)
    pieces = []
    for index, hops in enumerate((*HOPS, 4)):
        chip = (y - hops * sign + Y_SIZE) % Y_SIZE
        low, high = ret[2 * chip], ret[2 * chip + 1]
        shared = jnp.concatenate([low[ROWS:RET_ROWS], high[ROWS:RET_ROWS]], axis=0)
        attention = jnp.concatenate([low[:ROWS], shared, high[:ROWS]], axis=1)
        txt_out[:, pl.ds(pl.multiple_of(chip * TRIO, TRIO), TRIO)] = attention[VIS_ROWS:]
        pieces.append(attention)
        for copy in arrivals[index]:
            copy.wait()
        if index % 2 == 1:
            both = jnp.concatenate(pieces[-2:], axis=1)
            total += jnp.dot(both, held[index // 2], preferred_element_type=jnp.float32)
    vis_out[...] = total[:VIS_ROWS].astype(jnp.bfloat16)


def project(where, returned, weights):
    columns = weights[0].shape[1]
    return pl.pallas_call(
        project_kernel,
        grid_spec=pltpu.PrefetchScalarGridSpec(
            num_scalar_prefetch=1,
            grid=(),
            in_specs=[pl.BlockSpec(memory_space=pltpu.VMEM)] + [pl.BlockSpec(memory_space=pltpu.HBM)] * PIECES,
            out_specs=[pl.BlockSpec(memory_space=pltpu.VMEM)] * 3,
            scratch_shapes=[
                pltpu.VMEM((Y_SIZE // 2, 2 * TRIO, columns), jnp.bfloat16),
                pltpu.SemaphoreType.DMA((PIECES,)),
            ],
        ),
        out_shape=[
            jax.ShapeDtypeStruct((VIS_ROWS, columns), jnp.bfloat16),
            jax.ShapeDtypeStruct((TXT_ROWS, HEADS * HEAD_DIM), jnp.bfloat16),
            jax.ShapeDtypeStruct((SLOTS, VIS_SEQ + TXT_SEQ), jnp.float32),
        ],
        compiler_params=pltpu.CompilerParams(vmem_limit_bytes=PROJECT_VMEM),
        name="project",
    )(where, returned, *weights)


AXES = ("dp", "seq")
X_SIZE = 4
Y_SIZE = 8


def permute(operand, target, cores=(0, 1)):
    pairs = []
    for y in range(Y_SIZE):
        for x in range(X_SIZE):
            for s in range(N_SEQ):
                ty, tx, ts = target(y, x, s)
                there = (ty % Y_SIZE) * X_SIZE + tx % X_SIZE
                if s % 2 in cores:
                    pairs.append(((y * X_SIZE + x) * N_SEQ + s, there * N_SEQ + ts))
    return lax.ppermute(operand, AXES, pairs)


def swap(operand, cores=(0, 1)):
    return permute(operand, lambda y, x, s: (y, x, s ^ 1), cores)


def shift_x(operand, hops, cores=(0, 1)):
    return permute(operand, lambda y, x, s: (y, x + hops * (1 - 2 * (s % 2)), s), cores)


def shift_y(operand):
    return permute(operand, lambda y, x, s: (y + 1 - 2 * (s % 2), x, s))


def heads_of_slots(head_map, seq_index):
    mine = (head_map == seq_index).astype(jnp.int32)
    rank = jnp.cumsum(mine) - 1
    ids = jnp.arange(HEADS, dtype=jnp.int32)
    picked = mine[None] * (rank[None] == jnp.arange(SLOTS, dtype=jnp.int32)[:, None])
    return jnp.concatenate([jnp.sum(picked * ids[None], axis=1), jnp.sum(picked, axis=1)])


def on_device(qkv_vis, qkv_txt, vis_segments, txt_segments, head_map, w_out):
    seq_index = lax.axis_index("seq")
    dp_index = lax.axis_index("dp")
    core = seq_index % 2
    place_here = jnp.stack([dp_index // X_SIZE, dp_index % X_SIZE, core]).astype(jnp.int32)
    where = jnp.concatenate([place_here, heads_of_slots(head_map, seq_index)])

    near = shift_x(w_out, 1)
    part = shift_x(w_out, 2, cores=(0,))
    sending = pack(qkv_vis, qkv_txt, vis_segments, txt_segments)
    received = lax.all_to_all(sending, "seq", split_axis=0, concat_axis=0, tiled=True)
    halves = place(where, w_out, near, swap(near), part, swap(part, cores=(0,)))
    chunks = [[half.reshape(-1, half.shape[2]) for half in halves]]
    for _ in range(3):
        chunks.append([shift_y(half) for half in chunks[-1]])
    own_kv = received[:, A_ROWS + HALF : SEND_ROWS]
    far_kv = swap(own_kv)
    whole, whole_lse = attend_whole(received)
    returning = attend_shared(where, received, own_kv, far_kv, whole, whole_lse)
    returning, chunks[1:] = lax.optimization_barrier((returning, chunks[1:]))
    returned = lax.all_to_all(returning, "seq", split_axis=0, concat_axis=0, tiled=True)
    opposite = shift_y(jnp.where(core == 0, *chunks[3]))
    hops = join(chunks)
    weights = [*hops, *map(swap, hops[1:]), opposite, swap(opposite)]
    vis_out, txt_out, lse_slots = project(where, returned, weights)
    return vis_out, txt_out, lse_slots


def solution(mesh):
    in_specs = (
        P(("dp", "seq"), None),
        P(("dp", "seq"), None),
        P(("dp", "seq")),
        P(("dp", "seq")),
        P(),
        P("dp", None),
    )
    out_specs = (P(("dp", "seq"), None), P(("dp", "seq"), None), P("seq", "dp"))
    return jax.shard_map(
        on_device, mesh=mesh, in_specs=in_specs, out_specs=out_specs, check_vma=False
    )
```
